512 devices in a mesh: vel: 64 (over z, y), space: 8 (over x, core).
Axes of the slice: x: 4, y: 4, z: 16, core: 2. Of those that a mesh axis runs over, the one named last changes fastest.
Arguments:
- distribution: float32 [16384, 64, 128], P('vel', 'space'), may hold values from 0 to 11, as said below
- rate_class: int32 [64, 128], P('space'), may hold values from 0 to 7
- boundary_obstacle_indicator: int32 [64, 128], P('space'), may hold values 0 or 1
Outputs:
- field_out: float32 [16384, 64, 128], P('vel', 'space')
- latest_conserved_fields: float32 [5, 64, 128], P(None, 'space')
The draws below stay inside these ranges and needn't reach their ends.
Inputs may be any that keep to these rules, and one draw needn't show every extreme that they name: `distribution`: every entry positive.
All inputs are finite; a program needn't handle non-finite values. No bound on the sum of `boundary_obstacle_indicator` on one device may be relied on, other than what follows from the above.
Results may differ from the reference program's by a relative error of at most 0.0003.
Values sent between devices are 32-bit elements; how exact they have to be, the bound alone decides.
No kernel may reach another device: no remote copies, remote signals or barrier semaphores. Data moves between devices by JAX's collectives and lax.ppermute only.
A program may use at most 64 MiB of HBM per device.

```python
import jax
import jax.numpy as jnp
from jax import lax

VX = 32
VY = 32
VZ = 16
GRID_COLS_SPAN = 128
ITERS = 2
SWEEPS = 4
NV = 16384
GRID_ROWS_SPAN = 64


def draw_distribution(key, part):
    stochastic_seeds = jax.random.split(jax.random.fold_in(key, 71), 6)
    index = jnp.arange(NV, dtype=jnp.int32)
    discrete_abscissa_xaxis = (-5.0 + ((index % VX).astype(jnp.float32) + 0.5) * (10.0 / VX))[:, None, None]
    discrete_abscissa_yaxis = (-5.0 + ((index // VX % VY).astype(jnp.float32) + 0.5) * (10.0 / VY))[:, None, None]
    discrete_abscissa_zaxis = (-5.0 + ((index // (VX * VY)).astype(jnp.float32) + 0.5) * (10.0 / VZ))[:, None, None]
    particle_concentration = jax.random.uniform(stochastic_seeds[0], (GRID_ROWS_SPAN, GRID_COLS_SPAN), jnp.float32, 0.5, 2.0)
    kinetic_thermal_level = jax.random.uniform(stochastic_seeds[1], (GRID_ROWS_SPAN, GRID_COLS_SPAN), jnp.float32, 0.6, 1.6)
    rough_macro_guess = 0.5
    flow_x = jax.random.uniform(stochastic_seeds[2], (GRID_ROWS_SPAN, GRID_COLS_SPAN), jnp.float32, -0.5, 0.5)
    flow_y = jax.random.uniform(stochastic_seeds[3], (GRID_ROWS_SPAN, GRID_COLS_SPAN), jnp.float32, -0.5, 0.5)
    flow_z = jax.random.uniform(stochastic_seeds[4], (GRID_ROWS_SPAN, GRID_COLS_SPAN), jnp.float32, -0.2, 0.2)
    noisy_disturbance = jax.random.uniform(stochastic_seeds[5], (NV, GRID_ROWS_SPAN, GRID_COLS_SPAN), jnp.float32, -1.0, 1.0)
    quadratic_deviation = (discrete_abscissa_xaxis - flow_x) ** 2 + (discrete_abscissa_yaxis - flow_y) ** 2 + (discrete_abscissa_zaxis - flow_z) ** 2
    integral_averages = particle_concentration * kinetic_thermal_level ** (-1.5) * jnp.exp(-0.5 * quadratic_deviation / kinetic_thermal_level) * (1.0 + rough_macro_guess * noisy_disturbance)
    return integral_averages.astype(jnp.float32)


def place_ends(result, own_key, least, top_value):
    place = [jax.random.randint(jax.random.fold_in(own_key, axis), (), 0, length) for axis, length in enumerate(result.shape)]
    widest = result.shape.index(max(result.shape))
    next_to = place[:widest] + [(place[widest] + 1) % result.shape[widest]] + place[widest + 1:]
    return result.at[tuple(place)].set(least).at[tuple(next_to)].set(top_value)


def setup_inputs(seed: int = 0) -> dict:
    keys = jax.random.split(jax.random.key(seed), 4)
    distribution = draw_distribution(jax.random.fold_in(keys[3], 71), 0)
    rate_class = place_ends(jax.random.randint(keys[1], (GRID_ROWS_SPAN, GRID_COLS_SPAN), 0, 8), jax.random.fold_in(keys[1], 1), 0, 7).astype(jnp.int32)
    boundary_obstacle_indicator = place_ends((jax.random.randint(keys[2], (GRID_ROWS_SPAN, GRID_COLS_SPAN), 0, 8) < 1).astype(jnp.int32), jax.random.fold_in(keys[2], 1), 0, 1)
    return {"distribution": distribution, "rate_class": rate_class, "boundary_obstacle_indicator": boundary_obstacle_indicator}


speed_edge = 5.0
marching_step_length = 0.1
momentum_thermal_ratio = 2.0 / 3.0
shear_power_law_index = 0.81
diffusivity = 1.0


def velocity_table(index):
    index_x = index % VX
    index_y = (index // VX) % VY
    index_z = index // (VX * VY)
    discrete_abscissa_xaxis = -speed_edge + (index_x.astype(jnp.float32) + 0.5) * (2.0 * speed_edge / VX)
    discrete_abscissa_yaxis = -speed_edge + (index_y.astype(jnp.float32) + 0.5) * (2.0 * speed_edge / VY)
    discrete_abscissa_zaxis = -speed_edge + (index_z.astype(jnp.float32) + 0.5) * (2.0 * speed_edge / VZ)
    return discrete_abscissa_xaxis, discrete_abscissa_yaxis, discrete_abscissa_zaxis


def moment_weights(discrete_abscissa_xaxis, discrete_abscissa_yaxis, discrete_abscissa_zaxis):
    square = discrete_abscissa_xaxis * discrete_abscissa_xaxis + discrete_abscissa_yaxis * discrete_abscissa_yaxis + discrete_abscissa_zaxis * discrete_abscissa_zaxis
    quadrature = (2.0 * speed_edge / VX) * (2.0 * speed_edge / VY) * (2.0 * speed_edge / VZ) / (2.0 * jnp.pi) ** 1.5
    rows = [jnp.ones_like(discrete_abscissa_xaxis), discrete_abscissa_xaxis, discrete_abscissa_yaxis, discrete_abscissa_zaxis, square, discrete_abscissa_xaxis * discrete_abscissa_xaxis, discrete_abscissa_yaxis * discrete_abscissa_yaxis,
            discrete_abscissa_xaxis * discrete_abscissa_yaxis, discrete_abscissa_xaxis * discrete_abscissa_zaxis, discrete_abscissa_yaxis * discrete_abscissa_zaxis, discrete_abscissa_xaxis * square, discrete_abscissa_yaxis * square, discrete_abscissa_zaxis * square]
    return jnp.stack(rows) * quadrature


def conserved(moments):
    return jnp.stack([moments[0], moments[1], moments[2], moments[3], 0.5 * moments[4]])


def heat_flux(moments):
    mass = moments[0]
    flow_x = moments[1] / mass
    flow_y = moments[2] / mass
    flow_z = moments[3] / mass
    p_xx = moments[5]
    p_yy = moments[6]
    p_zz = moments[4] - moments[5] - moments[6]
    p_xy = moments[7]
    p_xz = moments[8]
    p_yz = moments[9]
    flow_sq = flow_x * flow_x + flow_y * flow_y + flow_z * flow_z
    heat_x = 0.5 * (moments[10] - 2.0 * (flow_x * p_xx + flow_y * p_xy + flow_z * p_xz) - flow_x * moments[4] + 2.0 * mass * flow_sq * flow_x)
    heat_y = 0.5 * (moments[11] - 2.0 * (flow_x * p_xy + flow_y * p_yy + flow_z * p_yz) - flow_y * moments[4] + 2.0 * mass * flow_sq * flow_y)
    heat_z = 0.5 * (moments[12] - 2.0 * (flow_x * p_xz + flow_y * p_yz + flow_z * p_zz) - flow_z * moments[4] + 2.0 * mass * flow_sq * flow_z)
    return jnp.stack([heat_x, heat_y, heat_z])


def transport_block(field, discrete_abscissa_xaxis, discrete_abscissa_yaxis):
    courant_x = (marching_step_length * discrete_abscissa_xaxis)[:, None, None]
    courant_y = (marching_step_length * discrete_abscissa_yaxis)[:, None, None]
    from_left = jnp.roll(field, 1, 2)
    from_right = jnp.roll(field, -1, 2)
    term_y = jnp.where(courant_y > 0, courant_y * (field - from_left), courant_y * (from_right - field))
    from_above = jnp.roll(field, 1, 1)
    from_below = jnp.roll(field, -1, 1)
    term_x = jnp.where(courant_x > 0, courant_x * (field - from_above), courant_x * (from_below - field))
    return field - term_x - term_y


def collision_update_piece(convected_fields, discrete_abscissa_xaxis, discrete_abscissa_yaxis, discrete_abscissa_zaxis, particle_concentration, mean_drift_velocity, kinetic_thermal_level, energy_flux_components, collision_frequency, obstacle_indicators):
    diff_x = discrete_abscissa_xaxis - mean_drift_velocity[0]
    diff_y = discrete_abscissa_yaxis - mean_drift_velocity[1]
    diff_z = discrete_abscissa_zaxis - mean_drift_velocity[2]
    quadratic_deviation = diff_x * diff_x + diff_y * diff_y + diff_z * diff_z
    prefactor_amplitude = particle_concentration * kinetic_thermal_level ** (-1.5)
    local_gaussian_population = prefactor_amplitude * jnp.exp(-0.5 * quadratic_deviation / kinetic_thermal_level)
    skewed_correction_multiplier = (1.0 - momentum_thermal_ratio) / (5.0 * particle_concentration * kinetic_thermal_level * kinetic_thermal_level)
    projected_energy_flux = diff_x * energy_flux_components[0] + diff_y * energy_flux_components[1] + diff_z * energy_flux_components[2]
    goal_population = local_gaussian_population * (1.0 + skewed_correction_multiplier * projected_energy_flux * (quadratic_deviation / kinetic_thermal_level - 5.0))
    wall_state = particle_concentration * jnp.exp(-0.5 * (discrete_abscissa_xaxis * discrete_abscissa_xaxis + discrete_abscissa_yaxis * discrete_abscissa_yaxis + discrete_abscissa_zaxis * discrete_abscissa_zaxis))
    relaxed = convected_fields + collision_frequency * (goal_population - convected_fields)
    return jnp.where(obstacle_indicators > 0, wall_state, relaxed)


def diffuse(source):
    iterate = source
    for sweep_index in range(SWEEPS):
        beside = (jnp.roll(iterate, 1, 1) + jnp.roll(iterate, -1, 1)) + jnp.roll(iterate, 1, 2) + jnp.roll(iterate, -1, 2)
        iterate = (source + diffusivity * beside) / (1.0 + 4.0 * diffusivity)
    return iterate


def reference(distribution, rate_class, boundary_obstacle_indicator):
    index = jnp.arange(NV, dtype=jnp.int32)
    discrete_abscissa_xaxis, discrete_abscissa_yaxis, discrete_abscissa_zaxis = velocity_table(index)
    block_rows = VX * VY
    blocks_x = discrete_abscissa_xaxis.reshape(VZ, block_rows)
    blocks_y = discrete_abscissa_yaxis.reshape(VZ, block_rows)
    blocks_z = discrete_abscissa_zaxis.reshape(VZ, block_rows)
    reference_collision_freq = 0.5 * jnp.exp2(rate_class.astype(jnp.float32))
    field = distribution
    latest_conserved_fields = jnp.zeros((5, GRID_ROWS_SPAN, GRID_COLS_SPAN), jnp.float32)
    for step_index in range(ITERS):
        field_blocks = field.reshape(VZ, block_rows, GRID_ROWS_SPAN, GRID_COLS_SPAN)

        def move(items):
            return transport_block(items[0], items[1], items[2])

        convected_fields = lax.map(move, (field_blocks, blocks_x, blocks_y))

        def accumulate(total, items):
            weights = moment_weights(items[1], items[2], items[3])
            part_sum = jnp.dot(weights, items[0].reshape(block_rows, GRID_ROWS_SPAN * GRID_COLS_SPAN), precision=lax.Precision.HIGHEST, preferred_element_type=jnp.float32)
            return total + part_sum, None

        moments, unused = lax.scan(accumulate, jnp.zeros((13, GRID_ROWS_SPAN * GRID_COLS_SPAN), jnp.float32), (convected_fields, blocks_x, blocks_y, blocks_z))
        source = conserved(moments).reshape(5, GRID_ROWS_SPAN, GRID_COLS_SPAN)
        energy_flux_components = heat_flux(moments).reshape(3, GRID_ROWS_SPAN, GRID_COLS_SPAN)
        latest_conserved_fields = diffuse(source)
        particle_concentration = latest_conserved_fields[0]
        mean_drift_velocity = latest_conserved_fields[1:4] / particle_concentration
        kinetic_thermal_level = (2.0 * latest_conserved_fields[4] / particle_concentration - (mean_drift_velocity[0] * mean_drift_velocity[0] + mean_drift_velocity[1] * mean_drift_velocity[1] + mean_drift_velocity[2] * mean_drift_velocity[2])) / 3.0
        collision_frequency = 1.0 - jnp.exp(-marching_step_length * reference_collision_freq * particle_concentration * kinetic_thermal_level ** (1.0 - shear_power_law_index))

        def collide(items):
            return collision_update_piece(items[0], items[1][:, None, None], items[2][:, None, None], items[3][:, None, None],
                               particle_concentration, mean_drift_velocity, kinetic_thermal_level, energy_flux_components, collision_frequency, boundary_obstacle_indicator)

        field = lax.map(collide, (convected_fields, blocks_x, blocks_y, blocks_z)).reshape(NV, GRID_ROWS_SPAN, GRID_COLS_SPAN)
    return field, latest_conserved_fields
```

```python
import jax
import jax.numpy as jnp
import numpy as np
from jax import lax
from jax.experimental import pallas as pl
from jax.experimental.pallas import tpu as pltpu
from jax.sharding import PartitionSpec as P

VX, VY, VZ = 32, 32, 16
SWEEPS = 4
EDGE = 5.0
STEP = 0.1
HX = 2.0 * EDGE / VX
HY = 2.0 * EDGE / VY
HZ = 2.0 * EDGE / VZ
QUAD = float(HX * HY * HZ / (2.0 * np.pi) ** 1.5)
SPEED_X = [-EDGE + (i + 0.5) * HX for i in range(VX)]
SPEED_Y = [-EDGE + (i + 0.5) * HY for i in range(VY)]
SPEED_Z = [-EDGE + (i + 0.5) * HZ for i in range(VZ)]
F32 = jnp.float32

MOMENTS = [
    ((0, 0, 0),),
    ((1, 0, 0),),
    ((0, 1, 0),),
    ((0, 0, 1),),
    ((2, 0, 0), (0, 2, 0), (0, 0, 2)),
    ((2, 0, 0),),
    ((0, 2, 0),),
    ((1, 1, 0),),
    ((1, 0, 1),),
    ((0, 1, 1),),
    ((3, 0, 0), (1, 2, 0), (1, 0, 2)),
    ((2, 1, 0), (0, 3, 0), (0, 1, 2)),
    ((2, 0, 1), (0, 2, 1), (0, 0, 3)),
]


def times(moment, axis):
    return tuple(tuple(p + (d == axis) for d, p in enumerate(m)) for m in moment)


def key_of(moment):
    return tuple(sorted(moment))


PLAIN = []
for _m in MOMENTS + [times(m, 0) for m in MOMENTS] + [times(m, 1) for m in MOMENTS]:
    if key_of(_m) not in PLAIN:
        PLAIN.append(key_of(_m))
AT = {k: i for i, k in enumerate(PLAIN)}
ABS_X = len(PLAIN)
ABS_Y = ABS_X + 13
SETS = ABS_Y + 13
SLOTS = 64


def rows_of():
    return lax.broadcasted_iota(jnp.int32, (8, 128), 0)


def place():
    vel = lax.axis_index("vel")
    return lax.rem(vel, 4), lax.div(vel, 4)


def local_y(block, iy):
    return -EDGE + ((block * 8 + iy).astype(F32) + 0.5) * HY


def local_z(iz):
    return -EDGE + (iz.astype(F32) + 0.5) * HZ


def moved(value, ix, courant_y, shift, row, before, after):
    courant_x = STEP * abs(SPEED_X[ix])
    if SPEED_X[ix] > 0:
        beside = jnp.where(row == 0, before, pltpu.roll(value, 1, 0))
    else:
        beside = jnp.where(row == 7, after, pltpu.roll(value, 7, 0))
    along = pltpu.roll(value, shift, 1)
    return ((1.0 - courant_x) - courant_y) * value + courant_x * beside + courant_y * along


def moments_kernel(f_ref, before_ref, after_ref, t_ref, part_ref, acc):
    block, iz = place()
    row = rows_of()
    shift = jnp.where(block >= 2, 1, 127)
    acc[...] = jnp.zeros_like(acc)

    def over_y(iy, carry):
        sy = local_y(block, iy)
        courant_y = STEP * jnp.abs(sy)
        sums = [[None] * 5, [None] * 5]
        for ix in range(VX):
            half = 1 if SPEED_X[ix] > 0 else 0
            k = ix - 16 if half else ix
            edge = (before_ref if half else after_ref)[iy, k : k + 1, :]
            value = moved(f_ref[iy * 32 + ix], ix, courant_y, shift, row, edge, edge)
            t_ref[iy * 32 + ix] = value
            for a in range(5):
                term = value if a == 0 else (SPEED_X[ix] ** a) * value
                sums[half][a] = term if sums[half][a] is None else sums[half][a] + term
        n = 0
        power = [1.0, sy, sy * sy, sy * sy * sy, sy * sy * sy * sy]
        full = [sums[1][a] + sums[0][a] for a in range(5)]
        odd = [sums[1][a] - sums[0][a] for a in range(5)]
        for a in range(5):
            for b in range(5 - a):
                acc[n] = acc[n] + power[b] * full[a]
                n += 1
        for a in range(1, 5):
            for b in range(5 - a):
                acc[n] = acc[n] + power[b] * odd[a]
                n += 1
        return carry

    lax.fori_loop(0, 8, over_y, 0)
    n, full, odd = 0, {}, {}
    for a in range(5):
        for b in range(5 - a):
            full[a, b] = n
            n += 1
    for a in range(1, 5):
        for b in range(5 - a):
            odd[a, b] = n
            n += 1
    sz = local_z(iz)
    zs = [QUAD * jnp.ones((), F32), QUAD * sz, QUAD * sz * sz, QUAD * sz * sz * sz]
    sign = jnp.where(block >= 2, 1.0, -1.0).astype(F32)
    for i, monos in enumerate(PLAIN):
        part_ref[i] = sum(zs[c] * acc[full[a, b]] for a, b, c in monos)
    for i, monos in enumerate(MOMENTS):
        part_ref[ABS_X + i] = sum(zs[c] * acc[odd[a + 1, b]] for a, b, c in monos)
        part_ref[ABS_Y + i] = sum((sign * zs[c]) * acc[full[a, b + 1]] for a, b, c in monos)
    for i in range(SETS, SLOTS):
        part_ref[i] = jnp.zeros((8, 128), F32)


def diffuse(own_source, far_source, row):
    own, far = own_source, far_source
    for _ in range(SWEEPS):
        own_down, far_down = pltpu.roll(own, 1, 0), pltpu.roll(far, 1, 0)
        own_up, far_up = pltpu.roll(own, 7, 0), pltpu.roll(far, 7, 0)
        new_own = (
            jnp.where(row == 0, far_down, own_down)
            + jnp.where(row == 7, far_up, own_up)
            + pltpu.roll(own, 1, 1)
            + pltpu.roll(own, 127, 1)
        )
        new_far = (
            jnp.where(row == 0, own_down, far_down)
            + jnp.where(row == 7, own_up, far_up)
            + pltpu.roll(far, 1, 1)
            + pltpu.roll(far, 127, 1)
        )
        own = (own_source + new_own) * 0.2
        far = (far_source + new_far) * 0.2
    return own


def heat_flux(m):
    inv = 1.0 / m[0]
    u = [m[1] * inv, m[2] * inv, m[3] * inv]
    p_zz = m[4] - m[5] - m[6]
    p = [[m[5], m[7], m[8]], [m[7], m[6], m[9]], [m[8], m[9], p_zz]]
    sq = u[0] * u[0] + u[1] * u[1] + u[2] * u[2]
    mass_sq = 2.0 * m[0] * sq
    return [
        0.5
        * (
            m[10 + i]
            - 2.0 * (u[0] * p[i][0] + u[1] * p[i][1] + u[2] * p[i][2])
            + u[i] * (mass_sq - m[4])
        )
        for i in range(3)
    ]


def cell_state(state, moments, rate_class, wall):
    density = state[0]
    inv = 1.0 / density
    u = [state[i] * inv for i in (1, 2, 3)]
    temperature = (2.0 * state[4] * inv - (u[0] * u[0] + u[1] * u[1] + u[2] * u[2])) * (1.0 / 3.0)
    heat = heat_flux(moments)
    frequency = 0.5 * jnp.exp2(rate_class.astype(F32))
    power = jnp.exp((1.0 - 0.81) * jnp.log(temperature))
    keep = jnp.exp(-STEP * frequency * density * power)
    inv_t = 1.0 / temperature
    rate = 1.0 - keep
    skew = ((1.0 - 2.0 / 3.0) / 5.0) * inv * inv_t * inv_t
    amplitude = rate * density * inv_t * lax.rsqrt(temperature)
    solid = wall > 0
    keep = jnp.where(solid, 0.0, keep)
    amplitude = jnp.where(solid, density, amplitude)
    inv_t = jnp.where(solid, 1.0, inv_t)
    u = [jnp.where(solid, 0.0, c) for c in u]
    heat = [jnp.where(solid, 0.0, skew * h) for h in heat]
    return keep, amplitude, inv_t, u, heat


def apply_added(iy, sy, sz, cell, profile):
    _, amplitude, inv_t, u, heat = cell
    dy, dz = sy - u[1], sz - u[2]
    square = (dy * dy + dz * dz) * inv_t
    return amplitude * jnp.exp(-0.5 * square), square - 5.0, dy * heat[1] + dz * heat[2]


def profile_x(cell, profile):
    _, _, inv_t, u, heat = cell
    for ix in range(VX):
        dx = SPEED_X[ix] - u[0]
        square = dx * dx * inv_t
        profile[0, ix] = jnp.exp(-0.5 * square)
        profile[1, ix] = square
        profile[2, ix] = dx * heat[0]


def line_sums(speeds, u, inv_t, top):
    out = [None] * (top + 1)
    for s in speeds:
        d = s - u
        e = jnp.exp(-0.5 * (d * d * inv_t))
        for a in range(top + 1):
            term = e if a == 0 else (s**a) * e
            out[a] = term if out[a] is None else out[a] + term
    return out


def central(raw, u, top):
    table = [raw]
    for _ in range(3):
        last = table[-1]
        table.append([last[a + 1] - u * last[a] for a in range(len(last) - 1)])
    return [line[: top + 1] for line in table]


def added_moments(cell):
    _, amplitude, inv_t, u, heat = cell
    scale = amplitude * QUAD
    half = VX // 2
    x_up = central(line_sums(SPEED_X[half:], u[0], inv_t, 7), u[0], 4)
    x_dn = central(line_sums(SPEED_X[:half], u[0], inv_t, 7), u[0], 4)
    y_up = central(line_sums(SPEED_Y[half:], u[1], inv_t, 7), u[1], 4)
    y_dn = central(line_sums(SPEED_Y[:half], u[1], inv_t, 7), u[1], 4)
    z_all = central([scale * z for z in line_sums(SPEED_Z, u[2], inv_t, 6)], u[2], 3)
    x_all = [[p + q for p, q in zip(r, s)] for r, s in zip(x_up, x_dn)]
    y_all = [[p + q for p, q in zip(r, s)] for r, s in zip(y_up, y_dn)]
    gx, gy, gz = heat
    hx, hy, hz = gx * inv_t, gy * inv_t, gz * inv_t

    def whole(xs, ys):
        plane = {}

        def at(a, b):
            if (a, b) not in plane:
                x = [xs[i][a] for i in range(4)]
                y = [ys[i][b] for i in range(4)]
                x0y0 = x[0] * y[0]
                x1y0, x0y1 = x[1] * y[0], x[0] * y[1]
                x2y0, x0y2 = x[2] * y[0], x[0] * y[2]
                p0 = (
                    x0y0
                    + hx * (x[3] * y[0] + x[1] * y[2])
                    + hy * (x[2] * y[1] + x[0] * y[3])
                    - 5.0 * (gx * x1y0 + gy * x0y1)
                )
                p1 = hz * (x2y0 + x0y2) - 5.0 * gz * x0y0
                p2 = hx * x1y0 + hy * x0y1
                p3 = hz * x0y0
                plane[a, b] = (p0, p1, p2, p3)
            return plane[a, b]

        out = []
        for monos in MOMENTS:
            total = None
            for a, b, c in monos:
                p = at(a, b)
                term = (
                    p[0] * z_all[0][c] + p[1] * z_all[1][c] + p[2] * z_all[2][c] + p[3] * z_all[3][c]
                )
                total = term if total is None else total + term
            out.append(total)
        return out

    def weighted(table, factor):
        return [[factor * v for v in line[1:5]] for line in table]

    return (
        whole(x_all, y_all),
        whole(weighted(x_up, STEP), y_all),
        whole(weighted(x_dn, -STEP), y_all),
        whole(x_all, weighted(y_up, STEP)),
        whole(x_all, weighted(y_dn, -STEP)),
    )


def first_kernel(
    q_ref, prev_ref, next_ref, class_ref, wall_ref, t_ref,
    f_ref, m_ref, add_ref, to_next_ref, to_prev_ref, profile,
):
    block, iz = place()
    row = rows_of()
    scale = [1.0, 1.0, 1.0, 1.0, 0.5]
    state = [
        diffuse(scale[k] * q_ref[k], scale[k] * jnp.where(row < 4, next_ref[k], prev_ref[k]), row)
        for k in range(5)
    ]
    cell = cell_state(state, [q_ref[k] for k in range(13)], class_ref[...], wall_ref[...])
    keep = cell[0]
    profile_x(cell, profile)
    sz = local_z(iz)

    def over_y(iy, carry):
        base, square, flux = apply_added(iy, local_y(block, iy), sz, cell, profile)
        for ix in range(VX):
            added = (base * profile[0, ix]) * (
                1.0 + (flux + profile[2, ix]) * (square + profile[1, ix])
            )
            value = keep * t_ref[iy * 32 + ix] + added
            f_ref[iy * 32 + ix] = value
            k = ix % 16
            if SPEED_X[ix] > 0:
                to_next_ref[6 + 2 * iy + k // 8, k % 8 : k % 8 + 1, :] = value[7:8, :]
            else:
                to_prev_ref[6 + 2 * iy + k // 8, k % 8 : k % 8 + 1, :] = value[0:1, :]
        return carry

    lax.fori_loop(0, 8, over_y, 0)

    g_all, g_xu, g_xd, g_yu, g_yd = added_moments(cell)
    part = 0.5 * STEP * keep
    for k, monos in enumerate(MOMENTS):
        sx_k, ax_k = q_ref[AT[key_of(times(monos, 0))]], q_ref[ABS_X + k]
        sy_k, ay_k = q_ref[AT[key_of(times(monos, 1))]], q_ref[ABS_Y + k]
        x_up = part * (ax_k + sx_k) + g_xu[k]
        x_dn = part * (ax_k - sx_k) + g_xd[k]
        y_up = part * (ay_k + sy_k) + g_yu[k]
        y_dn = part * (ay_k - sy_k) + g_yd[k]
        from_up, from_dn = pltpu.roll(x_up, 1, 0), pltpu.roll(x_dn, 7, 0)
        total = (
            (keep * q_ref[k] + g_all[k] - x_up - x_dn - y_up - y_dn)
            + jnp.where(row == 0, 0.0, from_up)
            + jnp.where(row == 7, 0.0, from_dn)
            + pltpu.roll(y_up, 1, 1)
            + pltpu.roll(y_dn, 127, 1)
        )
        m_ref[k] = total
        if k < 5:
            add_ref[k] = jnp.where(row == 0, from_up, jnp.where(row == 7, from_dn, 0.0))
            to_next_ref[k] = jnp.where(row == 0, from_up, total)
            to_prev_ref[k] = jnp.where(row == 7, from_dn, total)
        else:
            to_next_ref[5, k - 5 : k - 4, :] = x_up[7:8, :]
            to_prev_ref[5, k - 5 : k - 4, :] = x_dn[0:1, :]


def second_kernel(
    m_ref, add_ref, prev_ref, next_ref, class_ref, wall_ref, f_ref, out_ref, state_ref, profile
):
    block, iz = place()
    row = rows_of()
    shift = jnp.where(block >= 2, 1, 127)
    moments = []
    for k in range(13):
        if k < 5:
            before, after = prev_ref[k], next_ref[k]
        else:
            before, after = prev_ref[5, k - 5 : k - 4, :], next_ref[5, k - 5 : k - 4, :]
        moments.append(
            m_ref[k] + jnp.where(row == 0, before, jnp.where(row == 7, after, 0.0))
        )
    scale = [1.0, 1.0, 1.0, 1.0, 0.5]
    state = []
    for k in range(5):
        far = jnp.where(row < 4, next_ref[k], prev_ref[k]) + add_ref[k]
        state.append(diffuse(scale[k] * moments[k], scale[k] * far, row))
        state_ref[k] = state[k]
    cell = cell_state(state, moments, class_ref[...], wall_ref[...])
    keep = cell[0]
    profile_x(cell, profile)
    sz = local_z(iz)

    def over_y(iy, carry):
        sy = local_y(block, iy)
        courant_y = STEP * jnp.abs(sy)
        base, square, flux = apply_added(iy, sy, sz, cell, profile)
        for ix in range(VX):
            k = ix % 16
            edge = (prev_ref if SPEED_X[ix] > 0 else next_ref)[
                6 + 2 * iy + k // 8, k % 8 : k % 8 + 1, :
            ]
            value = moved(f_ref[iy * 32 + ix], ix, courant_y, shift, row, edge, edge)
            added = (base * profile[0, ix]) * (
                1.0 + (flux + profile[2, ix]) * (square + profile[1, ix])
            )
            out_ref[iy * 32 + ix] = keep * value + added
        return carry

    lax.fori_loop(0, 8, over_y, 0)


def kernel_call(body, outs, scratch):
    return pl.pallas_call(
        body,
        out_shape=[jax.ShapeDtypeStruct(s, F32) for s in outs],
        scratch_shapes=[pltpu.VMEM(s, F32) for s in scratch],
        compiler_params=pltpu.CompilerParams(vmem_limit_bytes=32 * 1024 * 1024),
    )


def to_both(up_value, down_value):
    size = lax.axis_size("space")
    up = [(i, (i + 1) % size) for i in range(size)]
    down = [(j, i) for i, j in up]
    return lax.ppermute(up_value, "space", up), lax.ppermute(down_value, "space", down)


NEAR = [[(4 * z + k) * 4 + y for k in range(4) for y in range(4)] for z in range(4)]
FAR = [[(z + 4 * k) * 4 + y for k in range(4)] for z in range(4) for y in range(4)]


def all_sum(part):
    piece = part.reshape(16, SLOTS // 2, 128)
    piece = lax.all_to_all(piece, "vel", 0, 0, tiled=True, axis_index_groups=NEAR)
    mine = jnp.sum(piece, 0)
    piece = jnp.broadcast_to(mine[None], (4,) + mine.shape)
    piece = lax.all_to_all(piece, "vel", 0, 0, tiled=True, axis_index_groups=FAR)
    mine = jnp.sum(piece, 0)
    piece = jnp.broadcast_to(mine[None], (16,) + mine.shape)
    piece = lax.all_to_all(piece, "vel", 0, 0, tiled=True, axis_index_groups=NEAR)
    return piece.reshape(SLOTS, 8, 128)


def per_device(distribution, rate_class, wall):
    grouped = distribution.reshape(8, 32, 8, 128)
    before, after = to_both(grouped[:, 16:, 7, :], grouped[:, :16, 0, :])
    block = (256, 8, 128)
    transported, part = kernel_call(moments_kernel, [block, (SLOTS, 8, 128)], [(25, 8, 128)])(
        distribution, before, after
    )
    sums = all_sum(part)
    prev, after = to_both(sums[:5], sums[:5])
    small = (22, 8, 128)
    field, moments, extra, to_next, to_prev = kernel_call(
        first_kernel, [block, (13, 8, 128), (5, 8, 128), small, small], [(3, 32, 8, 128)]
    )(sums, prev, after, rate_class, wall, transported)
    prev, after = to_both(to_next, to_prev)
    field, state = kernel_call(second_kernel, [block, (5, 8, 128)], [(3, 32, 8, 128)])(
        moments, extra, prev, after, rate_class, wall, field
    )
    return field, state


def solution(mesh):
    return jax.shard_map(
        per_device,
        mesh=mesh,
        in_specs=(P("vel", "space", None), P("space", None), P("space", None)),
        out_specs=(P("vel", "space", None), P(None, "space", None)),
        check_vma=False,
    )
```

```python
import jax
import jax.numpy as jnp
import numpy as np
from jax import lax
from jax.experimental import pallas as pl
from jax.experimental.pallas import tpu as pltpu
from jax.sharding import PartitionSpec as P

VX, VY, VZ = 32, 32, 16
SWEEPS = 4
EDGE = 5.0
STEP = 0.1
HX = 2.0 * EDGE / VX
HY = 2.0 * EDGE / VY
HZ = 2.0 * EDGE / VZ
QUAD = float(HX * HY * HZ / (2.0 * np.pi) ** 1.5)
SPEED_X = [-EDGE + (i + 0.5) * HX for i in range(VX)]
SPEED_Y = [-EDGE + (i + 0.5) * HY for i in range(VY)]
SPEED_Z = [-EDGE + (i + 0.5) * HZ for i in range(VZ)]
F32 = jnp.float32

MOMENTS = [
    ((0, 0, 0),),
    ((1, 0, 0),),
    ((0, 1, 0),),
    ((0, 0, 1),),
    ((2, 0, 0), (0, 2, 0), (0, 0, 2)),
    ((2, 0, 0),),
    ((0, 2, 0),),
    ((1, 1, 0),),
    ((1, 0, 1),),
    ((0, 1, 1),),
    ((3, 0, 0), (1, 2, 0), (1, 0, 2)),
    ((2, 1, 0), (0, 3, 0), (0, 1, 2)),
    ((2, 0, 1), (0, 2, 1), (0, 0, 3)),
]


def times(moment, axis):
    return tuple(tuple(p + (d == axis) for d, p in enumerate(m)) for m in moment)


def key_of(moment):
    return tuple(sorted(moment))


PLAIN = []
for _m in MOMENTS + [times(m, 0) for m in MOMENTS] + [times(m, 1) for m in MOMENTS]:
    if key_of(_m) not in PLAIN:
        PLAIN.append(key_of(_m))
AT = {k: i for i, k in enumerate(PLAIN)}
ABS_X = len(PLAIN)
ABS_Y = ABS_X + 13
SETS = ABS_Y + 13
SLOTS = 64
FIRST_SET = 7


def slot_of(i):
    return FIRST_SET + i if i < 5 else FIRST_SET + 6 + i


def row_up(i):
    return (i // 8, i % 8) if i < 48 else (6, i - 48)


def row_down(i):
    return (12 + i // 8, i % 8) if i < 48 else (6, i - 45)


def rows_of():
    return lax.broadcasted_iota(jnp.int32, (8, 128), 0)


def place():
    vel = lax.axis_index("vel")
    return lax.rem(vel, 4), lax.div(vel, 4)


def local_y(block, iy):
    return -EDGE + ((block * 8 + iy).astype(F32) + 0.5) * HY


def local_z(iz):
    return -EDGE + (iz.astype(F32) + 0.5) * HZ


def moved(value, ix, courant_y, shift, row, before, after):
    courant_x = STEP * abs(SPEED_X[ix])
    if SPEED_X[ix] > 0:
        beside = jnp.where(row == 0, before, pltpu.roll(value, 1, 0))
    else:
        beside = jnp.where(row == 7, after, pltpu.roll(value, 7, 0))
    along = pltpu.roll(value, shift, 1)
    return ((1.0 - courant_x) - courant_y) * value + courant_x * beside + courant_y * along


def powers():
    full = [(a, b) for a in range(5) for b in range(5 - a)]
    odd = [(a, b) for a in range(1, 5) for b in range(5 - a)]
    return {p: i for i, p in enumerate(full)}, {p: 15 + i for i, p in enumerate(odd)}


def moments_kernel(f_hbm, part_ref, to_next_ref, to_prev_ref, field, acc, edge_acc, sems):
    block, iz = place()
    row = rows_of()
    shift = jnp.where(block >= 2, 1, 127)
    full_at, odd_at = powers()

    def chunk(i):
        rows = pl.ds(i * 32, 32)
        return pltpu.make_async_copy(f_hbm.at[rows], field.at[rows], sems.at[i])

    for i in range(8):
        chunk(i).start()
    acc[...] = jnp.zeros_like(acc)
    edge_acc[...] = jnp.zeros_like(edge_acc)
    lane_x = (row.astype(F32) + 0.5) * HX

    def over_y(iy, carry):
        chunk(iy).wait()
        sy = local_y(block, iy)
        courant_y = STEP * jnp.abs(sy)
        sums = [[None] * 5, [None] * 5]
        for ix in range(VX):
            half = 1 if SPEED_X[ix] > 0 else 0
            k = ix % 16
            raw = field[iy * 32 + ix]
            if half:
                to_next_ref[2 * iy + k // 8, k % 8 : k % 8 + 1, :] = raw[7:8, :]
            else:
                to_prev_ref[2 * iy + k // 8, k % 8 : k % 8 + 1, :] = raw[0:1, :]
            value = moved(raw, ix, courant_y, shift, row, 0.0, 0.0)
            for a in range(5):
                term = value if a == 0 else (SPEED_X[ix] ** a) * value
                sums[half][a] = term if sums[half][a] is None else sums[half][a] + term
        power = [1.0, sy, sy * sy, sy * sy * sy, sy * sy * sy * sy]
        full = [sums[1][a] + sums[0][a] for a in range(5)]
        odd = [sums[1][a] - sums[0][a] for a in range(5)]
        for (a, b), n in full_at.items():
            acc[n] = acc[n] + power[b] * full[a]
        for (a, b), n in odd_at.items():
            acc[n] = acc[n] + power[b] * odd[a]
        for side, ref, base in ((0, to_next_ref, 0.0), (1, to_prev_ref, -EDGE)):
            edge = [None] * 5
            for j in range(2):
                sx = lane_x + (base + 8 * HX * j)
                term = (STEP * jnp.abs(sx)) * ref[2 * iy + j]
                for a in range(5):
                    term = term if a == 0 else sx * term
                    edge[a] = term if edge[a] is None else edge[a] + term
            for (a, b), n in full_at.items():
                edge_acc[side, n] = edge_acc[side, n] + power[b] * edge[a]
        return carry

    lax.fori_loop(0, 8, over_y, 0)
    sz = local_z(iz)
    zs = [QUAD * jnp.ones((), F32), QUAD * sz, QUAD * sz * sz, QUAD * sz * sz * sz]
    sign = jnp.where(block >= 2, 1.0, -1.0).astype(F32)
    zy = [sign * z for z in zs]

    def all_sets(full, odd):
        out = [sum(zs[c] * full(a, b) for a, b, c in monos) for monos in PLAIN]
        out += [sum(zs[c] * odd(a + 1, b) for a, b, c in monos) for monos in MOMENTS]
        out += [sum(zy[c] * full(a, b + 1) for a, b, c in monos) for monos in MOMENTS]
        return out

    for i, v in enumerate(all_sets(lambda a, b: acc[full_at[a, b]], lambda a, b: acc[odd_at[a, b]])):
        part_ref[slot_of(i)] = v
    part_ref[6] = jnp.zeros((8, 128), F32)
    for side, where in ((0, row_up), (1, row_down)):
        lines = {p: jnp.sum(edge_acc[side, n], axis=0, keepdims=True) for p, n in full_at.items()}
        factor = -1.0 if side else 1.0
        for i, v in enumerate(
            all_sets(lambda a, b: lines[a, b], lambda a, b: factor * lines[a, b])
        ):
            slot, r = where(i)
            part_ref[slot, r : r + 1, :] = v


def diffuse(own_source, far_source, row):
    own, far = own_source, far_source
    for _ in range(SWEEPS):
        own_down, far_down = pltpu.roll(own, 1, 0), pltpu.roll(far, 1, 0)
        own_up, far_up = pltpu.roll(own, 7, 0), pltpu.roll(far, 7, 0)
        new_own = (
            jnp.where(row == 0, far_down, own_down)
            + jnp.where(row == 7, far_up, own_up)
            + pltpu.roll(own, 1, 1)
            + pltpu.roll(own, 127, 1)
        )
        new_far = (
            jnp.where(row == 0, own_down, far_down)
            + jnp.where(row == 7, own_up, far_up)
            + pltpu.roll(far, 1, 1)
            + pltpu.roll(far, 127, 1)
        )
        own = (own_source + new_own) * 0.2
        far = (far_source + new_far) * 0.2
    return own


def heat_flux(m):
    inv = 1.0 / m[0]
    u = [m[1] * inv, m[2] * inv, m[3] * inv]
    p_zz = m[4] - m[5] - m[6]
    p = [[m[5], m[7], m[8]], [m[7], m[6], m[9]], [m[8], m[9], p_zz]]
    sq = u[0] * u[0] + u[1] * u[1] + u[2] * u[2]
    mass_sq = 2.0 * m[0] * sq
    return [
        0.5
        * (
            m[10 + i]
            - 2.0 * (u[0] * p[i][0] + u[1] * p[i][1] + u[2] * p[i][2])
            + u[i] * (mass_sq - m[4])
        )
        for i in range(3)
    ]


def cell_state(state, moments, rate_class, wall):
    density = state[0]
    inv = 1.0 / density
    u = [state[i] * inv for i in (1, 2, 3)]
    temperature = (2.0 * state[4] * inv - (u[0] * u[0] + u[1] * u[1] + u[2] * u[2])) * (1.0 / 3.0)
    heat = heat_flux(moments)
    frequency = 0.5 * jnp.exp2(rate_class.astype(F32))
    power = jnp.exp((1.0 - 0.81) * jnp.log(temperature))
    keep = jnp.exp(-STEP * frequency * density * power)
    inv_t = 1.0 / temperature
    rate = 1.0 - keep
    skew = ((1.0 - 2.0 / 3.0) / 5.0) * inv * inv_t * inv_t
    amplitude = rate * density * inv_t * lax.rsqrt(temperature)
    solid = wall > 0
    keep = jnp.where(solid, 0.0, keep)
    amplitude = jnp.where(solid, density, amplitude)
    inv_t = jnp.where(solid, 1.0, inv_t)
    u = [jnp.where(solid, 0.0, c) for c in u]
    heat = [jnp.where(solid, 0.0, skew * h) for h in heat]
    return keep, amplitude, inv_t, u, heat


def apply_added(sy, sz, cell):
    _, amplitude, inv_t, u, heat = cell
    dy, dz = sy - u[1], sz - u[2]
    square = (dy * dy + dz * dz) * inv_t
    return amplitude * jnp.exp(-0.5 * square), square - 5.0, dy * heat[1] + dz * heat[2]


def profile_x(cell, profile):
    _, _, inv_t, u, heat = cell
    for ix in range(VX):
        dx = SPEED_X[ix] - u[0]
        square = dx * dx * inv_t
        profile[0, ix] = jnp.exp(-0.5 * square)
        profile[1, ix] = square
        profile[2, ix] = dx * heat[0]


def line_sums(speeds, u, inv_t, top):
    out = [None] * (top + 1)
    for s in speeds:
        d = s - u
        e = jnp.exp(-0.5 * (d * d * inv_t))
        for a in range(top + 1):
            term = e if a == 0 else (s**a) * e
            out[a] = term if out[a] is None else out[a] + term
    return out


def central(raw, u, top):
    table = [raw]
    for _ in range(3):
        last = table[-1]
        table.append([last[a + 1] - u * last[a] for a in range(len(last) - 1)])
    return [line[: top + 1] for line in table]


def added_moments(cell):
    _, amplitude, inv_t, u, heat = cell
    scale = amplitude * QUAD
    half = VX // 2
    x_up = central(line_sums(SPEED_X[half:], u[0], inv_t, 7), u[0], 4)
    x_dn = central(line_sums(SPEED_X[:half], u[0], inv_t, 7), u[0], 4)
    y_up = central(line_sums(SPEED_Y[half:], u[1], inv_t, 7), u[1], 4)
    y_dn = central(line_sums(SPEED_Y[:half], u[1], inv_t, 7), u[1], 4)
    z_all = central([scale * z for z in line_sums(SPEED_Z, u[2], inv_t, 6)], u[2], 3)
    x_all = [[p + q for p, q in zip(r, s)] for r, s in zip(x_up, x_dn)]
    y_all = [[p + q for p, q in zip(r, s)] for r, s in zip(y_up, y_dn)]
    gx, gy, gz = heat
    hx, hy, hz = gx * inv_t, gy * inv_t, gz * inv_t

    def whole(xs, ys):
        plane = {}

        def at(a, b):
            if (a, b) not in plane:
                x = [xs[i][a] for i in range(4)]
                y = [ys[i][b] for i in range(4)]
                x0y0 = x[0] * y[0]
                x1y0, x0y1 = x[1] * y[0], x[0] * y[1]
                x2y0, x0y2 = x[2] * y[0], x[0] * y[2]
                p0 = (
                    x0y0
                    + hx * (x[3] * y[0] + x[1] * y[2])
                    + hy * (x[2] * y[1] + x[0] * y[3])
                    - 5.0 * (gx * x1y0 + gy * x0y1)
                )
                p1 = hz * (x2y0 + x0y2) - 5.0 * gz * x0y0
                p2 = hx * x1y0 + hy * x0y1
                p3 = hz * x0y0
                plane[a, b] = (p0, p1, p2, p3)
            return plane[a, b]

        out = []
        for monos in MOMENTS:
            total = None
            for a, b, c in monos:
                p = at(a, b)
                term = (
                    p[0] * z_all[0][c] + p[1] * z_all[1][c] + p[2] * z_all[2][c] + p[3] * z_all[3][c]
                )
                total = term if total is None else total + term
            out.append(total)
        return out

    def weighted(table, factor):
        return [[factor * v for v in line[1:5]] for line in table]

    return (
        whole(x_all, y_all),
        whole(weighted(x_up, STEP), y_all),
        whole(weighted(x_dn, -STEP), y_all),
        whole(x_all, weighted(y_up, STEP)),
        whole(x_all, weighted(y_dn, -STEP)),
    )


def first_kernel(
    q_ref, prev_ref, next_ref, before_ref, after_ref, class_ref, wall_ref, t_ref,
    f_ref, m_ref, add_ref, to_next_ref, to_prev_ref, profile,
):
    block, iz = place()
    row = rows_of()
    shift = jnp.where(block >= 2, 1, 127)

    def line(ref, first, at):
        return ref[at[0] - first, at[1] : at[1] + 1, :]

    def whole_set(i):
        above, below = line(prev_ref, 0, row_up(i)), line(next_ref, 6, row_down(i))
        return q_ref[slot_of(i)] + jnp.where(row == 0, above, jnp.where(row == 7, below, 0.0))

    sets = [whole_set(i) for i in range(SETS)]
    scale = [1.0, 1.0, 1.0, 1.0, 0.5]
    state = []
    for k in range(5):
        far = jnp.where(row < 4, next_ref[1 + k], prev_ref[FIRST_SET + k])
        up, down = line(q_ref, 0, row_up(k)), line(q_ref, 0, row_down(k))
        far = far + jnp.where(row == 0, up, jnp.where(row == 7, down, 0.0))
        state.append(diffuse(scale[k] * sets[k], scale[k] * far, row))
    cell = cell_state(state, sets[:13], class_ref[...], wall_ref[...])
    keep = cell[0]
    profile_x(cell, profile)
    sz = local_z(iz)

    def over_y(iy, carry):
        sy = local_y(block, iy)
        courant_y = STEP * jnp.abs(sy)
        base, square, flux = apply_added(sy, sz, cell)
        for ix in range(VX):
            k = ix % 16
            edge = (before_ref if SPEED_X[ix] > 0 else after_ref)[
                2 * iy + k // 8, k % 8 : k % 8 + 1, :
            ]
            value = moved(t_ref[iy * 32 + ix], ix, courant_y, shift, row, edge, edge)
            added = (base * profile[0, ix]) * (
                1.0 + (flux + profile[2, ix]) * (square + profile[1, ix])
            )
            value = keep * value + added
            f_ref[iy * 32 + ix] = value
            if SPEED_X[ix] > 0:
                to_next_ref[6 + 2 * iy + k // 8, k % 8 : k % 8 + 1, :] = value[7:8, :]
            else:
                to_prev_ref[6 + 2 * iy + k // 8, k % 8 : k % 8 + 1, :] = value[0:1, :]
        return carry

    lax.fori_loop(0, 8, over_y, 0)

    g_all, g_xu, g_xd, g_yu, g_yd = added_moments(cell)
    part = 0.5 * STEP * keep
    for k, monos in enumerate(MOMENTS):
        sx_k, ax_k = sets[AT[key_of(times(monos, 0))]], sets[ABS_X + k]
        sy_k, ay_k = sets[AT[key_of(times(monos, 1))]], sets[ABS_Y + k]
        x_up = part * (ax_k + sx_k) + g_xu[k]
        x_dn = part * (ax_k - sx_k) + g_xd[k]
        y_up = part * (ay_k + sy_k) + g_yu[k]
        y_dn = part * (ay_k - sy_k) + g_yd[k]
        from_up, from_dn = pltpu.roll(x_up, 1, 0), pltpu.roll(x_dn, 7, 0)
        total = (
            (keep * sets[k] + g_all[k] - x_up - x_dn - y_up - y_dn)
            + jnp.where(row == 0, 0.0, from_up)
            + jnp.where(row == 7, 0.0, from_dn)
            + pltpu.roll(y_up, 1, 1)
            + pltpu.roll(y_dn, 127, 1)
        )
        m_ref[k] = total
        if k < 5:
            add_ref[k] = jnp.where(row == 0, from_up, jnp.where(row == 7, from_dn, 0.0))
            to_next_ref[k] = jnp.where(row == 0, from_up, total)
            to_prev_ref[k] = jnp.where(row == 7, from_dn, total)
        else:
            to_next_ref[5, k - 5 : k - 4, :] = x_up[7:8, :]
            to_prev_ref[5, k - 5 : k - 4, :] = x_dn[0:1, :]


def second_kernel(
    m_ref, add_ref, prev_ref, next_ref, class_ref, wall_ref, f_ref, out_ref, state_ref, profile
):
    block, iz = place()
    row = rows_of()
    shift = jnp.where(block >= 2, 1, 127)
    moments = []
    for k in range(13):
        if k < 5:
            before, after = prev_ref[k], next_ref[k]
        else:
            before, after = prev_ref[5, k - 5 : k - 4, :], next_ref[5, k - 5 : k - 4, :]
        moments.append(
            m_ref[k] + jnp.where(row == 0, before, jnp.where(row == 7, after, 0.0))
        )
    scale = [1.0, 1.0, 1.0, 1.0, 0.5]
    state = []
    for k in range(5):
        far = jnp.where(row < 4, next_ref[k], prev_ref[k]) + add_ref[k]
        state.append(diffuse(scale[k] * moments[k], scale[k] * far, row))
        state_ref[k] = state[k]
    cell = cell_state(state, moments, class_ref[...], wall_ref[...])
    keep = cell[0]
    profile_x(cell, profile)
    sz = local_z(iz)

    def over_y(iy, carry):
        sy = local_y(block, iy)
        courant_y = STEP * jnp.abs(sy)
        base, square, flux = apply_added(sy, sz, cell)
        for ix in range(VX):
            k = ix % 16
            edge = (prev_ref if SPEED_X[ix] > 0 else next_ref)[
                6 + 2 * iy + k // 8, k % 8 : k % 8 + 1, :
            ]
            value = moved(f_ref[iy * 32 + ix], ix, courant_y, shift, row, edge, edge)
            added = (base * profile[0, ix]) * (
                1.0 + (flux + profile[2, ix]) * (square + profile[1, ix])
            )
            out_ref[iy * 32 + ix] = keep * value + added
        return carry

    lax.fori_loop(0, 8, over_y, 0)


def kernel_call(body, outs, scratch, **kw):
    return pl.pallas_call(
        body,
        out_shape=[jax.ShapeDtypeStruct(s, F32) for s in outs],
        scratch_shapes=[pltpu.VMEM(s, F32) if isinstance(s, tuple) else s for s in scratch],
        compiler_params=pltpu.CompilerParams(vmem_limit_bytes=32 * 1024 * 1024),
        **kw,
    )


def to_both(up_value, down_value):
    size = lax.axis_size("space")
    up = [(i, (i + 1) % size) for i in range(size)]
    down = [(j, i) for i, j in up]
    return lax.ppermute(up_value, "space", up), lax.ppermute(down_value, "space", down)


NEAR = [[(4 * z + k) * 4 + y for k in range(4) for y in range(4)] for z in range(4)]
FAR = [[(z + 4 * k) * 4 + y for k in range(4)] for z in range(4) for y in range(4)]


def all_sum(part):
    piece = part.reshape(16, SLOTS // 2, 128)
    piece = lax.all_to_all(piece, "vel", 0, 0, tiled=True, axis_index_groups=NEAR)
    mine = jnp.sum(piece, 0)
    piece = jnp.broadcast_to(mine[None], (4,) + mine.shape)
    piece = lax.all_to_all(piece, "vel", 0, 0, tiled=True, axis_index_groups=FAR)
    mine = jnp.sum(piece, 0)
    piece = jnp.broadcast_to(mine[None], (16,) + mine.shape)
    piece = lax.all_to_all(piece, "vel", 0, 0, tiled=True, axis_index_groups=NEAR)
    return piece.reshape(SLOTS, 8, 128)


def per_device(distribution, rate_class, wall):
    block, edges, small = (256, 8, 128), (16, 8, 128), (22, 8, 128)
    part, to_next, to_prev = kernel_call(
        moments_kernel,
        [(SLOTS, 8, 128), edges, edges],
        [block, (25, 8, 128), (2, 15, 8, 128), pltpu.SemaphoreType.DMA((8,))],
        in_specs=[pl.BlockSpec(memory_space=pl.ANY)],
    )(distribution)
    before, after = to_both(to_next, to_prev)
    sums = all_sum(part)
    prev, following = to_both(sums[:12], sums[6:18])
    field, moments, extra, to_next, to_prev = kernel_call(
        first_kernel, [block, (13, 8, 128), (5, 8, 128), small, small], [(3, 32, 8, 128)]
    )(sums, prev, following, before, after, rate_class, wall, distribution)
    prev, following = to_both(to_next, to_prev)
    field, state = kernel_call(second_kernel, [block, (5, 8, 128)], [(3, 32, 8, 128)])(
        moments, extra, prev, following, rate_class, wall, field
    )
    return field, state


def solution(mesh):
    return jax.shard_map(
        per_device,
        mesh=mesh,
        in_specs=(P("vel", "space", None), P("space", None), P("space", None)),
        out_specs=(P("vel", "space", None), P(None, "space", None)),
        check_vma=False,
    )
```

```python
import jax
import jax.numpy as jnp
import numpy as np
from jax import lax
from jax.experimental import pallas as pl
from jax.experimental.pallas import tpu as pltpu
from jax.sharding import PartitionSpec as P

VX, VY, VZ = 32, 32, 16
SWEEPS = 4
EDGE = 5.0
STEP = 0.1
HX = 2.0 * EDGE / VX
HY = 2.0 * EDGE / VY
HZ = 2.0 * EDGE / VZ
QUAD = float(HX * HY * HZ / (2.0 * np.pi) ** 1.5)
SPEED_X = [-EDGE + (i + 0.5) * HX for i in range(VX)]
SPEED_Y = [-EDGE + (i + 0.5) * HY for i in range(VY)]
SPEED_Z = [-EDGE + (i + 0.5) * HZ for i in range(VZ)]
F32 = jnp.float32

MOMENTS = [
    ((0, 0, 0),),
    ((1, 0, 0),),
    ((0, 1, 0),),
    ((0, 0, 1),),
    ((2, 0, 0), (0, 2, 0), (0, 0, 2)),
    ((2, 0, 0),),
    ((0, 2, 0),),
    ((1, 1, 0),),
    ((1, 0, 1),),
    ((0, 1, 1),),
    ((3, 0, 0), (1, 2, 0), (1, 0, 2)),
    ((2, 1, 0), (0, 3, 0), (0, 1, 2)),
    ((2, 0, 1), (0, 2, 1), (0, 0, 3)),
]


def times(moment, axis):
    return tuple(tuple(p + (d == axis) for d, p in enumerate(m)) for m in moment)


def key_of(moment):
    return tuple(sorted(moment))


PLAIN = []
for _m in MOMENTS + [times(m, 0) for m in MOMENTS] + [times(m, 1) for m in MOMENTS]:
    if key_of(_m) not in PLAIN:
        PLAIN.append(key_of(_m))
AT = {k: i for i, k in enumerate(PLAIN)}
ABS_X = len(PLAIN)
ABS_Y = ABS_X + 13
SETS = ABS_Y + 13
SLOTS = 64
FIRST_SET = 7


def slot_of(i):
    return FIRST_SET + i if i < 5 else FIRST_SET + 6 + i


def row_up(i):
    return (i // 8, i % 8) if i < 48 else (6, i - 48)


def row_down(i):
    return (12 + i // 8, i % 8) if i < 48 else (6, i - 45)


def rows_of():
    return lax.broadcasted_iota(jnp.int32, (8, 128), 0)


def added_up(terms):
    total = None
    for t in terms:
        total = t if total is None else total + t
    return total


def place():
    vel = lax.axis_index("vel")
    return lax.rem(vel, 4), lax.div(vel, 4)


def local_y(block, iy):
    return -EDGE + ((block * 8 + iy).astype(F32) + 0.5) * HY


def local_z(iz):
    return -EDGE + (iz.astype(F32) + 0.5) * HZ


def moved(value, ix, courant_y, shift, row, before, after):
    courant_x = STEP * abs(SPEED_X[ix])
    if SPEED_X[ix] > 0:
        beside = jnp.where(row == 0, before, pltpu.roll(value, 1, 0))
    else:
        beside = jnp.where(row == 7, after, pltpu.roll(value, 7, 0))
    along = pltpu.roll(value, shift, 1)
    return ((1.0 - courant_x) - courant_y) * value + courant_x * beside + courant_y * along


def powers():
    full = [(a, b) for a in range(5) for b in range(5 - a)]
    odd = [(a, b) for a in range(1, 5) for b in range(5 - a)]
    return {p: i for i, p in enumerate(full)}, {p: 15 + i for i, p in enumerate(odd)}


def moments_kernel(f_hbm, part_ref, to_next_ref, to_prev_ref, field, acc, edge_acc, sems):
    block, iz = place()
    row = rows_of()
    shift = jnp.where(block >= 2, 1, 127)
    full_at, odd_at = powers()

    def chunk(i):
        rows = pl.ds(i * 32, 32)
        return pltpu.make_async_copy(f_hbm.at[rows], field.at[rows], sems.at[i])

    for i in range(8):
        chunk(i).start()
    acc[...] = jnp.zeros_like(acc)
    edge_acc[...] = jnp.zeros_like(edge_acc)
    lane_x = (row.astype(F32) + 0.5) * HX

    def over_y(iy, carry):
        chunk(iy).wait()
        sy = local_y(block, iy)
        courant_y = STEP * jnp.abs(sy)
        sums = [[None] * 5, [None] * 5]
        for ix in range(VX):
            half = 1 if SPEED_X[ix] > 0 else 0
            k = ix % 16
            raw = field[iy * 32 + ix]
            if half:
                to_next_ref[2 * iy + k // 8, k % 8 : k % 8 + 1, :] = raw[7:8, :]
            else:
                to_prev_ref[2 * iy + k // 8, k % 8 : k % 8 + 1, :] = raw[0:1, :]
            value = moved(raw, ix, courant_y, shift, row, 0.0, 0.0)
            for a in range(5):
                term = value if a == 0 else (SPEED_X[ix] ** a) * value
                sums[half][a] = term if sums[half][a] is None else sums[half][a] + term
        power = [1.0, sy, sy * sy, sy * sy * sy, sy * sy * sy * sy]
        full = [sums[1][a] + sums[0][a] for a in range(5)]
        odd = [sums[1][a] - sums[0][a] for a in range(5)]
        for (a, b), n in full_at.items():
            acc[n] = acc[n] + power[b] * full[a]
        for (a, b), n in odd_at.items():
            acc[n] = acc[n] + power[b] * odd[a]
        for side, ref, base in ((0, to_next_ref, 0.0), (1, to_prev_ref, -EDGE)):
            edge = [None] * 5
            for j in range(2):
                sx = lane_x + (base + 8 * HX * j)
                term = (STEP * jnp.abs(sx)) * ref[2 * iy + j]
                for a in range(5):
                    term = term if a == 0 else sx * term
                    edge[a] = term if edge[a] is None else edge[a] + term
            for (a, b), n in full_at.items():
                edge_acc[side, n] = edge_acc[side, n] + power[b] * edge[a]
        return carry

    lax.fori_loop(0, 8, over_y, 0)
    sz = local_z(iz)
    zs = [QUAD * jnp.ones((), F32), QUAD * sz, QUAD * sz * sz, QUAD * sz * sz * sz]
    sign = jnp.where(block >= 2, 1.0, -1.0).astype(F32)
    zy = [sign * z for z in zs]

    def all_sets(full, odd):
        out = [added_up(zs[c] * full(a, b) for a, b, c in monos) for monos in PLAIN]
        out += [added_up(zs[c] * odd(a + 1, b) for a, b, c in monos) for monos in MOMENTS]
        out += [added_up(zy[c] * full(a, b + 1) for a, b, c in monos) for monos in MOMENTS]
        return out

    for i, v in enumerate(all_sets(lambda a, b: acc[full_at[a, b]], lambda a, b: acc[odd_at[a, b]])):
        part_ref[slot_of(i)] = v
    part_ref[6] = jnp.zeros((8, 128), F32)
    for side, where in ((0, row_up), (1, row_down)):
        lines = {p: jnp.sum(edge_acc[side, n], axis=0, keepdims=True) for p, n in full_at.items()}
        factor = -1.0 if side else 1.0
        for i, v in enumerate(
            all_sets(lambda a, b: lines[a, b], lambda a, b: factor * lines[a, b])
        ):
            slot, r = where(i)
            part_ref[slot, r : r + 1, :] = v


def diffuse(own_source, far_source, row):
    own, far = own_source, far_source
    for _ in range(SWEEPS):
        own_down, far_down = pltpu.roll(own, 1, 0), pltpu.roll(far, 1, 0)
        own_up, far_up = pltpu.roll(own, 7, 0), pltpu.roll(far, 7, 0)
        new_own = (
            jnp.where(row == 0, far_down, own_down)
            + jnp.where(row == 7, far_up, own_up)
            + pltpu.roll(own, 1, 1)
            + pltpu.roll(own, 127, 1)
        )
        new_far = (
            jnp.where(row == 0, own_down, far_down)
            + jnp.where(row == 7, own_up, far_up)
            + pltpu.roll(far, 1, 1)
            + pltpu.roll(far, 127, 1)
        )
        own = (own_source + new_own) * 0.2
        far = (far_source + new_far) * 0.2
    return own


def heat_flux(m):
    inv = 1.0 / m[0]
    u = [m[1] * inv, m[2] * inv, m[3] * inv]
    p_zz = m[4] - m[5] - m[6]
    p = [[m[5], m[7], m[8]], [m[7], m[6], m[9]], [m[8], m[9], p_zz]]
    sq = u[0] * u[0] + u[1] * u[1] + u[2] * u[2]
    mass_sq = 2.0 * m[0] * sq
    return [
        0.5
        * (
            m[10 + i]
            - 2.0 * (u[0] * p[i][0] + u[1] * p[i][1] + u[2] * p[i][2])
            + u[i] * (mass_sq - m[4])
        )
        for i in range(3)
    ]


def cell_state(state, moments, rate_class, wall):
    density = state[0]
    inv = 1.0 / density
    u = [state[i] * inv for i in (1, 2, 3)]
    temperature = (2.0 * state[4] * inv - (u[0] * u[0] + u[1] * u[1] + u[2] * u[2])) * (1.0 / 3.0)
    heat = heat_flux(moments)
    frequency = 0.5 * jnp.exp2(rate_class.astype(F32))
    power = jnp.exp((1.0 - 0.81) * jnp.log(temperature))
    keep = jnp.exp(-STEP * frequency * density * power)
    inv_t = 1.0 / temperature
    rate = 1.0 - keep
    skew = ((1.0 - 2.0 / 3.0) / 5.0) * inv * inv_t * inv_t
    amplitude = rate * density * inv_t * lax.rsqrt(temperature)
    solid = wall > 0
    keep = jnp.where(solid, 0.0, keep)
    amplitude = jnp.where(solid, density, amplitude)
    inv_t = jnp.where(solid, 1.0, inv_t)
    u = [jnp.where(solid, 0.0, c) for c in u]
    heat = [jnp.where(solid, 0.0, skew * h) for h in heat]
    return keep, amplitude, inv_t, u, heat


def apply_added(sy, sz, cell):
    _, amplitude, inv_t, u, heat = cell
    dy, dz = sy - u[1], sz - u[2]
    square = (dy * dy + dz * dz) * inv_t
    return amplitude * jnp.exp(-0.5 * square), square - 5.0, dy * heat[1] + dz * heat[2]


def profile_x(cell, profile):
    _, _, inv_t, u, heat = cell
    for ix in range(VX):
        dx = SPEED_X[ix] - u[0]
        square = dx * dx * inv_t
        profile[0, ix] = jnp.exp(-0.5 * square)
        profile[1, ix] = square
        profile[2, ix] = dx * heat[0]


def line_sums(speeds, u, inv_t, top):
    out = [None] * (top + 1)
    for s in speeds:
        d = s - u
        e = jnp.exp(-0.5 * (d * d * inv_t))
        for a in range(top + 1):
            term = e if a == 0 else (s**a) * e
            out[a] = term if out[a] is None else out[a] + term
    return out


def central(raw, u, top):
    table = [raw]
    for _ in range(3):
        last = table[-1]
        table.append([last[a + 1] - u * last[a] for a in range(len(last) - 1)])
    return [line[: top + 1] for line in table]


def added_moments(cell):
    _, amplitude, inv_t, u, heat = cell
    scale = amplitude * QUAD
    half = VX // 2
    x_up = central(line_sums(SPEED_X[half:], u[0], inv_t, 7), u[0], 4)
    x_dn = central(line_sums(SPEED_X[:half], u[0], inv_t, 7), u[0], 4)
    y_up = central(line_sums(SPEED_Y[half:], u[1], inv_t, 7), u[1], 4)
    y_dn = central(line_sums(SPEED_Y[:half], u[1], inv_t, 7), u[1], 4)
    z_all = central([scale * z for z in line_sums(SPEED_Z, u[2], inv_t, 6)], u[2], 3)
    x_all = [[p + q for p, q in zip(r, s)] for r, s in zip(x_up, x_dn)]
    y_all = [[p + q for p, q in zip(r, s)] for r, s in zip(y_up, y_dn)]
    gx, gy, gz = heat
    hx, hy, hz = gx * inv_t, gy * inv_t, gz * inv_t

    def whole(xs, ys):
        plane = {}

        def at(a, b):
            if (a, b) not in plane:
                x = [xs[i][a] for i in range(4)]
                y = [ys[i][b] for i in range(4)]
                x0y0 = x[0] * y[0]
                x1y0, x0y1 = x[1] * y[0], x[0] * y[1]
                x2y0, x0y2 = x[2] * y[0], x[0] * y[2]
                p0 = (
                    x0y0
                    + hx * (x[3] * y[0] + x[1] * y[2])
                    + hy * (x[2] * y[1] + x[0] * y[3])
                    - 5.0 * (gx * x1y0 + gy * x0y1)
                )
                p1 = hz * (x2y0 + x0y2) - 5.0 * gz * x0y0
                p2 = hx * x1y0 + hy * x0y1
                p3 = hz * x0y0
                plane[a, b] = (p0, p1, p2, p3)
            return plane[a, b]

        out = []
        for monos in MOMENTS:
            total = None
            for a, b, c in monos:
                p = at(a, b)
                term = (
                    p[0] * z_all[0][c] + p[1] * z_all[1][c] + p[2] * z_all[2][c] + p[3] * z_all[3][c]
                )
                total = term if total is None else total + term
            out.append(total)
        return out

    def weighted(table, factor):
        return [[factor * v for v in line[1:5]] for line in table]

    return (
        whole(x_all, y_all),
        whole(weighted(x_up, STEP), y_all),
        whole(weighted(x_dn, -STEP), y_all),
        whole(x_all, weighted(y_up, STEP)),
        whole(x_all, weighted(y_dn, -STEP)),
    )


def first_kernel(
    q_ref, prev_ref, next_ref, before_ref, after_ref, class_ref, wall_ref, t_ref,
    f_ref, m_ref, add_ref, to_next_ref, to_prev_ref, profile,
):
    block, iz = place()
    row = rows_of()
    shift = jnp.where(block >= 2, 1, 127)

    def line(ref, first, at):
        return ref[at[0] - first, at[1] : at[1] + 1, :]

    def whole_set(i):
        above, below = line(prev_ref, 0, row_up(i)), line(next_ref, 6, row_down(i))
        return q_ref[slot_of(i)] + jnp.where(row == 0, above, jnp.where(row == 7, below, 0.0))

    sets = [whole_set(i) for i in range(SETS)]
    scale = [1.0, 1.0, 1.0, 1.0, 0.5]
    state = []
    for k in range(5):
        far = jnp.where(row < 4, next_ref[1 + k], prev_ref[FIRST_SET + k])
        up, down = line(q_ref, 0, row_up(k)), line(q_ref, 0, row_down(k))
        far = far + jnp.where(row == 0, up, jnp.where(row == 7, down, 0.0))
        state.append(diffuse(scale[k] * sets[k], scale[k] * far, row))
    cell = cell_state(state, sets[:13], class_ref[...], wall_ref[...])
    keep = cell[0]
    profile_x(cell, profile)
    sz = local_z(iz)

    def over_y(iy, carry):
        sy = local_y(block, iy)
        courant_y = STEP * jnp.abs(sy)
        base, square, flux = apply_added(sy, sz, cell)
        for ix in range(VX):
            k = ix % 16
            edge = (before_ref if SPEED_X[ix] > 0 else after_ref)[
                2 * iy + k // 8, k % 8 : k % 8 + 1, :
            ]
            value = moved(t_ref[iy * 32 + ix], ix, courant_y, shift, row, edge, edge)
            added = (base * profile[0, ix]) * (
                1.0 + (flux + profile[2, ix]) * (square + profile[1, ix])
            )
            value = keep * value + added
            f_ref[iy * 32 + ix] = value
            if SPEED_X[ix] > 0:
                to_next_ref[6 + 2 * iy + k // 8, k % 8 : k % 8 + 1, :] = value[7:8, :]
            else:
                to_prev_ref[6 + 2 * iy + k // 8, k % 8 : k % 8 + 1, :] = value[0:1, :]
        return carry

    lax.fori_loop(0, 8, over_y, 0)

    g_all, g_xu, g_xd, g_yu, g_yd = added_moments(cell)
    part = 0.5 * STEP * keep
    for k, monos in enumerate(MOMENTS):
        sx_k, ax_k = sets[AT[key_of(times(monos, 0))]], sets[ABS_X + k]
        sy_k, ay_k = sets[AT[key_of(times(monos, 1))]], sets[ABS_Y + k]
        x_up = part * (ax_k + sx_k) + g_xu[k]
        x_dn = part * (ax_k - sx_k) + g_xd[k]
        y_up = part * (ay_k + sy_k) + g_yu[k]
        y_dn = part * (ay_k - sy_k) + g_yd[k]
        from_up, from_dn = pltpu.roll(x_up, 1, 0), pltpu.roll(x_dn, 7, 0)
        total = (
            (keep * sets[k] + g_all[k] - x_up - x_dn - y_up - y_dn)
            + jnp.where(row == 0, 0.0, from_up)
            + jnp.where(row == 7, 0.0, from_dn)
            + pltpu.roll(y_up, 1, 1)
            + pltpu.roll(y_dn, 127, 1)
        )
        m_ref[k] = total
        if k < 5:
            add_ref[k] = jnp.where(row == 0, from_up, jnp.where(row == 7, from_dn, 0.0))
            to_next_ref[k] = jnp.where(row == 0, from_up, total)
            to_prev_ref[k] = jnp.where(row == 7, from_dn, total)
        else:
            to_next_ref[5, k - 5 : k - 4, :] = x_up[7:8, :]
            to_prev_ref[5, k - 5 : k - 4, :] = x_dn[0:1, :]


def second_kernel(
    m_ref, add_ref, prev_ref, next_ref, class_ref, wall_ref, f_ref,
    out_hbm, state_ref, profile, out, sems,
):
    block, iz = place()
    row = rows_of()
    shift = jnp.where(block >= 2, 1, 127)
    moments = []
    for k in range(13):
        if k < 5:
            before, after = prev_ref[k], next_ref[k]
        else:
            before, after = prev_ref[5, k - 5 : k - 4, :], next_ref[5, k - 5 : k - 4, :]
        moments.append(
            m_ref[k] + jnp.where(row == 0, before, jnp.where(row == 7, after, 0.0))
        )
    scale = [1.0, 1.0, 1.0, 1.0, 0.5]
    state = []
    for k in range(5):
        far = jnp.where(row < 4, next_ref[k], prev_ref[k]) + add_ref[k]
        state.append(diffuse(scale[k] * moments[k], scale[k] * far, row))
        state_ref[k] = state[k]
    cell = cell_state(state, moments, class_ref[...], wall_ref[...])
    keep = cell[0]
    profile_x(cell, profile)
    sz = local_z(iz)

    def chunk(i):
        rows = pl.ds(i * 32, 32)
        return pltpu.make_async_copy(out.at[rows], out_hbm.at[rows], sems.at[i])

    def over_y(iy, carry):
        sy = local_y(block, iy)
        courant_y = STEP * jnp.abs(sy)
        base, square, flux = apply_added(sy, sz, cell)
        for ix in range(VX):
            k = ix % 16
            edge = (prev_ref if SPEED_X[ix] > 0 else next_ref)[
                6 + 2 * iy + k // 8, k % 8 : k % 8 + 1, :
            ]
            value = moved(f_ref[iy * 32 + ix], ix, courant_y, shift, row, edge, edge)
            added = (base * profile[0, ix]) * (
                1.0 + (flux + profile[2, ix]) * (square + profile[1, ix])
            )
            out[iy * 32 + ix] = keep * value + added
        chunk(iy).start()
        return carry

    lax.fori_loop(0, 8, over_y, 0)
    for i in range(8):
        chunk(i).wait()


def kernel_call(body, outs, scratch, **kw):
    return pl.pallas_call(
        body,
        out_shape=[jax.ShapeDtypeStruct(s, F32) for s in outs],
        scratch_shapes=[pltpu.VMEM(s, F32) if isinstance(s, tuple) else s for s in scratch],
        compiler_params=pltpu.CompilerParams(vmem_limit_bytes=32 * 1024 * 1024),
        **kw,
    )


def to_both(up_value, down_value):
    size = lax.axis_size("space")
    up = [(i, (i + 1) % size) for i in range(size)]
    down = [(j, i) for i, j in up]
    return lax.ppermute(up_value, "space", up), lax.ppermute(down_value, "space", down)


NEAR = [[(4 * z + k) * 4 + y for k in range(4) for y in range(4)] for z in range(4)]
FAR = [[(z + 4 * k) * 4 + y for k in range(4)] for z in range(4) for y in range(4)]


def all_sum(part, beside):
    piece = part.reshape(16, SLOTS // 2, 128)
    piece = lax.all_to_all(piece, "vel", 0, 0, tiled=True, axis_index_groups=NEAR)
    piece, beside = lax.optimization_barrier((piece, beside))
    mine = jnp.sum(piece, 0)
    piece = jnp.broadcast_to(mine[None], (4,) + mine.shape)
    piece = lax.all_to_all(piece, "vel", 0, 0, tiled=True, axis_index_groups=FAR)
    mine = jnp.sum(piece, 0)
    piece = jnp.broadcast_to(mine[None], (16,) + mine.shape)
    piece = lax.all_to_all(piece, "vel", 0, 0, tiled=True, axis_index_groups=NEAR)
    return piece.reshape(SLOTS, 8, 128), beside


def per_device(distribution, rate_class, wall):
    block, edges, small = (256, 8, 128), (16, 8, 128), (22, 8, 128)
    part, to_next, to_prev = kernel_call(
        moments_kernel,
        [(SLOTS, 8, 128), edges, edges],
        [block, (25, 8, 128), (2, 15, 8, 128), pltpu.SemaphoreType.DMA((8,))],
        in_specs=[pl.BlockSpec(memory_space=pltpu.HBM)],
    )(distribution)
    sums, (before, after) = all_sum(part, to_both(to_next, to_prev))
    prev, following = to_both(sums[:12], sums[6:18])
    field, moments, extra, to_next, to_prev = kernel_call(
        first_kernel, [block, (13, 8, 128), (5, 8, 128), small, small], [(3, 32, 8, 128)]
    )(sums, prev, following, before, after, rate_class, wall, distribution)
    prev, following = to_both(to_next, to_prev)
    field, state = kernel_call(
        second_kernel,
        [block, (5, 8, 128)],
        [(3, 32, 8, 128), block, pltpu.SemaphoreType.DMA((8,))],
        out_specs=[pl.BlockSpec(memory_space=pltpu.HBM), pl.BlockSpec(memory_space=pltpu.VMEM)],
    )(moments, extra, prev, following, rate_class, wall, field)
    return field, state


def solution(mesh):
    return jax.shard_map(
        per_device,
        mesh=mesh,
        in_specs=(P("vel", "space", None), P("space", None), P("space", None)),
        out_specs=(P("vel", "space", None), P(None, "space", None)),
        check_vma=False,
    )
```

```python
import jax
import jax.numpy as jnp
import numpy as np
from jax import lax
from jax.experimental import pallas as pl
from jax.experimental.pallas import tpu as pltpu
from jax.sharding import PartitionSpec as P

VX, VY, VZ = 32, 32, 16
SWEEPS = 4
EDGE = 5.0
STEP = 0.1
HX = 2.0 * EDGE / VX
HY = 2.0 * EDGE / VY
HZ = 2.0 * EDGE / VZ
QUAD = float(HX * HY * HZ / (2.0 * np.pi) ** 1.5)
SPEED_X = [-EDGE + (i + 0.5) * HX for i in range(VX)]
SPEED_Y = [-EDGE + (i + 0.5) * HY for i in range(VY)]
SPEED_Z = [-EDGE + (i + 0.5) * HZ for i in range(VZ)]
F32 = jnp.float32

MOMENTS = [
    ((0, 0, 0),),
    ((1, 0, 0),),
    ((0, 1, 0),),
    ((0, 0, 1),),
    ((2, 0, 0), (0, 2, 0), (0, 0, 2)),
    ((2, 0, 0),),
    ((0, 2, 0),),
    ((1, 1, 0),),
    ((1, 0, 1),),
    ((0, 1, 1),),
    ((3, 0, 0), (1, 2, 0), (1, 0, 2)),
    ((2, 1, 0), (0, 3, 0), (0, 1, 2)),
    ((2, 0, 1), (0, 2, 1), (0, 0, 3)),
]


def times(moment, axis):
    return tuple(tuple(p + (d == axis) for d, p in enumerate(m)) for m in moment)


def key_of(moment):
    return tuple(sorted(moment))


PLAIN = []
for _m in MOMENTS + [times(m, 0) for m in MOMENTS] + [times(m, 1) for m in MOMENTS]:
    if key_of(_m) not in PLAIN:
        PLAIN.append(key_of(_m))
AT = {k: i for i, k in enumerate(PLAIN)}
ABS_X = len(PLAIN)
ABS_Y = ABS_X + 13
SETS = ABS_Y + 13
SLOTS = 64
FIRST_SET = 7


def slot_of(i):
    return FIRST_SET + i if i < 5 else FIRST_SET + 6 + i


def row_up(i):
    return (i // 8, i % 8) if i < 48 else (6, i - 48)


def row_down(i):
    return (12 + i // 8, i % 8) if i < 48 else (6, i - 45)


def rows_of():
    return lax.broadcasted_iota(jnp.int32, (8, 128), 0)


def added_up(terms):
    total = None
    for t in terms:
        total = t if total is None else total + t
    return total


def place():
    vel = lax.axis_index("vel")
    return lax.rem(vel, 4), lax.div(vel, 4)


def local_y(block, iy):
    return -EDGE + ((block * 8 + iy).astype(F32) + 0.5) * HY


def local_z(iz):
    return -EDGE + (iz.astype(F32) + 0.5) * HZ


def moved(value, ix, courant_y, shift, row, before, after):
    courant_x = STEP * abs(SPEED_X[ix])
    if SPEED_X[ix] > 0:
        beside = jnp.where(row == 0, before, pltpu.roll(value, 1, 0))
    else:
        beside = jnp.where(row == 7, after, pltpu.roll(value, 7, 0))
    along = pltpu.roll(value, shift, 1)
    return ((1.0 - courant_x) - courant_y) * value + courant_x * beside + courant_y * along


def powers():
    full = [(a, b) for a in range(5) for b in range(5 - a)]
    odd = [(a, b) for a in range(1, 5) for b in range(5 - a)]
    return {p: i for i, p in enumerate(full)}, {p: 15 + i for i, p in enumerate(odd)}


def moments_kernel(f_ref, part_ref, to_next_ref, to_prev_ref, acc, edge_acc):
    block, iz = place()
    row = rows_of()
    shift = jnp.where(block >= 2, 1, 127)
    full_at, odd_at = powers()
    acc[...] = jnp.zeros_like(acc)
    edge_acc[...] = jnp.zeros_like(edge_acc)
    lane_x = (row.astype(F32) + 0.5) * HX

    def over_y(iy, carry):
        sy = local_y(block, iy)
        courant_y = STEP * jnp.abs(sy)
        sums = [[None] * 5, [None] * 5]
        for ix in range(VX):
            half = 1 if SPEED_X[ix] > 0 else 0
            k = ix % 16
            raw = f_ref[iy * 32 + ix]
            if half:
                to_next_ref[2 * iy + k // 8, k % 8 : k % 8 + 1, :] = raw[7:8, :]
            else:
                to_prev_ref[2 * iy + k // 8, k % 8 : k % 8 + 1, :] = raw[0:1, :]
            value = moved(raw, ix, courant_y, shift, row, 0.0, 0.0)
            for a in range(5):
                term = value if a == 0 else (SPEED_X[ix] ** a) * value
                sums[half][a] = term if sums[half][a] is None else sums[half][a] + term
        power = [1.0, sy, sy * sy, sy * sy * sy, sy * sy * sy * sy]
        full = [sums[1][a] + sums[0][a] for a in range(5)]
        odd = [sums[1][a] - sums[0][a] for a in range(5)]
        for (a, b), n in full_at.items():
            acc[n] = acc[n] + power[b] * full[a]
        for (a, b), n in odd_at.items():
            acc[n] = acc[n] + power[b] * odd[a]
        for side, ref, base in ((0, to_next_ref, 0.0), (1, to_prev_ref, -EDGE)):
            edge = [None] * 5
            for j in range(2):
                sx = lane_x + (base + 8 * HX * j)
                term = (STEP * jnp.abs(sx)) * ref[2 * iy + j]
                for a in range(5):
                    term = term if a == 0 else sx * term
                    edge[a] = term if edge[a] is None else edge[a] + term
            for (a, b), n in full_at.items():
                edge_acc[side, n] = edge_acc[side, n] + power[b] * edge[a]
        return carry

    lax.fori_loop(0, 8, over_y, 0)
    sz = local_z(iz)
    zs = [QUAD * jnp.ones((), F32), QUAD * sz, QUAD * sz * sz, QUAD * sz * sz * sz]
    sign = jnp.where(block >= 2, 1.0, -1.0).astype(F32)
    zy = [sign * z for z in zs]

    def all_sets(full, odd):
        out = [added_up(zs[c] * full(a, b) for a, b, c in monos) for monos in PLAIN]
        out += [added_up(zs[c] * odd(a + 1, b) for a, b, c in monos) for monos in MOMENTS]
        out += [added_up(zy[c] * full(a, b + 1) for a, b, c in monos) for monos in MOMENTS]
        return out

    for i, v in enumerate(all_sets(lambda a, b: acc[full_at[a, b]], lambda a, b: acc[odd_at[a, b]])):
        part_ref[slot_of(i)] = v
    part_ref[6] = jnp.zeros((8, 128), F32)
    for side, where in ((0, row_up), (1, row_down)):
        lines = {p: jnp.sum(edge_acc[side, n], axis=0, keepdims=True) for p, n in full_at.items()}
        factor = -1.0 if side else 1.0
        for i, v in enumerate(
            all_sets(lambda a, b: lines[a, b], lambda a, b: factor * lines[a, b])
        ):
            slot, r = where(i)
            part_ref[slot, r : r + 1, :] = v


def diffuse(own_source, far_source, row):
    own, far = own_source, far_source
    for _ in range(SWEEPS):
        own_down, far_down = pltpu.roll(own, 1, 0), pltpu.roll(far, 1, 0)
        own_up, far_up = pltpu.roll(own, 7, 0), pltpu.roll(far, 7, 0)
        new_own = (
            jnp.where(row == 0, far_down, own_down)
            + jnp.where(row == 7, far_up, own_up)
            + pltpu.roll(own, 1, 1)
            + pltpu.roll(own, 127, 1)
        )
        new_far = (
            jnp.where(row == 0, own_down, far_down)
            + jnp.where(row == 7, own_up, far_up)
            + pltpu.roll(far, 1, 1)
            + pltpu.roll(far, 127, 1)
        )
        own = (own_source + new_own) * 0.2
        far = (far_source + new_far) * 0.2
    return own


def heat_flux(m):
    inv = 1.0 / m[0]
    u = [m[1] * inv, m[2] * inv, m[3] * inv]
    p_zz = m[4] - m[5] - m[6]
    p = [[m[5], m[7], m[8]], [m[7], m[6], m[9]], [m[8], m[9], p_zz]]
    sq = u[0] * u[0] + u[1] * u[1] + u[2] * u[2]
    mass_sq = 2.0 * m[0] * sq
    return [
        0.5
        * (
            m[10 + i]
            - 2.0 * (u[0] * p[i][0] + u[1] * p[i][1] + u[2] * p[i][2])
            + u[i] * (mass_sq - m[4])
        )
        for i in range(3)
    ]


def cell_state(state, moments, rate_class, wall):
    density = state[0]
    inv = 1.0 / density
    u = [state[i] * inv for i in (1, 2, 3)]
    temperature = (2.0 * state[4] * inv - (u[0] * u[0] + u[1] * u[1] + u[2] * u[2])) * (1.0 / 3.0)
    heat = heat_flux(moments)
    frequency = 0.5 * jnp.exp2(rate_class.astype(F32))
    power = jnp.exp((1.0 - 0.81) * jnp.log(temperature))
    keep = jnp.exp(-STEP * frequency * density * power)
    inv_t = 1.0 / temperature
    rate = 1.0 - keep
    skew = ((1.0 - 2.0 / 3.0) / 5.0) * inv * inv_t * inv_t
    amplitude = rate * density * inv_t * lax.rsqrt(temperature)
    solid = wall > 0
    keep = jnp.where(solid, 0.0, keep)
    amplitude = jnp.where(solid, density, amplitude)
    inv_t = jnp.where(solid, 1.0, inv_t)
    u = [jnp.where(solid, 0.0, c) for c in u]
    heat = [jnp.where(solid, 0.0, skew * h) for h in heat]
    return keep, amplitude, inv_t, u, heat


def apply_added(sy, sz, cell):
    _, amplitude, inv_t, u, heat = cell
    dy, dz = sy - u[1], sz - u[2]
    square = (dy * dy + dz * dz) * inv_t
    return amplitude * jnp.exp(-0.5 * square), square - 5.0, dy * heat[1] + dz * heat[2]


def profile_x(cell, profile):
    _, _, inv_t, u, heat = cell
    for ix in range(VX):
        dx = SPEED_X[ix] - u[0]
        square = dx * dx * inv_t
        profile[0, ix] = jnp.exp(-0.5 * square)
        profile[1, ix] = square
        profile[2, ix] = dx * heat[0]


def line_sums(speeds, u, inv_t, top):
    out = [None] * (top + 1)
    for s in speeds:
        d = s - u
        e = jnp.exp(-0.5 * (d * d * inv_t))
        for a in range(top + 1):
            term = e if a == 0 else (s**a) * e
            out[a] = term if out[a] is None else out[a] + term
    return out


def central(raw, u, top):
    table = [raw]
    for _ in range(3):
        last = table[-1]
        table.append([last[a + 1] - u * last[a] for a in range(len(last) - 1)])
    return [line[: top + 1] for line in table]


def added_moments(cell):
    _, amplitude, inv_t, u, heat = cell
    scale = amplitude * QUAD
    half = VX // 2
    x_up = central(line_sums(SPEED_X[half:], u[0], inv_t, 7), u[0], 4)
    x_dn = central(line_sums(SPEED_X[:half], u[0], inv_t, 7), u[0], 4)
    y_up = central(line_sums(SPEED_Y[half:], u[1], inv_t, 7), u[1], 4)
    y_dn = central(line_sums(SPEED_Y[:half], u[1], inv_t, 7), u[1], 4)
    z_all = central([scale * z for z in line_sums(SPEED_Z, u[2], inv_t, 6)], u[2], 3)
    x_all = [[p + q for p, q in zip(r, s)] for r, s in zip(x_up, x_dn)]
    y_all = [[p + q for p, q in zip(r, s)] for r, s in zip(y_up, y_dn)]
    gx, gy, gz = heat
    hx, hy, hz = gx * inv_t, gy * inv_t, gz * inv_t

    def whole(xs, ys):
        plane = {}

        def at(a, b):
            if (a, b) not in plane:
                x = [xs[i][a] for i in range(4)]
                y = [ys[i][b] for i in range(4)]
                x0y0 = x[0] * y[0]
                x1y0, x0y1 = x[1] * y[0], x[0] * y[1]
                x2y0, x0y2 = x[2] * y[0], x[0] * y[2]
                p0 = (
                    x0y0
                    + hx * (x[3] * y[0] + x[1] * y[2])
                    + hy * (x[2] * y[1] + x[0] * y[3])
                    - 5.0 * (gx * x1y0 + gy * x0y1)
                )
                p1 = hz * (x2y0 + x0y2) - 5.0 * gz * x0y0
                p2 = hx * x1y0 + hy * x0y1
                p3 = hz * x0y0
                plane[a, b] = (p0, p1, p2, p3)
            return plane[a, b]

        out = []
        for monos in MOMENTS:
            total = None
            for a, b, c in monos:
                p = at(a, b)
                term = (
                    p[0] * z_all[0][c] + p[1] * z_all[1][c] + p[2] * z_all[2][c] + p[3] * z_all[3][c]
                )
                total = term if total is None else total + term
            out.append(total)
        return out

    def weighted(table, factor):
        return [[factor * v for v in line[1:5]] for line in table]

    return (
        whole(x_all, y_all),
        whole(weighted(x_up, STEP), y_all),
        whole(weighted(x_dn, -STEP), y_all),
        whole(x_all, weighted(y_up, STEP)),
        whole(x_all, weighted(y_dn, -STEP)),
    )


def first_kernel(
    q_ref, prev_ref, next_ref, before_ref, after_ref, class_ref, wall_ref, t_ref,
    f_ref, m_ref, add_ref, to_next_ref, to_prev_ref, profile,
):
    block, iz = place()
    row = rows_of()
    shift = jnp.where(block >= 2, 1, 127)

    def line(ref, first, at):
        return ref[at[0] - first, at[1] : at[1] + 1, :]

    def whole_set(i):
        above, below = line(prev_ref, 0, row_up(i)), line(next_ref, 6, row_down(i))
        return q_ref[slot_of(i)] + jnp.where(row == 0, above, jnp.where(row == 7, below, 0.0))

    sets = [whole_set(i) for i in range(SETS)]
    scale = [1.0, 1.0, 1.0, 1.0, 0.5]
    state = []
    for k in range(5):
        far = jnp.where(row < 4, next_ref[1 + k], prev_ref[FIRST_SET + k])
        up, down = line(q_ref, 0, row_up(k)), line(q_ref, 0, row_down(k))
        far = far + jnp.where(row == 0, up, jnp.where(row == 7, down, 0.0))
        state.append(diffuse(scale[k] * sets[k], scale[k] * far, row))
    cell = cell_state(state, sets[:13], class_ref[...], wall_ref[...])
    keep = cell[0]
    profile_x(cell, profile)
    sz = local_z(iz)

    def over_y(iy, carry):
        sy = local_y(block, iy)
        courant_y = STEP * jnp.abs(sy)
        base, square, flux = apply_added(sy, sz, cell)
        for ix in range(VX):
            k = ix % 16
            edge = (before_ref if SPEED_X[ix] > 0 else after_ref)[
                2 * iy + k // 8, k % 8 : k % 8 + 1, :
            ]
            value = moved(t_ref[iy * 32 + ix], ix, courant_y, shift, row, edge, edge)
            added = (base * profile[0, ix]) * (
                1.0 + (flux + profile[2, ix]) * (square + profile[1, ix])
            )
            value = keep * value + added
            f_ref[iy * 32 + ix] = value
            if SPEED_X[ix] > 0:
                to_next_ref[6 + 2 * iy + k // 8, k % 8 : k % 8 + 1, :] = value[7:8, :]
            else:
                to_prev_ref[6 + 2 * iy + k // 8, k % 8 : k % 8 + 1, :] = value[0:1, :]
        return carry

    lax.fori_loop(0, 8, over_y, 0)

    g_all, g_xu, g_xd, g_yu, g_yd = added_moments(cell)
    part = 0.5 * STEP * keep
    for k, monos in enumerate(MOMENTS):
        sx_k, ax_k = sets[AT[key_of(times(monos, 0))]], sets[ABS_X + k]
        sy_k, ay_k = sets[AT[key_of(times(monos, 1))]], sets[ABS_Y + k]
        x_up = part * (ax_k + sx_k) + g_xu[k]
        x_dn = part * (ax_k - sx_k) + g_xd[k]
        y_up = part * (ay_k + sy_k) + g_yu[k]
        y_dn = part * (ay_k - sy_k) + g_yd[k]
        from_up, from_dn = pltpu.roll(x_up, 1, 0), pltpu.roll(x_dn, 7, 0)
        total = (
            (keep * sets[k] + g_all[k] - x_up - x_dn - y_up - y_dn)
            + jnp.where(row == 0, 0.0, from_up)
            + jnp.where(row == 7, 0.0, from_dn)
            + pltpu.roll(y_up, 1, 1)
            + pltpu.roll(y_dn, 127, 1)
        )
        m_ref[k] = total
        if k < 5:
            add_ref[k] = jnp.where(row == 0, from_up, jnp.where(row == 7, from_dn, 0.0))
            to_next_ref[k] = jnp.where(row == 0, from_up, total)
            to_prev_ref[k] = jnp.where(row == 7, from_dn, total)
        else:
            to_next_ref[5, k - 5 : k - 4, :] = x_up[7:8, :]
            to_prev_ref[5, k - 5 : k - 4, :] = x_dn[0:1, :]


def second_kernel(
    m_ref, add_ref, prev_ref, next_ref, class_ref, wall_ref, f_ref,
    out_ref, state_ref, profile,
):
    block, iz = place()
    row = rows_of()
    shift = jnp.where(block >= 2, 1, 127)
    moments = []
    for k in range(13):
        if k < 5:
            before, after = prev_ref[k], next_ref[k]
        else:
            before, after = prev_ref[5, k - 5 : k - 4, :], next_ref[5, k - 5 : k - 4, :]
        moments.append(
            m_ref[k] + jnp.where(row == 0, before, jnp.where(row == 7, after, 0.0))
        )
    scale = [1.0, 1.0, 1.0, 1.0, 0.5]
    state = []
    for k in range(5):
        far = jnp.where(row < 4, next_ref[k], prev_ref[k]) + add_ref[k]
        state.append(diffuse(scale[k] * moments[k], scale[k] * far, row))
        state_ref[k] = state[k]
    cell = cell_state(state, moments, class_ref[...], wall_ref[...])
    keep = cell[0]
    profile_x(cell, profile)
    sz = local_z(iz)

    def over_y(iy, carry):
        sy = local_y(block, iy)
        courant_y = STEP * jnp.abs(sy)
        base, square, flux = apply_added(sy, sz, cell)
        for ix in range(VX):
            k = ix % 16
            edge = (prev_ref if SPEED_X[ix] > 0 else next_ref)[
                6 + 2 * iy + k // 8, k % 8 : k % 8 + 1, :
            ]
            value = moved(f_ref[iy * 32 + ix], ix, courant_y, shift, row, edge, edge)
            added = (base * profile[0, ix]) * (
                1.0 + (flux + profile[2, ix]) * (square + profile[1, ix])
            )
            out_ref[iy * 32 + ix] = keep * value + added
        return carry

    lax.fori_loop(0, 8, over_y, 0)


def kernel_call(body, outs, scratch, limit=32):
    return pl.pallas_call(
        body,
        out_shape=[jax.ShapeDtypeStruct(s, F32) for s in outs],
        scratch_shapes=[pltpu.VMEM(s, F32) for s in scratch],
        compiler_params=pltpu.CompilerParams(vmem_limit_bytes=limit * 1024 * 1024),
    )


def to_both(up_value, down_value):
    size = lax.axis_size("space")
    up = [(i, (i + 1) % size) for i in range(size)]
    down = [(j, i) for i, j in up]
    return lax.ppermute(up_value, "space", up), lax.ppermute(down_value, "space", down)


NEAR = [[(4 * z + k) * 4 + y for k in range(4) for y in range(4)] for z in range(4)]
FAR = [[(z + 4 * ((k + 2) % 4)) * 4 + y for k in range(4)] for z in range(4) for y in range(4)]


def all_sum(part, beside):
    piece = part.reshape(16, SLOTS // 2, 128)
    piece = lax.all_to_all(piece, "vel", 0, 0, tiled=True, axis_index_groups=NEAR)
    piece, beside = lax.optimization_barrier((piece, beside))
    mine = jnp.sum(piece, 0)
    piece = jnp.broadcast_to(mine[None], (4,) + mine.shape)
    piece = lax.all_to_all(piece, "vel", 0, 0, tiled=True, axis_index_groups=FAR)
    mine = jnp.sum(piece, 0)
    piece = jnp.broadcast_to(mine[None], (16,) + mine.shape)
    piece = lax.all_to_all(piece, "vel", 0, 0, tiled=True, axis_index_groups=NEAR)
    return piece.reshape(SLOTS, 8, 128), beside


def per_device(distribution, rate_class, wall):
    block, edges, small = (256, 8, 128), (16, 8, 128), (22, 8, 128)
    part, to_next, to_prev = kernel_call(
        moments_kernel,
        [(SLOTS, 8, 128), edges, edges],
        [(25, 8, 128), (2, 15, 8, 128)],
    )(distribution)
    sums, (before, after) = all_sum(part, to_both(to_next, to_prev))
    prev, following = to_both(sums[:12], sums[6:18])
    field, moments, extra, to_next, to_prev = kernel_call(
        first_kernel, [block, (13, 8, 128), (5, 8, 128), small, small], [(3, 32, 8, 128)]
    )(sums, prev, following, before, after, rate_class, wall, distribution)
    prev, following = to_both(to_next, to_prev)
    field, state = kernel_call(
        second_kernel,
        [block, (5, 8, 128)],
        [(3, 32, 8, 128)],
    )(moments, extra, prev, following, rate_class, wall, field)
    return field, state


def solution(mesh):
    return jax.shard_map(
        per_device,
        mesh=mesh,
        in_specs=(P("vel", "space", None), P("space", None), P("space", None)),
        out_specs=(P("vel", "space", None), P(None, "space", None)),
        check_vma=False,
    )
```

```python
import jax
import jax.numpy as jnp
import numpy as np
from jax import lax
from jax.experimental import pallas as pl
from jax.experimental.pallas import tpu as pltpu
from jax.sharding import PartitionSpec as P

VX, VY, VZ = 32, 32, 16
SWEEPS = 4
EDGE = 5.0
STEP = 0.1
HX = 2.0 * EDGE / VX
HY = 2.0 * EDGE / VY
HZ = 2.0 * EDGE / VZ
QUAD = float(HX * HY * HZ / (2.0 * np.pi) ** 1.5)
SPEED_X = [-EDGE + (i + 0.5) * HX for i in range(VX)]
SPEED_Y = [-EDGE + (i + 0.5) * HY for i in range(VY)]
SPEED_Z = [-EDGE + (i + 0.5) * HZ for i in range(VZ)]
F32 = jnp.float32

MOMENTS = [
    ((0, 0, 0),),
    ((1, 0, 0),),
    ((0, 1, 0),),
    ((0, 0, 1),),
    ((2, 0, 0), (0, 2, 0), (0, 0, 2)),
    ((2, 0, 0),),
    ((0, 2, 0),),
    ((1, 1, 0),),
    ((1, 0, 1),),
    ((0, 1, 1),),
    ((3, 0, 0), (1, 2, 0), (1, 0, 2)),
    ((2, 1, 0), (0, 3, 0), (0, 1, 2)),
    ((2, 0, 1), (0, 2, 1), (0, 0, 3)),
]


def times(moment, axis):
    return tuple(tuple(p + (d == axis) for d, p in enumerate(m)) for m in moment)


def key_of(moment):
    return tuple(sorted(moment))


PLAIN = []
for _m in MOMENTS + [times(m, 0) for m in MOMENTS] + [times(m, 1) for m in MOMENTS]:
    if key_of(_m) not in PLAIN:
        PLAIN.append(key_of(_m))
AT = {k: i for i, k in enumerate(PLAIN)}
ABS_X = len(PLAIN)
ABS_Y = ABS_X + 13
SETS = ABS_Y + 13
SLOTS = 64
FIRST_SET = 7


def slot_of(i):
    return FIRST_SET + i if i < 5 else FIRST_SET + 6 + i


def row_up(i):
    return (i // 8, i % 8) if i < 48 else (6, i - 48)


def row_down(i):
    return (12 + i // 8, i % 8) if i < 48 else (6, i - 45)


def rows_of():
    return lax.broadcasted_iota(jnp.int32, (8, 128), 0)


def added_up(terms):
    total = None
    for t in terms:
        total = t if total is None else total + t
    return total


def place():
    vel = lax.axis_index("vel")
    return lax.rem(vel, 4), lax.div(vel, 4)


def local_y(block, iy):
    return -EDGE + ((block * 8 + iy).astype(F32) + 0.5) * HY


def local_z(iz):
    return -EDGE + (iz.astype(F32) + 0.5) * HZ


def moved(value, ix, courant_y, shift, row, before, after):
    courant_x = STEP * abs(SPEED_X[ix])
    if SPEED_X[ix] > 0:
        beside = jnp.where(row == 0, before, pltpu.roll(value, 1, 0))
    else:
        beside = jnp.where(row == 7, after, pltpu.roll(value, 7, 0))
    along = pltpu.roll(value, shift, 1)
    return ((1.0 - courant_x) - courant_y) * value + courant_x * beside + courant_y * along


def powers():
    full = [(a, b) for a in range(5) for b in range(5 - a)]
    odd = [(a, b) for a in range(1, 5) for b in range(5 - a)]
    return {p: i for i, p in enumerate(full)}, {p: 15 + i for i, p in enumerate(odd)}


def moments_kernel(f_ref, part_ref, to_next_ref, to_prev_ref, acc, edge_acc):
    block, iz = place()
    row = rows_of()
    shift = jnp.where(block >= 2, 1, 127)
    full_at, odd_at = powers()
    acc[...] = jnp.zeros_like(acc)
    edge_acc[...] = jnp.zeros_like(edge_acc)
    lane_x = (row.astype(F32) + 0.5) * HX

    def over_y(iy, carry):
        sy = local_y(block, iy)
        courant_y = STEP * jnp.abs(sy)
        sums = [[None] * 5, [None] * 5]
        for ix in range(VX):
            half = 1 if SPEED_X[ix] > 0 else 0
            k = ix % 16
            raw = f_ref[iy * 32 + ix]
            if half:
                to_next_ref[2 * iy + k // 8, k % 8 : k % 8 + 1, :] = raw[7:8, :]
            else:
                to_prev_ref[2 * iy + k // 8, k % 8 : k % 8 + 1, :] = raw[0:1, :]
            value = moved(raw, ix, courant_y, shift, row, 0.0, 0.0)
            for a in range(5):
                term = value if a == 0 else (SPEED_X[ix] ** a) * value
                sums[half][a] = term if sums[half][a] is None else sums[half][a] + term
        power = [1.0, sy, sy * sy, sy * sy * sy, sy * sy * sy * sy]
        full = [sums[1][a] + sums[0][a] for a in range(5)]
        odd = [sums[1][a] - sums[0][a] for a in range(5)]
        for (a, b), n in full_at.items():
            acc[n] = acc[n] + power[b] * full[a]
        for (a, b), n in odd_at.items():
            acc[n] = acc[n] + power[b] * odd[a]
        for side, ref, base in ((0, to_next_ref, 0.0), (1, to_prev_ref, -EDGE)):
            edge = [None] * 5
            for j in range(2):
                sx = lane_x + (base + 8 * HX * j)
                term = (STEP * jnp.abs(sx)) * ref[2 * iy + j]
                for a in range(5):
                    term = term if a == 0 else sx * term
                    edge[a] = term if edge[a] is None else edge[a] + term
            for (a, b), n in full_at.items():
                edge_acc[side, n] = edge_acc[side, n] + power[b] * edge[a]
        return carry

    lax.fori_loop(0, 8, over_y, 0)
    sz = local_z(iz)
    zs = [QUAD * jnp.ones((), F32), QUAD * sz, QUAD * sz * sz, QUAD * sz * sz * sz]
    sign = jnp.where(block >= 2, 1.0, -1.0).astype(F32)
    zy = [sign * z for z in zs]

    def all_sets(full, odd):
        out = [added_up(zs[c] * full(a, b) for a, b, c in monos) for monos in PLAIN]
        out += [added_up(zs[c] * odd(a + 1, b) for a, b, c in monos) for monos in MOMENTS]
        out += [added_up(zy[c] * full(a, b + 1) for a, b, c in monos) for monos in MOMENTS]
        return out

    for i, v in enumerate(all_sets(lambda a, b: acc[full_at[a, b]], lambda a, b: acc[odd_at[a, b]])):
        part_ref[slot_of(i)] = v
    part_ref[6] = jnp.zeros((8, 128), F32)
    for side, where in ((0, row_up), (1, row_down)):
        lines = {p: jnp.sum(edge_acc[side, n], axis=0, keepdims=True) for p, n in full_at.items()}
        factor = -1.0 if side else 1.0
        for i, v in enumerate(
            all_sets(lambda a, b: lines[a, b], lambda a, b: factor * lines[a, b])
        ):
            slot, r = where(i)
            part_ref[slot, r : r + 1, :] = v


def diffuse(own_source, far_source, row):
    own, far = own_source, far_source
    for _ in range(SWEEPS):
        own_down, far_down = pltpu.roll(own, 1, 0), pltpu.roll(far, 1, 0)
        own_up, far_up = pltpu.roll(own, 7, 0), pltpu.roll(far, 7, 0)
        new_own = (
            jnp.where(row == 0, far_down, own_down)
            + jnp.where(row == 7, far_up, own_up)
            + pltpu.roll(own, 1, 1)
            + pltpu.roll(own, 127, 1)
        )
        new_far = (
            jnp.where(row == 0, own_down, far_down)
            + jnp.where(row == 7, own_up, far_up)
            + pltpu.roll(far, 1, 1)
            + pltpu.roll(far, 127, 1)
        )
        own = (own_source + new_own) * 0.2
        far = (far_source + new_far) * 0.2
    return own


def heat_flux(m):
    inv = 1.0 / m[0]
    u = [m[1] * inv, m[2] * inv, m[3] * inv]
    p_zz = m[4] - m[5] - m[6]
    p = [[m[5], m[7], m[8]], [m[7], m[6], m[9]], [m[8], m[9], p_zz]]
    sq = u[0] * u[0] + u[1] * u[1] + u[2] * u[2]
    mass_sq = 2.0 * m[0] * sq
    return [
        0.5
        * (
            m[10 + i]
            - 2.0 * (u[0] * p[i][0] + u[1] * p[i][1] + u[2] * p[i][2])
            + u[i] * (mass_sq - m[4])
        )
        for i in range(3)
    ]


def cell_state(state, moments, rate_class, wall):
    density = state[0]
    inv = 1.0 / density
    u = [state[i] * inv for i in (1, 2, 3)]
    temperature = (2.0 * state[4] * inv - (u[0] * u[0] + u[1] * u[1] + u[2] * u[2])) * (1.0 / 3.0)
    heat = heat_flux(moments)
    frequency = 0.5 * jnp.exp2(rate_class.astype(F32))
    power = jnp.exp((1.0 - 0.81) * jnp.log(temperature))
    keep = jnp.exp(-STEP * frequency * density * power)
    inv_t = 1.0 / temperature
    rate = 1.0 - keep
    skew = ((1.0 - 2.0 / 3.0) / 5.0) * inv * inv_t * inv_t
    amplitude = rate * density * inv_t * lax.rsqrt(temperature)
    solid = wall > 0
    keep = jnp.where(solid, 0.0, keep)
    amplitude = jnp.where(solid, density, amplitude)
    inv_t = jnp.where(solid, 1.0, inv_t)
    u = [jnp.where(solid, 0.0, c) for c in u]
    heat = [jnp.where(solid, 0.0, skew * h) for h in heat]
    return keep, amplitude, inv_t, u, heat


def apply_added(sy, sz, cell):
    _, amplitude, inv_t, u, heat = cell
    dy, dz = sy - u[1], sz - u[2]
    square = (dy * dy + dz * dz) * inv_t
    return amplitude * jnp.exp(-0.5 * square), square - 5.0, dy * heat[1] + dz * heat[2]


def profile_x(cell, profile):
    _, _, inv_t, u, heat = cell
    for ix in range(VX):
        dx = SPEED_X[ix] - u[0]
        square = dx * dx * inv_t
        profile[0, ix] = jnp.exp(-0.5 * square)
        profile[1, ix] = square
        profile[2, ix] = dx * heat[0]


def line_sums(speeds, u, inv_t, top):
    out = [None] * (top + 1)
    for s in speeds:
        d = s - u
        e = jnp.exp(-0.5 * (d * d * inv_t))
        for a in range(top + 1):
            term = e if a == 0 else (s**a) * e
            out[a] = term if out[a] is None else out[a] + term
    return out


def central(raw, u, top):
    table = [raw]
    for _ in range(3):
        last = table[-1]
        table.append([last[a + 1] - u * last[a] for a in range(len(last) - 1)])
    return [line[: top + 1] for line in table]


def added_moments(cell):
    _, amplitude, inv_t, u, heat = cell
    scale = amplitude * QUAD
    half = VX // 2
    x_up = central(line_sums(SPEED_X[half:], u[0], inv_t, 7), u[0], 4)
    x_dn = central(line_sums(SPEED_X[:half], u[0], inv_t, 7), u[0], 4)
    y_up = central(line_sums(SPEED_Y[half:], u[1], inv_t, 7), u[1], 4)
    y_dn = central(line_sums(SPEED_Y[:half], u[1], inv_t, 7), u[1], 4)
    z_all = central([scale * z for z in line_sums(SPEED_Z, u[2], inv_t, 6)], u[2], 3)
    x_all = [[p + q for p, q in zip(r, s)] for r, s in zip(x_up, x_dn)]
    y_all = [[p + q for p, q in zip(r, s)] for r, s in zip(y_up, y_dn)]
    gx, gy, gz = heat
    hx, hy, hz = gx * inv_t, gy * inv_t, gz * inv_t

    def whole(xs, ys):
        plane = {}

        def at(a, b):
            if (a, b) not in plane:
                x = [xs[i][a] for i in range(4)]
                y = [ys[i][b] for i in range(4)]
                x0y0 = x[0] * y[0]
                x1y0, x0y1 = x[1] * y[0], x[0] * y[1]
                x2y0, x0y2 = x[2] * y[0], x[0] * y[2]
                p0 = (
                    x0y0
                    + hx * (x[3] * y[0] + x[1] * y[2])
                    + hy * (x[2] * y[1] + x[0] * y[3])
                    - 5.0 * (gx * x1y0 + gy * x0y1)
                )
                p1 = hz * (x2y0 + x0y2) - 5.0 * gz * x0y0
                p2 = hx * x1y0 + hy * x0y1
                p3 = hz * x0y0
                plane[a, b] = (p0, p1, p2, p3)
            return plane[a, b]

        out = []
        for monos in MOMENTS:
            total = None
            for a, b, c in monos:
                p = at(a, b)
                term = (
                    p[0] * z_all[0][c] + p[1] * z_all[1][c] + p[2] * z_all[2][c] + p[3] * z_all[3][c]
                )
                total = term if total is None else total + term
            out.append(total)
        return out

    def weighted(table, factor):
        return [[factor * v for v in line[1:5]] for line in table]

    return (
        whole(x_all, y_all),
        whole(weighted(x_up, STEP), y_all),
        whole(weighted(x_dn, -STEP), y_all),
        whole(x_all, weighted(y_up, STEP)),
        whole(x_all, weighted(y_dn, -STEP)),
    )


def first_kernel(
    q_ref, prev_ref, next_ref, before_ref, after_ref, class_ref, wall_ref, t_ref,
    f_ref, m_ref, add_ref, to_next_ref, to_prev_ref, profile,
):
    block, iz = place()
    row = rows_of()
    shift = jnp.where(block >= 2, 1, 127)

    def line(ref, first, at):
        return ref[at[0] - first, at[1] : at[1] + 1, :]

    def whole_set(i):
        above, below = line(prev_ref, 0, row_up(i)), line(next_ref, 6, row_down(i))
        return q_ref[slot_of(i)] + jnp.where(row == 0, above, jnp.where(row == 7, below, 0.0))

    sets = [whole_set(i) for i in range(SETS)]
    scale = [1.0, 1.0, 1.0, 1.0, 0.5]
    state = []
    for k in range(5):
        far = jnp.where(row < 4, next_ref[1 + k], prev_ref[FIRST_SET + k])
        up, down = line(q_ref, 0, row_up(k)), line(q_ref, 0, row_down(k))
        far = far + jnp.where(row == 0, up, jnp.where(row == 7, down, 0.0))
        state.append(diffuse(scale[k] * sets[k], scale[k] * far, row))
    cell = cell_state(state, sets[:13], class_ref[...], wall_ref[...])
    keep = cell[0]
    profile_x(cell, profile)
    sz = local_z(iz)

    def over_y(iy, carry):
        sy = local_y(block, iy)
        courant_y = STEP * jnp.abs(sy)
        base, square, flux = apply_added(sy, sz, cell)
        for ix in range(VX):
            k = ix % 16
            edge = (before_ref if SPEED_X[ix] > 0 else after_ref)[
                2 * iy + k // 8, k % 8 : k % 8 + 1, :
            ]
            value = moved(t_ref[iy * 32 + ix], ix, courant_y, shift, row, edge, edge)
            added = (base * profile[0, ix]) * (
                1.0 + (flux + profile[2, ix]) * (square + profile[1, ix])
            )
            value = keep * value + added
            f_ref[iy * 32 + ix] = value
            if SPEED_X[ix] > 0:
                to_next_ref[6 + 2 * iy + k // 8, k % 8 : k % 8 + 1, :] = value[7:8, :]
            else:
                to_prev_ref[6 + 2 * iy + k // 8, k % 8 : k % 8 + 1, :] = value[0:1, :]
        return carry

    lax.fori_loop(0, 8, over_y, 0)

    g_all, g_xu, g_xd, g_yu, g_yd = added_moments(cell)
    part = 0.5 * STEP * keep
    for k, monos in enumerate(MOMENTS):
        sx_k, ax_k = sets[AT[key_of(times(monos, 0))]], sets[ABS_X + k]
        sy_k, ay_k = sets[AT[key_of(times(monos, 1))]], sets[ABS_Y + k]
        x_up = part * (ax_k + sx_k) + g_xu[k]
        x_dn = part * (ax_k - sx_k) + g_xd[k]
        y_up = part * (ay_k + sy_k) + g_yu[k]
        y_dn = part * (ay_k - sy_k) + g_yd[k]
        from_up, from_dn = pltpu.roll(x_up, 1, 0), pltpu.roll(x_dn, 7, 0)
        total = (
            (keep * sets[k] + g_all[k] - x_up - x_dn - y_up - y_dn)
            + jnp.where(row == 0, 0.0, from_up)
            + jnp.where(row == 7, 0.0, from_dn)
            + pltpu.roll(y_up, 1, 1)
            + pltpu.roll(y_dn, 127, 1)
        )
        m_ref[k] = total
        if k < 5:
            add_ref[k] = jnp.where(row == 0, from_up, jnp.where(row == 7, from_dn, 0.0))
            to_next_ref[k] = jnp.where(row == 0, from_up, total)
            to_prev_ref[k] = jnp.where(row == 7, from_dn, total)
        else:
            to_next_ref[5, k - 5 : k - 4, :] = x_up[7:8, :]
            to_prev_ref[5, k - 5 : k - 4, :] = x_dn[0:1, :]


def second_kernel(
    m_ref, add_ref, prev_ref, next_ref, class_ref, wall_ref, f_ref,
    out_ref, state_ref, profile,
):
    block, iz = place()
    row = rows_of()
    shift = jnp.where(block >= 2, 1, 127)
    moments = []
    for k in range(13):
        if k < 5:
            before, after = prev_ref[k], next_ref[k]
        else:
            before, after = prev_ref[5, k - 5 : k - 4, :], next_ref[5, k - 5 : k - 4, :]
        moments.append(
            m_ref[k] + jnp.where(row == 0, before, jnp.where(row == 7, after, 0.0))
        )
    scale = [1.0, 1.0, 1.0, 1.0, 0.5]
    state = []
    for k in range(5):
        far = jnp.where(row < 4, next_ref[k], prev_ref[k]) + add_ref[k]
        state.append(diffuse(scale[k] * moments[k], scale[k] * far, row))
        state_ref[k] = state[k]
    cell = cell_state(state, moments, class_ref[...], wall_ref[...])
    keep = cell[0]
    profile_x(cell, profile)
    sz = local_z(iz)

    def over_y(iy, carry):
        sy = local_y(block, iy)
        courant_y = STEP * jnp.abs(sy)
        base, square, flux = apply_added(sy, sz, cell)
        for ix in range(VX):
            k = ix % 16
            edge = (prev_ref if SPEED_X[ix] > 0 else next_ref)[
                6 + 2 * iy + k // 8, k % 8 : k % 8 + 1, :
            ]
            value = moved(f_ref[iy * 32 + ix], ix, courant_y, shift, row, edge, edge)
            added = (base * profile[0, ix]) * (
                1.0 + (flux + profile[2, ix]) * (square + profile[1, ix])
            )
            out_ref[iy * 32 + ix] = keep * value + added
        return carry

    lax.fori_loop(0, 8, over_y, 0)


def kernel_call(body, outs, scratch, limit=32):
    return pl.pallas_call(
        body,
        out_shape=[jax.ShapeDtypeStruct(s, F32) for s in outs],
        scratch_shapes=[pltpu.VMEM(s, F32) for s in scratch],
        compiler_params=pltpu.CompilerParams(vmem_limit_bytes=limit * 1024 * 1024),
    )


def to_both(up_value, down_value):
    size = lax.axis_size("space")
    up = [(i, (i + 1) % size) for i in range(size)]
    down = [(j, i) for i, j in up]
    return lax.ppermute(up_value, "space", up), lax.ppermute(down_value, "space", down)


NEAR = [
    [(4 * b + k) * 4 + y for k in order for y in (2, 3, 0, 1)]
    for b, order in enumerate(((1, 0, 2, 3), (2, 3, 1, 0), (1, 0, 2, 3), (1, 0, 2, 3)))
]
FAR = [[NEAR[b][p] for b in (2, 3, 0, 1)] for p in range(16)]


def all_sum(part, beside):
    piece = part.reshape(16, SLOTS // 2, 128)
    piece = lax.all_to_all(piece, "vel", 0, 0, tiled=True, axis_index_groups=NEAR)
    piece, beside = lax.optimization_barrier((piece, beside))
    mine = jnp.sum(piece, 0)
    piece = jnp.broadcast_to(mine[None], (4,) + mine.shape)
    piece = lax.all_to_all(piece, "vel", 0, 0, tiled=True, axis_index_groups=FAR)
    mine = jnp.sum(piece, 0)
    piece = jnp.broadcast_to(mine[None], (16,) + mine.shape)
    piece = lax.all_to_all(piece, "vel", 0, 0, tiled=True, axis_index_groups=NEAR)
    return piece.reshape(SLOTS, 8, 128), beside


def per_device(distribution, rate_class, wall):
    block, edges, small = (256, 8, 128), (16, 8, 128), (22, 8, 128)
    part, to_next, to_prev = kernel_call(
        moments_kernel,
        [(SLOTS, 8, 128), edges, edges],
        [(25, 8, 128), (2, 15, 8, 128)],
    )(distribution)
    sums, (before, after) = all_sum(part, to_both(to_next, to_prev))
    prev, following = to_both(sums[:12], sums[6:18])
    field, moments, extra, to_next, to_prev = kernel_call(
        first_kernel, [block, (13, 8, 128), (5, 8, 128), small, small], [(3, 32, 8, 128)]
    )(sums, prev, following, before, after, rate_class, wall, distribution)
    prev, following = to_both(to_next, to_prev)
    field, state = kernel_call(
        second_kernel,
        [block, (5, 8, 128)],
        [(3, 32, 8, 128)],
    )(moments, extra, prev, following, rate_class, wall, field)
    return field, state


def solution(mesh):
    return jax.shard_map(
        per_device,
        mesh=mesh,
        in_specs=(P("vel", "space", None), P("space", None), P("space", None)),
        out_specs=(P("vel", "space", None), P(None, "space", None)),
        check_vma=False,
    )
```

```python
import jax
import jax.numpy as jnp
import numpy as np
from jax import lax
from jax.experimental import pallas as pl
from jax.experimental.pallas import tpu as pltpu
from jax.sharding import PartitionSpec as P

VX, VY, VZ = 32, 32, 16
SWEEPS = 4
EDGE = 5.0
STEP = 0.1
HX = 2.0 * EDGE / VX
HY = 2.0 * EDGE / VY
HZ = 2.0 * EDGE / VZ
QUAD = float(HX * HY * HZ / (2.0 * np.pi) ** 1.5)
SPEED_X = [-EDGE + (i + 0.5) * HX for i in range(VX)]
SPEED_Y = [-EDGE + (i + 0.5) * HY for i in range(VY)]
SPEED_Z = [-EDGE + (i + 0.5) * HZ for i in range(VZ)]
F32 = jnp.float32

MOMENTS = [
    ((0, 0, 0),),
    ((1, 0, 0),),
    ((0, 1, 0),),
    ((0, 0, 1),),
    ((2, 0, 0), (0, 2, 0), (0, 0, 2)),
    ((2, 0, 0),),
    ((0, 2, 0),),
    ((1, 1, 0),),
    ((1, 0, 1),),
    ((0, 1, 1),),
    ((3, 0, 0), (1, 2, 0), (1, 0, 2)),
    ((2, 1, 0), (0, 3, 0), (0, 1, 2)),
    ((2, 0, 1), (0, 2, 1), (0, 0, 3)),
]


def times(moment, axis):
    return tuple(tuple(p + (d == axis) for d, p in enumerate(m)) for m in moment)


def key_of(moment):
    return tuple(sorted(moment))


PLAIN = []
for _m in MOMENTS + [times(m, 0) for m in MOMENTS] + [times(m, 1) for m in MOMENTS]:
    if key_of(_m) not in PLAIN:
        PLAIN.append(key_of(_m))
AT = {k: i for i, k in enumerate(PLAIN)}
ABS_X = len(PLAIN)
ABS_Y = ABS_X + 13
SETS = ABS_Y + 13
SLOTS = 64
FIRST_SET = 7


def slot_of(i):
    return FIRST_SET + i if i < 5 else FIRST_SET + 6 + i


def row_up(i):
    return (i // 8, i % 8) if i < 48 else (6, i - 48)


def row_down(i):
    return (12 + i // 8, i % 8) if i < 48 else (6, i - 45)


def rows_of():
    return lax.broadcasted_iota(jnp.int32, (8, 128), 0)


def added_up(terms):
    total = None
    for t in terms:
        total = t if total is None else total + t
    return total


def place():
    vel = lax.axis_index("vel")
    return lax.rem(vel, 4), lax.div(vel, 4)


def local_y(block, iy):
    return -EDGE + ((block * 8 + iy).astype(F32) + 0.5) * HY


def local_z(iz):
    return -EDGE + (iz.astype(F32) + 0.5) * HZ


def moved(value, ix, courant_y, shift, row, before, after):
    courant_x = STEP * abs(SPEED_X[ix])
    if SPEED_X[ix] > 0:
        beside = jnp.where(row == 0, before, pltpu.roll(value, 1, 0))
    else:
        beside = jnp.where(row == 7, after, pltpu.roll(value, 7, 0))
    along = pltpu.roll(value, shift, 1)
    return ((1.0 - courant_x) - courant_y) * value + courant_x * beside + courant_y * along


def powers():
    full = [(a, b) for a in range(5) for b in range(5 - a)]
    odd = [(a, b) for a in range(1, 5) for b in range(5 - a)]
    return {p: i for i, p in enumerate(full)}, {p: 15 + i for i, p in enumerate(odd)}


def moments_kernel(f_ref, part_ref, to_next_ref, to_prev_ref, acc, edge_acc):
    block, iz = place()
    row = rows_of()
    shift = jnp.where(block >= 2, 1, 127)
    full_at, odd_at = powers()
    acc[...] = jnp.zeros_like(acc)
    edge_acc[...] = jnp.zeros_like(edge_acc)
    lane_x = (row.astype(F32) + 0.5) * HX

    def over_y(iy, carry):
        sy = local_y(block, iy)
        courant_y = STEP * jnp.abs(sy)
        sums = [[None] * 5, [None] * 5]
        for ix in range(VX):
            half = 1 if SPEED_X[ix] > 0 else 0
            k = ix % 16
            raw = f_ref[iy * 32 + ix]
            if half:
                to_next_ref[2 * iy + k // 8, k % 8 : k % 8 + 1, :] = raw[7:8, :]
            else:
                to_prev_ref[2 * iy + k // 8, k % 8 : k % 8 + 1, :] = raw[0:1, :]
            value = moved(raw, ix, courant_y, shift, row, 0.0, 0.0)
            for a in range(5):
                term = value if a == 0 else (SPEED_X[ix] ** a) * value
                sums[half][a] = term if sums[half][a] is None else sums[half][a] + term
        power = [1.0, sy, sy * sy, sy * sy * sy, sy * sy * sy * sy]
        full = [sums[1][a] + sums[0][a] for a in range(5)]
        odd = [sums[1][a] - sums[0][a] for a in range(5)]
        for (a, b), n in full_at.items():
            acc[n] = acc[n] + power[b] * full[a]
        for (a, b), n in odd_at.items():
            acc[n] = acc[n] + power[b] * odd[a]
        for side, ref, base in ((0, to_next_ref, 0.0), (1, to_prev_ref, -EDGE)):
            edge = [None] * 5
            for j in range(2):
                sx = lane_x + (base + 8 * HX * j)
                term = (STEP * jnp.abs(sx)) * ref[2 * iy + j]
                for a in range(5):
                    term = term if a == 0 else sx * term
                    edge[a] = term if edge[a] is None else edge[a] + term
            for (a, b), n in full_at.items():
                edge_acc[side, n] = edge_acc[side, n] + power[b] * edge[a]
        return carry

    lax.fori_loop(0, 8, over_y, 0)
    sz = local_z(iz)
    zs = [QUAD * jnp.ones((), F32), QUAD * sz, QUAD * sz * sz, QUAD * sz * sz * sz]
    sign = jnp.where(block >= 2, 1.0, -1.0).astype(F32)
    zy = [sign * z for z in zs]

    def all_sets(full, odd):
        out = [added_up(zs[c] * full(a, b) for a, b, c in monos) for monos in PLAIN]
        out += [added_up(zs[c] * odd(a + 1, b) for a, b, c in monos) for monos in MOMENTS]
        out += [added_up(zy[c] * full(a, b + 1) for a, b, c in monos) for monos in MOMENTS]
        return out

    for i, v in enumerate(all_sets(lambda a, b: acc[full_at[a, b]], lambda a, b: acc[odd_at[a, b]])):
        part_ref[slot_of(i)] = v
    part_ref[6] = jnp.zeros((8, 128), F32)
    for side, where in ((0, row_up), (1, row_down)):
        lines = {p: jnp.sum(edge_acc[side, n], axis=0, keepdims=True) for p, n in full_at.items()}
        factor = -1.0 if side else 1.0
        for i, v in enumerate(
            all_sets(lambda a, b: lines[a, b], lambda a, b: factor * lines[a, b])
        ):
            slot, r = where(i)
            part_ref[slot, r : r + 1, :] = v


def diffuse(own_source, far_source, row):
    own, far = own_source, far_source
    for _ in range(SWEEPS):
        own_down, far_down = pltpu.roll(own, 1, 0), pltpu.roll(far, 1, 0)
        own_up, far_up = pltpu.roll(own, 7, 0), pltpu.roll(far, 7, 0)
        new_own = (
            jnp.where(row == 0, far_down, own_down)
            + jnp.where(row == 7, far_up, own_up)
            + pltpu.roll(own, 1, 1)
            + pltpu.roll(own, 127, 1)
        )
        new_far = (
            jnp.where(row == 0, own_down, far_down)
            + jnp.where(row == 7, own_up, far_up)
            + pltpu.roll(far, 1, 1)
            + pltpu.roll(far, 127, 1)
        )
        own = (own_source + new_own) * 0.2
        far = (far_source + new_far) * 0.2
    return own


def heat_flux(m):
    inv = 1.0 / m[0]
    u = [m[1] * inv, m[2] * inv, m[3] * inv]
    p_zz = m[4] - m[5] - m[6]
    p = [[m[5], m[7], m[8]], [m[7], m[6], m[9]], [m[8], m[9], p_zz]]
    sq = u[0] * u[0] + u[1] * u[1] + u[2] * u[2]
    mass_sq = 2.0 * m[0] * sq
    return [
        0.5
        * (
            m[10 + i]
            - 2.0 * (u[0] * p[i][0] + u[1] * p[i][1] + u[2] * p[i][2])
            + u[i] * (mass_sq - m[4])
        )
        for i in range(3)
    ]


def cell_state(state, moments, rate_class, wall):
    density = state[0]
    inv = 1.0 / density
    u = [state[i] * inv for i in (1, 2, 3)]
    temperature = (2.0 * state[4] * inv - (u[0] * u[0] + u[1] * u[1] + u[2] * u[2])) * (1.0 / 3.0)
    heat = heat_flux(moments)
    frequency = 0.5 * jnp.exp2(rate_class.astype(F32))
    power = jnp.exp((1.0 - 0.81) * jnp.log(temperature))
    keep = jnp.exp(-STEP * frequency * density * power)
    inv_t = 1.0 / temperature
    rate = 1.0 - keep
    skew = ((1.0 - 2.0 / 3.0) / 5.0) * inv * inv_t * inv_t
    amplitude = rate * density * inv_t * lax.rsqrt(temperature)
    solid = wall > 0
    keep = jnp.where(solid, 0.0, keep)
    amplitude = jnp.where(solid, density, amplitude)
    inv_t = jnp.where(solid, 1.0, inv_t)
    u = [jnp.where(solid, 0.0, c) for c in u]
    heat = [jnp.where(solid, 0.0, skew * h) for h in heat]
    return keep, amplitude, inv_t, u, heat


def apply_added(sy, sz, cell):
    _, amplitude, inv_t, u, heat = cell
    dy, dz = sy - u[1], sz - u[2]
    square = (dy * dy + dz * dz) * inv_t
    return amplitude * jnp.exp(-0.5 * square), square - 5.0, dy * heat[1] + dz * heat[2]


def profile_x(cell, profile):
    _, _, inv_t, u, heat = cell
    for ix in range(VX):
        dx = SPEED_X[ix] - u[0]
        square = dx * dx * inv_t
        profile[0, ix] = jnp.exp(-0.5 * square)
        profile[1, ix] = square
        profile[2, ix] = dx * heat[0]


def line_sums(speeds, u, inv_t, top):
    out = [None] * (top + 1)
    for s in speeds:
        d = s - u
        e = jnp.exp(-0.5 * (d * d * inv_t))
        for a in range(top + 1):
            term = e if a == 0 else (s**a) * e
            out[a] = term if out[a] is None else out[a] + term
    return out


def central(raw, u, top):
    table = [raw]
    for _ in range(3):
        last = table[-1]
        table.append([last[a + 1] - u * last[a] for a in range(len(last) - 1)])
    return [line[: top + 1] for line in table]


def added_moments(cell):
    _, amplitude, inv_t, u, heat = cell
    scale = amplitude * QUAD
    half = VX // 2
    x_up = central(line_sums(SPEED_X[half:], u[0], inv_t, 7), u[0], 4)
    x_dn = central(line_sums(SPEED_X[:half], u[0], inv_t, 7), u[0], 4)
    y_up = central(line_sums(SPEED_Y[half:], u[1], inv_t, 7), u[1], 4)
    y_dn = central(line_sums(SPEED_Y[:half], u[1], inv_t, 7), u[1], 4)
    z_all = central([scale * z for z in line_sums(SPEED_Z, u[2], inv_t, 6)], u[2], 3)
    x_all = [[p + q for p, q in zip(r, s)] for r, s in zip(x_up, x_dn)]
    y_all = [[p + q for p, q in zip(r, s)] for r, s in zip(y_up, y_dn)]
    gx, gy, gz = heat
    hx, hy, hz = gx * inv_t, gy * inv_t, gz * inv_t

    def whole(xs, ys):
        plane = {}

        def at(a, b):
            if (a, b) not in plane:
                x = [xs[i][a] for i in range(4)]
                y = [ys[i][b] for i in range(4)]
                x0y0 = x[0] * y[0]
                x1y0, x0y1 = x[1] * y[0], x[0] * y[1]
                x2y0, x0y2 = x[2] * y[0], x[0] * y[2]
                p0 = (
                    x0y0
                    + hx * (x[3] * y[0] + x[1] * y[2])
                    + hy * (x[2] * y[1] + x[0] * y[3])
                    - 5.0 * (gx * x1y0 + gy * x0y1)
                )
                p1 = hz * (x2y0 + x0y2) - 5.0 * gz * x0y0
                p2 = hx * x1y0 + hy * x0y1
                p3 = hz * x0y0
                plane[a, b] = (p0, p1, p2, p3)
            return plane[a, b]

        out = []
        for monos in MOMENTS:
            total = None
            for a, b, c in monos:
                p = at(a, b)
                term = (
                    p[0] * z_all[0][c] + p[1] * z_all[1][c] + p[2] * z_all[2][c] + p[3] * z_all[3][c]
                )
                total = term if total is None else total + term
            out.append(total)
        return out

    def weighted(table, factor):
        return [[factor * v for v in line[1:5]] for line in table]

    return (
        whole(x_all, y_all),
        whole(weighted(x_up, STEP), y_all),
        whole(weighted(x_dn, -STEP), y_all),
        whole(x_all, weighted(y_up, STEP)),
        whole(x_all, weighted(y_dn, -STEP)),
    )


def first_kernel(
    q_ref, prev_ref, next_ref, before_ref, after_ref, class_ref, wall_ref, t_ref,
    f_ref, m_ref, add_ref, to_next_ref, to_prev_ref, profile,
):
    block, iz = place()
    row = rows_of()
    shift = jnp.where(block >= 2, 1, 127)

    def line(ref, first, at):
        return ref[at[0] - first, at[1] : at[1] + 1, :]

    def whole_set(i):
        above, below = line(prev_ref, 0, row_up(i)), line(next_ref, 6, row_down(i))
        return q_ref[slot_of(i)] + jnp.where(row == 0, above, jnp.where(row == 7, below, 0.0))

    sets = [whole_set(i) for i in range(SETS)]
    scale = [1.0, 1.0, 1.0, 1.0, 0.5]
    state = []
    for k in range(5):
        far = jnp.where(row < 4, next_ref[1 + k], prev_ref[FIRST_SET + k])
        up, down = line(q_ref, 0, row_up(k)), line(q_ref, 0, row_down(k))
        far = far + jnp.where(row == 0, up, jnp.where(row == 7, down, 0.0))
        state.append(diffuse(scale[k] * sets[k], scale[k] * far, row))
    cell = cell_state(state, sets[:13], class_ref[...], wall_ref[...])
    keep = cell[0]
    profile_x(cell, profile)
    sz = local_z(iz)

    def over_y(iy, carry):
        sy = local_y(block, iy)
        courant_y = STEP * jnp.abs(sy)
        base, square, flux = apply_added(sy, sz, cell)
        for ix in range(VX):
            k = ix % 16
            edge = (before_ref if SPEED_X[ix] > 0 else after_ref)[
                2 * iy + k // 8, k % 8 : k % 8 + 1, :
            ]
            value = moved(t_ref[iy * 32 + ix], ix, courant_y, shift, row, edge, edge)
            added = (base * profile[0, ix]) * (
                1.0 + (flux + profile[2, ix]) * (square + profile[1, ix])
            )
            value = keep * value + added
            f_ref[iy * 32 + ix] = value
            if SPEED_X[ix] > 0:
                to_next_ref[6 + 2 * iy + k // 8, k % 8 : k % 8 + 1, :] = value[7:8, :]
            else:
                to_prev_ref[6 + 2 * iy + k // 8, k % 8 : k % 8 + 1, :] = value[0:1, :]
        return carry

    lax.fori_loop(0, 8, over_y, 0)

    g_all, g_xu, g_xd, g_yu, g_yd = added_moments(cell)
    part = 0.5 * STEP * keep
    for k, monos in enumerate(MOMENTS):
        sx_k, ax_k = sets[AT[key_of(times(monos, 0))]], sets[ABS_X + k]
        sy_k, ay_k = sets[AT[key_of(times(monos, 1))]], sets[ABS_Y + k]
        x_up = part * (ax_k + sx_k) + g_xu[k]
        x_dn = part * (ax_k - sx_k) + g_xd[k]
        y_up = part * (ay_k + sy_k) + g_yu[k]
        y_dn = part * (ay_k - sy_k) + g_yd[k]
        from_up, from_dn = pltpu.roll(x_up, 1, 0), pltpu.roll(x_dn, 7, 0)
        total = (
            (keep * sets[k] + g_all[k] - x_up - x_dn - y_up - y_dn)
            + jnp.where(row == 0, 0.0, from_up)
            + jnp.where(row == 7, 0.0, from_dn)
            + pltpu.roll(y_up, 1, 1)
            + pltpu.roll(y_dn, 127, 1)
        )
        m_ref[k] = total
        if k < 5:
            add_ref[k] = jnp.where(row == 0, from_up, jnp.where(row == 7, from_dn, 0.0))
            to_next_ref[k] = jnp.where(row == 0, from_up, total)
            to_prev_ref[k] = jnp.where(row == 7, from_dn, total)
        else:
            to_next_ref[5, k - 5 : k - 4, :] = x_up[7:8, :]
            to_prev_ref[5, k - 5 : k - 4, :] = x_dn[0:1, :]


def second_kernel(
    m_ref, add_ref, prev_ref, next_ref, class_ref, wall_ref, f_ref,
    out_ref, state_ref, profile,
):
    block, iz = place()
    row = rows_of()
    shift = jnp.where(block >= 2, 1, 127)
    moments = []
    for k in range(13):
        if k < 5:
            before, after = prev_ref[k], next_ref[k]
        else:
            before, after = prev_ref[5, k - 5 : k - 4, :], next_ref[5, k - 5 : k - 4, :]
        moments.append(
            m_ref[k] + jnp.where(row == 0, before, jnp.where(row == 7, after, 0.0))
        )
    scale = [1.0, 1.0, 1.0, 1.0, 0.5]
    state = []
    for k in range(5):
        far = jnp.where(row < 4, next_ref[k], prev_ref[k]) + add_ref[k]
        state.append(diffuse(scale[k] * moments[k], scale[k] * far, row))
        state_ref[k] = state[k]
    cell = cell_state(state, moments, class_ref[...], wall_ref[...])
    keep = cell[0]
    profile_x(cell, profile)
    sz = local_z(iz)

    def over_y(iy, carry):
        sy = local_y(block, iy)
        courant_y = STEP * jnp.abs(sy)
        base, square, flux = apply_added(sy, sz, cell)
        for ix in range(VX):
            k = ix % 16
            edge = (prev_ref if SPEED_X[ix] > 0 else next_ref)[
                6 + 2 * iy + k // 8, k % 8 : k % 8 + 1, :
            ]
            value = moved(f_ref[iy * 32 + ix], ix, courant_y, shift, row, edge, edge)
            added = (base * profile[0, ix]) * (
                1.0 + (flux + profile[2, ix]) * (square + profile[1, ix])
            )
            out_ref[iy * 32 + ix] = keep * value + added
        return carry

    lax.fori_loop(0, 8, over_y, 0)


def kernel_call(body, outs, scratch, limit=32):
    return pl.pallas_call(
        body,
        out_shape=[jax.ShapeDtypeStruct(s, F32) for s in outs],
        scratch_shapes=[pltpu.VMEM(s, F32) for s in scratch],
        compiler_params=pltpu.CompilerParams(vmem_limit_bytes=limit * 1024 * 1024),
    )


def to_both(up_value, down_value):
    size = lax.axis_size("space")
    up = [(i, (i + 1) % size) for i in range(size)]
    down = [(j, i) for i, j in up]
    return lax.ppermute(up_value, "space", up), lax.ppermute(down_value, "space", down)


NEAR = [
    [(4 * b + k) * 4 + y for k in order for y in (2, 3, 0, 1)]
    for b, order in enumerate(((1, 0, 2, 3), (2, 3, 1, 0), (1, 0, 2, 3), (1, 0, 2, 3)))
]
FAR = [[NEAR[b][p] for b in (2, 3, 0, 1)] for p in range(16)]


def all_sum(part, edges):
    piece = part.reshape(16, SLOTS // 2, 128)
    piece = lax.all_to_all(piece, "vel", 0, 0, tiled=True, axis_index_groups=NEAR)
    piece, edges = lax.optimization_barrier((piece, edges))
    beside = to_both(*edges)
    mine = jnp.sum(piece, 0)
    piece = jnp.broadcast_to(mine[None], (4,) + mine.shape)
    piece = lax.all_to_all(piece, "vel", 0, 0, tiled=True, axis_index_groups=FAR)
    piece, beside = lax.optimization_barrier((piece, beside))
    mine = jnp.sum(piece, 0)
    piece = jnp.broadcast_to(mine[None], (16,) + mine.shape)
    piece = lax.all_to_all(piece, "vel", 0, 0, tiled=True, axis_index_groups=NEAR)
    return piece.reshape(SLOTS, 8, 128), beside


def per_device(distribution, rate_class, wall):
    block, edges, small = (256, 8, 128), (16, 8, 128), (22, 8, 128)
    part, to_next, to_prev = kernel_call(
        moments_kernel,
        [(SLOTS, 8, 128), edges, edges],
        [(25, 8, 128), (2, 15, 8, 128)],
    )(distribution)
    sums, (before, after) = all_sum(part, (to_next, to_prev))
    prev, following = to_both(sums[:12], sums[6:18])
    field, moments, extra, to_next, to_prev = kernel_call(
        first_kernel, [block, (13, 8, 128), (5, 8, 128), small, small], [(3, 32, 8, 128)]
    )(sums, prev, following, before, after, rate_class, wall, distribution)
    prev, following = to_both(to_next, to_prev)
    field, state = kernel_call(
        second_kernel,
        [block, (5, 8, 128)],
        [(3, 32, 8, 128)],
    )(moments, extra, prev, following, rate_class, wall, field)
    return field, state


def solution(mesh):
    return jax.shard_map(
        per_device,
        mesh=mesh,
        in_specs=(P("vel", "space", None), P("space", None), P("space", None)),
        out_specs=(P("vel", "space", None), P(None, "space", None)),
        check_vma=False,
    )
```

```python
import jax
import jax.numpy as jnp
import numpy as np
from jax import lax
from jax.experimental import pallas as pl
from jax.experimental.pallas import tpu as pltpu
from jax.sharding import PartitionSpec as P

VX, VY, VZ = 32, 32, 16
SWEEPS = 4
EDGE = 5.0
STEP = 0.1
HX = 2.0 * EDGE / VX
HY = 2.0 * EDGE / VY
HZ = 2.0 * EDGE / VZ
QUAD = float(HX * HY * HZ / (2.0 * np.pi) ** 1.5)
SPEED_X = [-EDGE + (i + 0.5) * HX for i in range(VX)]
SPEED_Y = [-EDGE + (i + 0.5) * HY for i in range(VY)]
SPEED_Z = [-EDGE + (i + 0.5) * HZ for i in range(VZ)]
F32 = jnp.float32

MOMENTS = [
    ((0, 0, 0),),
    ((1, 0, 0),),
    ((0, 1, 0),),
    ((0, 0, 1),),
    ((2, 0, 0), (0, 2, 0), (0, 0, 2)),
    ((2, 0, 0),),
    ((0, 2, 0),),
    ((1, 1, 0),),
    ((1, 0, 1),),
    ((0, 1, 1),),
    ((3, 0, 0), (1, 2, 0), (1, 0, 2)),
    ((2, 1, 0), (0, 3, 0), (0, 1, 2)),
    ((2, 0, 1), (0, 2, 1), (0, 0, 3)),
]


def times(moment, axis):
    return tuple(tuple(p + (d == axis) for d, p in enumerate(m)) for m in moment)


def key_of(moment):
    return tuple(sorted(moment))


PLAIN = []
for _m in MOMENTS + [times(m, 0) for m in MOMENTS] + [times(m, 1) for m in MOMENTS]:
    if key_of(_m) not in PLAIN:
        PLAIN.append(key_of(_m))
AT = {k: i for i, k in enumerate(PLAIN)}
ABS_X = len(PLAIN)
ABS_Y = ABS_X + 13
SETS = ABS_Y + 13
SLOTS = 64
FIRST_SET = 7


def slot_of(i):
    return FIRST_SET + i if i < 5 else FIRST_SET + 6 + i


def row_up(i):
    return (i // 8, i % 8) if i < 48 else (6, i - 48)


def row_down(i):
    return (12 + i // 8, i % 8) if i < 48 else (6, i - 45)


def rows_of():
    return lax.broadcasted_iota(jnp.int32, (8, 128), 0)


def added_up(terms):
    total = None
    for t in terms:
        total = t if total is None else total + t
    return total


def place():
    vel = lax.axis_index("vel")
    return lax.rem(vel, 4), lax.div(vel, 4)


def local_y(block, iy):
    return -EDGE + ((block * 8 + iy).astype(F32) + 0.5) * HY


def local_z(iz):
    return -EDGE + (iz.astype(F32) + 0.5) * HZ


def moved(value, ix, courant_y, shift, row, before, after):
    courant_x = STEP * abs(SPEED_X[ix])
    if SPEED_X[ix] > 0:
        beside = jnp.where(row == 0, before, pltpu.roll(value, 1, 0))
    else:
        beside = jnp.where(row == 7, after, pltpu.roll(value, 7, 0))
    along = pltpu.roll(value, shift, 1)
    return ((1.0 - courant_x) - courant_y) * value + courant_x * beside + courant_y * along


def powers():
    full = [(a, b) for a in range(5) for b in range(5 - a)]
    odd = [(a, b) for a in range(1, 5) for b in range(5 - a)]
    return {p: i for i, p in enumerate(full)}, {p: 15 + i for i, p in enumerate(odd)}


def moments_kernel(
    f_ref, part_ref, to_next_ref, to_prev_ref, inner_last_ref, inner_first_ref, acc, edge_acc
):
    block, iz = place()
    row = rows_of()
    shift = jnp.where(block >= 2, 1, 127)
    full_at, odd_at = powers()
    acc[...] = jnp.zeros_like(acc)
    edge_acc[...] = jnp.zeros_like(edge_acc)
    lane_x = (row.astype(F32) + 0.5) * HX

    def over_y(iy, carry):
        sy = local_y(block, iy)
        courant_y = STEP * jnp.abs(sy)
        sums = [[None] * 5, [None] * 5]
        for ix in range(VX):
            half = 1 if SPEED_X[ix] > 0 else 0
            k = ix % 16
            raw = f_ref[iy * 32 + ix]
            at = (2 * iy + k // 8, slice(k % 8, k % 8 + 1), slice(None))
            if half:
                to_next_ref[at] = raw[7:8, :]
                inner_last_ref[at] = raw[6:7, :]
            else:
                to_prev_ref[at] = raw[0:1, :]
                inner_first_ref[at] = raw[1:2, :]
            value = moved(raw, ix, courant_y, shift, row, 0.0, 0.0)
            for a in range(5):
                term = value if a == 0 else (SPEED_X[ix] ** a) * value
                sums[half][a] = term if sums[half][a] is None else sums[half][a] + term
        power = [1.0, sy, sy * sy, sy * sy * sy, sy * sy * sy * sy]
        full = [sums[1][a] + sums[0][a] for a in range(5)]
        odd = [sums[1][a] - sums[0][a] for a in range(5)]
        for (a, b), n in full_at.items():
            acc[n] = acc[n] + power[b] * full[a]
        for (a, b), n in odd_at.items():
            acc[n] = acc[n] + power[b] * odd[a]
        for side, ref, base in ((0, to_next_ref, 0.0), (1, to_prev_ref, -EDGE)):
            edge = [None] * 5
            for j in range(2):
                sx = lane_x + (base + 8 * HX * j)
                term = (STEP * jnp.abs(sx)) * ref[2 * iy + j]
                for a in range(5):
                    term = term if a == 0 else sx * term
                    edge[a] = term if edge[a] is None else edge[a] + term
            for (a, b), n in full_at.items():
                edge_acc[side, n] = edge_acc[side, n] + power[b] * edge[a]
        return carry

    lax.fori_loop(0, 8, over_y, 0)
    sz = local_z(iz)
    zs = [QUAD * jnp.ones((), F32), QUAD * sz, QUAD * sz * sz, QUAD * sz * sz * sz]
    sign = jnp.where(block >= 2, 1.0, -1.0).astype(F32)
    zy = [sign * z for z in zs]

    def all_sets(full, odd):
        out = [added_up(zs[c] * full(a, b) for a, b, c in monos) for monos in PLAIN]
        out += [added_up(zs[c] * odd(a + 1, b) for a, b, c in monos) for monos in MOMENTS]
        out += [added_up(zy[c] * full(a, b + 1) for a, b, c in monos) for monos in MOMENTS]
        return out

    for i, v in enumerate(all_sets(lambda a, b: acc[full_at[a, b]], lambda a, b: acc[odd_at[a, b]])):
        part_ref[slot_of(i)] = v
    part_ref[6] = jnp.zeros((8, 128), F32)
    for side, where in ((0, row_up), (1, row_down)):
        lines = {p: jnp.sum(edge_acc[side, n], axis=0, keepdims=True) for p, n in full_at.items()}
        factor = -1.0 if side else 1.0
        for i, v in enumerate(
            all_sets(lambda a, b: lines[a, b], lambda a, b: factor * lines[a, b])
        ):
            slot, r = where(i)
            part_ref[slot, r : r + 1, :] = v


def diffuse(own_source, far_source, row):
    own, far = own_source, far_source
    for _ in range(SWEEPS):
        own_down, far_down = pltpu.roll(own, 1, 0), pltpu.roll(far, 1, 0)
        own_up, far_up = pltpu.roll(own, 7, 0), pltpu.roll(far, 7, 0)
        new_own = (
            jnp.where(row == 0, far_down, own_down)
            + jnp.where(row == 7, far_up, own_up)
            + pltpu.roll(own, 1, 1)
            + pltpu.roll(own, 127, 1)
        )
        new_far = (
            jnp.where(row == 0, own_down, far_down)
            + jnp.where(row == 7, own_up, far_up)
            + pltpu.roll(far, 1, 1)
            + pltpu.roll(far, 127, 1)
        )
        own = (own_source + new_own) * 0.2
        far = (far_source + new_far) * 0.2
    return own


def heat_flux(m):
    inv = 1.0 / m[0]
    u = [m[1] * inv, m[2] * inv, m[3] * inv]
    p_zz = m[4] - m[5] - m[6]
    p = [[m[5], m[7], m[8]], [m[7], m[6], m[9]], [m[8], m[9], p_zz]]
    sq = u[0] * u[0] + u[1] * u[1] + u[2] * u[2]
    mass_sq = 2.0 * m[0] * sq
    return [
        0.5
        * (
            m[10 + i]
            - 2.0 * (u[0] * p[i][0] + u[1] * p[i][1] + u[2] * p[i][2])
            + u[i] * (mass_sq - m[4])
        )
        for i in range(3)
    ]


def cell_state(state, moments, rate_class, wall):
    density = state[0]
    inv = 1.0 / density
    u = [state[i] * inv for i in (1, 2, 3)]
    temperature = (2.0 * state[4] * inv - (u[0] * u[0] + u[1] * u[1] + u[2] * u[2])) * (1.0 / 3.0)
    heat = heat_flux(moments)
    frequency = 0.5 * jnp.exp2(rate_class.astype(F32))
    power = jnp.exp((1.0 - 0.81) * jnp.log(temperature))
    keep = jnp.exp(-STEP * frequency * density * power)
    inv_t = 1.0 / temperature
    rate = 1.0 - keep
    skew = ((1.0 - 2.0 / 3.0) / 5.0) * inv * inv_t * inv_t
    amplitude = rate * density * inv_t * lax.rsqrt(temperature)
    solid = wall > 0
    keep = jnp.where(solid, 0.0, keep)
    amplitude = jnp.where(solid, density, amplitude)
    inv_t = jnp.where(solid, 1.0, inv_t)
    u = [jnp.where(solid, 0.0, c) for c in u]
    heat = [jnp.where(solid, 0.0, skew * h) for h in heat]
    return keep, amplitude, inv_t, u, heat


def apply_added(sy, sz, cell):
    _, amplitude, inv_t, u, heat = cell
    dy, dz = sy - u[1], sz - u[2]
    square = (dy * dy + dz * dz) * inv_t
    return amplitude * jnp.exp(-0.5 * square), square - 5.0, dy * heat[1] + dz * heat[2]


def profile_x(cell, profile):
    _, _, inv_t, u, heat = cell
    for ix in range(VX):
        dx = SPEED_X[ix] - u[0]
        square = dx * dx * inv_t
        profile[0, ix] = jnp.exp(-0.5 * square)
        profile[1, ix] = square
        profile[2, ix] = dx * heat[0]


def line_sums(speeds, u, inv_t, top):
    out = [None] * (top + 1)
    for s in speeds:
        d = s - u
        e = jnp.exp(-0.5 * (d * d * inv_t))
        for a in range(top + 1):
            term = e if a == 0 else (s**a) * e
            out[a] = term if out[a] is None else out[a] + term
    return out


def central(raw, u, top):
    table = [raw]
    for _ in range(3):
        last = table[-1]
        table.append([last[a + 1] - u * last[a] for a in range(len(last) - 1)])
    return [line[: top + 1] for line in table]


def added_moments(cell):
    _, amplitude, inv_t, u, heat = cell
    scale = amplitude * QUAD
    half = VX // 2
    x_up = central(line_sums(SPEED_X[half:], u[0], inv_t, 7), u[0], 4)
    x_dn = central(line_sums(SPEED_X[:half], u[0], inv_t, 7), u[0], 4)
    y_up = central(line_sums(SPEED_Y[half:], u[1], inv_t, 7), u[1], 4)
    y_dn = central(line_sums(SPEED_Y[:half], u[1], inv_t, 7), u[1], 4)
    z_all = central([scale * z for z in line_sums(SPEED_Z, u[2], inv_t, 6)], u[2], 3)
    x_all = [[p + q for p, q in zip(r, s)] for r, s in zip(x_up, x_dn)]
    y_all = [[p + q for p, q in zip(r, s)] for r, s in zip(y_up, y_dn)]
    gx, gy, gz = heat
    hx, hy, hz = gx * inv_t, gy * inv_t, gz * inv_t

    def whole(xs, ys):
        plane = {}

        def at(a, b):
            if (a, b) not in plane:
                x = [xs[i][a] for i in range(4)]
                y = [ys[i][b] for i in range(4)]
                x0y0 = x[0] * y[0]
                x1y0, x0y1 = x[1] * y[0], x[0] * y[1]
                x2y0, x0y2 = x[2] * y[0], x[0] * y[2]
                p0 = (
                    x0y0
                    + hx * (x[3] * y[0] + x[1] * y[2])
                    + hy * (x[2] * y[1] + x[0] * y[3])
                    - 5.0 * (gx * x1y0 + gy * x0y1)
                )
                p1 = hz * (x2y0 + x0y2) - 5.0 * gz * x0y0
                p2 = hx * x1y0 + hy * x0y1
                p3 = hz * x0y0
                plane[a, b] = (p0, p1, p2, p3)
            return plane[a, b]

        out = []
        for monos in MOMENTS:
            total = None
            for a, b, c in monos:
                p = at(a, b)
                term = (
                    p[0] * z_all[0][c] + p[1] * z_all[1][c] + p[2] * z_all[2][c] + p[3] * z_all[3][c]
                )
                total = term if total is None else total + term
            out.append(total)
        return out

    def weighted(table, factor):
        return [[factor * v for v in line[1:5]] for line in table]

    return (
        whole(x_all, y_all),
        whole(weighted(x_up, STEP), y_all),
        whole(weighted(x_dn, -STEP), y_all),
        whole(x_all, weighted(y_up, STEP)),
        whole(x_all, weighted(y_dn, -STEP)),
    )


def flat(cell):
    keep, amplitude, inv_t, u, heat = cell
    return [keep, amplitude, inv_t, *u, *heat]


def cell_of(v):
    return v[0], v[1], v[2], v[3:6], v[6:9]


def keep_out(cell, ref):
    for i, v in enumerate(flat(cell)):
        ref[i] = v


def first_kernel(
    q_ref, prev_ref, next_ref, class_ref, wall_ref, last_ref, first_ref, inner_last_ref, inner_first_ref,
    m_ref, add_ref, to_next_ref, to_prev_ref, cell_ref,
):
    block, iz = place()
    row = rows_of()
    shift = jnp.where(block >= 2, 1, 127)

    def line(ref, first, at):
        return ref[at[0] - first, at[1] : at[1] + 1, :]

    def whole_set(i):
        above, below = line(prev_ref, 0, row_up(i)), line(next_ref, 6, row_down(i))
        return q_ref[slot_of(i)] + jnp.where(row == 0, above, jnp.where(row == 7, below, 0.0))

    sets = [whole_set(i) for i in range(SETS)]
    scale = [1.0, 1.0, 1.0, 1.0, 0.5]
    state = []
    for k in range(5):
        far = jnp.where(row < 4, next_ref[1 + k], prev_ref[FIRST_SET + k])
        up, down = line(q_ref, 0, row_up(k)), line(q_ref, 0, row_down(k))
        far = far + jnp.where(row == 0, up, jnp.where(row == 7, down, 0.0))
        state.append(diffuse(scale[k] * sets[k], scale[k] * far, row))
    cell = cell_state(state, sets[:13], class_ref[...], wall_ref[...])
    keep = cell[0]
    keep_out(cell, cell_ref)
    sz = local_z(iz)

    for r, base_x, outer, inner, out in (
        (7, 0.0, last_ref, inner_last_ref, to_next_ref),
        (0, -EDGE, first_ref, inner_first_ref, to_prev_ref),
    ):
        line_cell = cell_of([jnp.broadcast_to(v[r : r + 1, :], (8, 128)) for v in flat(cell)])
        parts = []
        for j in range(2):
            sx = (row.astype(F32) + 0.5) * HX + (base_x + 8 * HX * j)
            dx = sx - line_cell[3][0]
            square = dx * dx * line_cell[2]
            parts.append(
                (STEP * jnp.abs(sx), jnp.exp(-0.5 * square), square, dx * line_cell[4][0])
            )

        def edge_y(iy, carry, line_cell=line_cell, parts=parts, outer=outer, inner=inner, out=out):
            sy = local_y(block, iy)
            courant_y = STEP * jnp.abs(sy)
            base, square, flux = apply_added(sy, sz, line_cell)
            for j, (courant_x, bell, square_x, flux_x) in enumerate(parts):
                value = outer[2 * iy + j]
                value = (
                    ((1.0 - courant_x) - courant_y) * value
                    + courant_x * inner[2 * iy + j]
                    + courant_y * pltpu.roll(value, shift, 1)
                )
                added = (base * bell) * (1.0 + (flux + flux_x) * (square + square_x))
                out[6 + 2 * iy + j] = line_cell[0] * value + added
            return carry

        lax.fori_loop(0, 8, edge_y, 0, unroll=True)

    g_all, g_xu, g_xd, g_yu, g_yd = added_moments(cell)
    part = 0.5 * STEP * keep
    for k, monos in enumerate(MOMENTS):
        sx_k, ax_k = sets[AT[key_of(times(monos, 0))]], sets[ABS_X + k]
        sy_k, ay_k = sets[AT[key_of(times(monos, 1))]], sets[ABS_Y + k]
        x_up = part * (ax_k + sx_k) + g_xu[k]
        x_dn = part * (ax_k - sx_k) + g_xd[k]
        y_up = part * (ay_k + sy_k) + g_yu[k]
        y_dn = part * (ay_k - sy_k) + g_yd[k]
        from_up, from_dn = pltpu.roll(x_up, 1, 0), pltpu.roll(x_dn, 7, 0)
        total = (
            (keep * sets[k] + g_all[k] - x_up - x_dn - y_up - y_dn)
            + jnp.where(row == 0, 0.0, from_up)
            + jnp.where(row == 7, 0.0, from_dn)
            + pltpu.roll(y_up, 1, 1)
            + pltpu.roll(y_dn, 127, 1)
        )
        m_ref[k] = total
        if k < 5:
            add_ref[k] = jnp.where(row == 0, from_up, jnp.where(row == 7, from_dn, 0.0))
            to_next_ref[k] = jnp.where(row == 0, from_up, total)
            to_prev_ref[k] = jnp.where(row == 7, from_dn, total)
        else:
            to_next_ref[5, k - 5 : k - 4, :] = x_up[7:8, :]
            to_prev_ref[5, k - 5 : k - 4, :] = x_dn[0:1, :]


def field_kernel(cell_ref, f_ref, before_ref, after_ref, t_ref, profile):
    block, iz = place()
    row = rows_of()
    shift = jnp.where(block >= 2, 1, 127)
    cell = cell_of([cell_ref[i] for i in range(9)])
    keep = cell[0]
    profile_x(cell, profile)
    sz = local_z(iz)

    def over_y(iy, carry):
        sy = local_y(block, iy)
        courant_y = STEP * jnp.abs(sy)
        base, square, flux = apply_added(sy, sz, cell)
        for ix in range(VX):
            k = ix % 16
            edge = (before_ref if SPEED_X[ix] > 0 else after_ref)[
                2 * iy + k // 8, k % 8 : k % 8 + 1, :
            ]
            value = moved(f_ref[iy * 32 + ix], ix, courant_y, shift, row, edge, edge)
            added = (base * profile[0, ix]) * (
                1.0 + (flux + profile[2, ix]) * (square + profile[1, ix])
            )
            value = keep * value + added
            t_ref[iy * 32 + ix] = moved(value, ix, courant_y, shift, row, 0.0, 0.0)
        return carry

    lax.fori_loop(0, 8, over_y, 0)


def second_kernel(
    m_ref, add_ref, prev_ref, next_ref, class_ref, wall_ref, t_ref,
    out_ref, state_ref, profile,
):
    block, iz = place()
    row = rows_of()
    moments = []
    for k in range(13):
        if k < 5:
            before, after = prev_ref[k], next_ref[k]
        else:
            before, after = prev_ref[5, k - 5 : k - 4, :], next_ref[5, k - 5 : k - 4, :]
        moments.append(
            m_ref[k] + jnp.where(row == 0, before, jnp.where(row == 7, after, 0.0))
        )
    scale = [1.0, 1.0, 1.0, 1.0, 0.5]
    state = []
    for k in range(5):
        far = jnp.where(row < 4, next_ref[k], prev_ref[k]) + add_ref[k]
        state.append(diffuse(scale[k] * moments[k], scale[k] * far, row))
        state_ref[k] = state[k]
    cell = cell_state(state, moments, class_ref[...], wall_ref[...])
    keep = cell[0]
    profile_x(cell, profile)
    sz = local_z(iz)

    def over_y(iy, carry):
        sy = local_y(block, iy)
        base, square, flux = apply_added(sy, sz, cell)
        for ix in range(VX):
            k = ix % 16
            edge = (prev_ref if SPEED_X[ix] > 0 else next_ref)[
                6 + 2 * iy + k // 8, k % 8 : k % 8 + 1, :
            ]
            courant_x = STEP * abs(SPEED_X[ix])
            here = row == (0 if SPEED_X[ix] > 0 else 7)
            value = t_ref[iy * 32 + ix] + jnp.where(here, courant_x * edge, 0.0)
            added = (base * profile[0, ix]) * (
                1.0 + (flux + profile[2, ix]) * (square + profile[1, ix])
            )
            out_ref[iy * 32 + ix] = keep * value + added
        return carry

    lax.fori_loop(0, 8, over_y, 0)


def kernel_call(body, outs, scratch, limit=32):
    return pl.pallas_call(
        body,
        out_shape=[jax.ShapeDtypeStruct(s, F32) for s in outs],
        scratch_shapes=[pltpu.VMEM(s, F32) for s in scratch],
        compiler_params=pltpu.CompilerParams(vmem_limit_bytes=limit * 1024 * 1024),
    )


def to_both(up_value, down_value):
    size = lax.axis_size("space")
    up = [(i, (i + 1) % size) for i in range(size)]
    down = [(j, i) for i, j in up]
    return lax.ppermute(up_value, "space", up), lax.ppermute(down_value, "space", down)


NEAR = [
    [(4 * b + k) * 4 + y for k in order for y in (2, 3, 0, 1)]
    for b, order in enumerate(((1, 0, 2, 3), (2, 3, 1, 0), (1, 0, 2, 3), (1, 0, 2, 3)))
]
FAR = [[NEAR[b][p] for b in (2, 3, 0, 1)] for p in range(16)]


def all_sum(part):
    piece = part.reshape(16, SLOTS // 2, 128)
    piece = lax.all_to_all(piece, "vel", 0, 0, tiled=True, axis_index_groups=NEAR)
    mine = jnp.sum(piece, 0)
    piece = jnp.broadcast_to(mine[None], (4,) + mine.shape)
    piece = lax.all_to_all(piece, "vel", 0, 0, tiled=True, axis_index_groups=FAR)
    mine = jnp.sum(piece, 0)
    piece = jnp.broadcast_to(mine[None], (16,) + mine.shape)
    piece = lax.all_to_all(piece, "vel", 0, 0, tiled=True, axis_index_groups=NEAR)
    return piece.reshape(SLOTS, 8, 128)


def per_device(distribution, rate_class, wall):
    block, edges, small = (256, 8, 128), (16, 8, 128), (22, 8, 128)
    part, last, first, inner_last, inner_first = kernel_call(
        moments_kernel, [(SLOTS, 8, 128)] + [edges] * 4, [(25, 8, 128), (2, 15, 8, 128)]
    )(distribution)
    sums = all_sum(part)
    sums, last_out, first_out = lax.optimization_barrier((sums, last, first))
    prev, following = to_both(sums[:12], sums[6:18])
    before, after = to_both(last_out, first_out)
    moments, extra, to_next, to_prev, cell = kernel_call(
        first_kernel, [(13, 8, 128), (5, 8, 128), small, small, (9, 8, 128)], []
    )(sums, prev, following, rate_class, wall, last, first, inner_last, inner_first)
    prev, following = to_both(to_next, to_prev)
    (moved_field,) = kernel_call(field_kernel, [block], [(3, 32, 8, 128)])(
        cell, distribution, before, after
    )
    field, state = kernel_call(second_kernel, [block, (5, 8, 128)], [(3, 32, 8, 128)])(
        moments, extra, prev, following, rate_class, wall, moved_field
    )
    return field, state


def solution(mesh):
    return jax.shard_map(
        per_device,
        mesh=mesh,
        in_specs=(P("vel", "space", None), P("space", None), P("space", None)),
        out_specs=(P("vel", "space", None), P(None, "space", None)),
        check_vma=False,
    )
```

```python
import jax
import jax.numpy as jnp
import numpy as np
from jax import lax
from jax.experimental import pallas as pl
from jax.experimental.pallas import tpu as pltpu
from jax.sharding import PartitionSpec as P

VX, VY, VZ = 32, 32, 16
SWEEPS = 4
EDGE = 5.0
STEP = 0.1
HX = 2.0 * EDGE / VX
HY = 2.0 * EDGE / VY
HZ = 2.0 * EDGE / VZ
QUAD = float(HX * HY * HZ / (2.0 * np.pi) ** 1.5)
SPEED_X = [-EDGE + (i + 0.5) * HX for i in range(VX)]
SPEED_Y = [-EDGE + (i + 0.5) * HY for i in range(VY)]
SPEED_Z = [-EDGE + (i + 0.5) * HZ for i in range(VZ)]
F32 = jnp.float32

MOMENTS = [
    ((0, 0, 0),),
    ((1, 0, 0),),
    ((0, 1, 0),),
    ((0, 0, 1),),
    ((2, 0, 0), (0, 2, 0), (0, 0, 2)),
    ((2, 0, 0),),
    ((0, 2, 0),),
    ((1, 1, 0),),
    ((1, 0, 1),),
    ((0, 1, 1),),
    ((3, 0, 0), (1, 2, 0), (1, 0, 2)),
    ((2, 1, 0), (0, 3, 0), (0, 1, 2)),
    ((2, 0, 1), (0, 2, 1), (0, 0, 3)),
]


def times(moment, axis):
    return tuple(tuple(p + (d == axis) for d, p in enumerate(m)) for m in moment)


def key_of(moment):
    return tuple(sorted(moment))


PLAIN = []
for _m in MOMENTS + [times(m, 0) for m in MOMENTS] + [times(m, 1) for m in MOMENTS]:
    if key_of(_m) not in PLAIN:
        PLAIN.append(key_of(_m))
AT = {k: i for i, k in enumerate(PLAIN)}
ABS_X = len(PLAIN)
ABS_Y = ABS_X + 13
SETS = ABS_Y + 13
SLOTS = 64
FIRST_SET = 7


def slot_of(i):
    return FIRST_SET + i if i < 5 else FIRST_SET + 6 + i


def row_up(i):
    return (i // 8, i % 8) if i < 48 else (6, i - 48)


def row_down(i):
    return (12 + i // 8, i % 8) if i < 48 else (6, i - 45)


def rows_of():
    return lax.broadcasted_iota(jnp.int32, (8, 128), 0)


def added_up(terms):
    total = None
    for t in terms:
        total = t if total is None else total + t
    return total


def place():
    vel = lax.axis_index("vel")
    return lax.rem(vel, 4), lax.div(vel, 4)


def local_y(block, iy):
    return -EDGE + ((block * 8 + iy).astype(F32) + 0.5) * HY


def local_z(iz):
    return -EDGE + (iz.astype(F32) + 0.5) * HZ


def moved(value, ix, courant_y, shift, row, before, after):
    courant_x = STEP * abs(SPEED_X[ix])
    if SPEED_X[ix] > 0:
        beside = jnp.where(row == 0, before, pltpu.roll(value, 1, 0))
    else:
        beside = jnp.where(row == 7, after, pltpu.roll(value, 7, 0))
    along = pltpu.roll(value, shift, 1)
    return ((1.0 - courant_x) - courant_y) * value + courant_x * beside + courant_y * along


def powers():
    full = [(a, b) for a in range(5) for b in range(5 - a)]
    odd = [(a, b) for a in range(1, 5) for b in range(5 - a)]
    return {p: i for i, p in enumerate(full)}, {p: 15 + i for i, p in enumerate(odd)}


def moments_kernel(
    f_ref, part_ref, to_next_ref, to_prev_ref, inner_last_ref, inner_first_ref, acc, edge_acc
):
    block, iz = place()
    row = rows_of()
    shift = jnp.where(block >= 2, 1, 127)
    full_at, odd_at = powers()
    acc[...] = jnp.zeros_like(acc)
    edge_acc[...] = jnp.zeros_like(edge_acc)
    lane_x = (row.astype(F32) + 0.5) * HX

    def over_y(iy, carry):
        sy = local_y(block, iy)
        courant_y = STEP * jnp.abs(sy)
        sums = [[None] * 5, [None] * 5]
        for ix in range(VX):
            half = 1 if SPEED_X[ix] > 0 else 0
            k = ix % 16
            raw = f_ref[iy * 32 + ix]
            at = (2 * iy + k // 8, slice(k % 8, k % 8 + 1), slice(None))
            if half:
                to_next_ref[at] = raw[7:8, :]
                inner_last_ref[at] = raw[6:7, :]
            else:
                to_prev_ref[at] = raw[0:1, :]
                inner_first_ref[at] = raw[1:2, :]
            value = moved(raw, ix, courant_y, shift, row, 0.0, 0.0)
            for a in range(5):
                term = value if a == 0 else (SPEED_X[ix] ** a) * value
                sums[half][a] = term if sums[half][a] is None else sums[half][a] + term
        power = [1.0, sy, sy * sy, sy * sy * sy, sy * sy * sy * sy]
        full = [sums[1][a] + sums[0][a] for a in range(5)]
        odd = [sums[1][a] - sums[0][a] for a in range(5)]
        for (a, b), n in full_at.items():
            acc[n] = acc[n] + power[b] * full[a]
        for (a, b), n in odd_at.items():
            acc[n] = acc[n] + power[b] * odd[a]
        for side, ref, base in ((0, to_next_ref, 0.0), (1, to_prev_ref, -EDGE)):
            edge = [None] * 5
            for j in range(2):
                sx = lane_x + (base + 8 * HX * j)
                term = (STEP * jnp.abs(sx)) * ref[2 * iy + j]
                for a in range(5):
                    term = term if a == 0 else sx * term
                    edge[a] = term if edge[a] is None else edge[a] + term
            for (a, b), n in full_at.items():
                edge_acc[side, n] = edge_acc[side, n] + power[b] * edge[a]
        return carry

    lax.fori_loop(0, 8, over_y, 0)
    sz = local_z(iz)
    zs = [QUAD * jnp.ones((), F32), QUAD * sz, QUAD * sz * sz, QUAD * sz * sz * sz]
    sign = jnp.where(block >= 2, 1.0, -1.0).astype(F32)
    zy = [sign * z for z in zs]

    def all_sets(full, odd):
        out = [added_up(zs[c] * full(a, b) for a, b, c in monos) for monos in PLAIN]
        out += [added_up(zs[c] * odd(a + 1, b) for a, b, c in monos) for monos in MOMENTS]
        out += [added_up(zy[c] * full(a, b + 1) for a, b, c in monos) for monos in MOMENTS]
        return out

    for i, v in enumerate(all_sets(lambda a, b: acc[full_at[a, b]], lambda a, b: acc[odd_at[a, b]])):
        part_ref[slot_of(i)] = v
    part_ref[6] = jnp.zeros((8, 128), F32)
    for side, where in ((0, row_up), (1, row_down)):
        lines = {p: jnp.sum(edge_acc[side, n], axis=0, keepdims=True) for p, n in full_at.items()}
        factor = -1.0 if side else 1.0
        for i, v in enumerate(
            all_sets(lambda a, b: lines[a, b], lambda a, b: factor * lines[a, b])
        ):
            slot, r = where(i)
            part_ref[slot, r : r + 1, :] = v


def diffuse(own_source, far_source, row):
    own, far = own_source, far_source
    for _ in range(SWEEPS):
        own_down, far_down = pltpu.roll(own, 1, 0), pltpu.roll(far, 1, 0)
        own_up, far_up = pltpu.roll(own, 7, 0), pltpu.roll(far, 7, 0)
        new_own = (
            jnp.where(row == 0, far_down, own_down)
            + jnp.where(row == 7, far_up, own_up)
            + pltpu.roll(own, 1, 1)
            + pltpu.roll(own, 127, 1)
        )
        new_far = (
            jnp.where(row == 0, own_down, far_down)
            + jnp.where(row == 7, own_up, far_up)
            + pltpu.roll(far, 1, 1)
            + pltpu.roll(far, 127, 1)
        )
        own = (own_source + new_own) * 0.2
        far = (far_source + new_far) * 0.2
    return own


def heat_flux(m):
    inv = 1.0 / m[0]
    u = [m[1] * inv, m[2] * inv, m[3] * inv]
    p_zz = m[4] - m[5] - m[6]
    p = [[m[5], m[7], m[8]], [m[7], m[6], m[9]], [m[8], m[9], p_zz]]
    sq = u[0] * u[0] + u[1] * u[1] + u[2] * u[2]
    mass_sq = 2.0 * m[0] * sq
    return [
        0.5
        * (
            m[10 + i]
            - 2.0 * (u[0] * p[i][0] + u[1] * p[i][1] + u[2] * p[i][2])
            + u[i] * (mass_sq - m[4])
        )
        for i in range(3)
    ]


def cell_state(state, moments, rate_class, wall):
    density = state[0]
    inv = 1.0 / density
    u = [state[i] * inv for i in (1, 2, 3)]
    temperature = (2.0 * state[4] * inv - (u[0] * u[0] + u[1] * u[1] + u[2] * u[2])) * (1.0 / 3.0)
    heat = heat_flux(moments)
    frequency = 0.5 * jnp.exp2(rate_class.astype(F32))
    power = jnp.exp((1.0 - 0.81) * jnp.log(temperature))
    keep = jnp.exp(-STEP * frequency * density * power)
    inv_t = 1.0 / temperature
    rate = 1.0 - keep
    skew = ((1.0 - 2.0 / 3.0) / 5.0) * inv * inv_t * inv_t
    amplitude = rate * density * inv_t * lax.rsqrt(temperature)
    solid = wall > 0
    keep = jnp.where(solid, 0.0, keep)
    amplitude = jnp.where(solid, density, amplitude)
    inv_t = jnp.where(solid, 1.0, inv_t)
    u = [jnp.where(solid, 0.0, c) for c in u]
    heat = [jnp.where(solid, 0.0, skew * h) for h in heat]
    return keep, amplitude, inv_t, u, heat


def apply_added(sy, sz, cell):
    _, amplitude, inv_t, u, heat = cell
    dy, dz = sy - u[1], sz - u[2]
    square = (dy * dy + dz * dz) * inv_t
    return amplitude * jnp.exp(-0.5 * square), square - 5.0, dy * heat[1] + dz * heat[2]


def profile_x(cell, profile):
    _, _, inv_t, u, heat = cell
    for ix in range(VX):
        dx = SPEED_X[ix] - u[0]
        square = dx * dx * inv_t
        profile[0, ix] = jnp.exp(-0.5 * square)
        profile[1, ix] = square
        profile[2, ix] = dx * heat[0]


def line_sums(speeds, u, inv_t, top):
    out = [None] * (top + 1)
    for s in speeds:
        d = s - u
        e = jnp.exp(-0.5 * (d * d * inv_t))
        for a in range(top + 1):
            term = e if a == 0 else (s**a) * e
            out[a] = term if out[a] is None else out[a] + term
    return out


def central(raw, u, top):
    table = [raw]
    for _ in range(3):
        last = table[-1]
        table.append([last[a + 1] - u * last[a] for a in range(len(last) - 1)])
    return [line[: top + 1] for line in table]


def added_moments(cell):
    _, amplitude, inv_t, u, heat = cell
    scale = amplitude * QUAD
    half = VX // 2
    x_up = central(line_sums(SPEED_X[half:], u[0], inv_t, 7), u[0], 4)
    x_dn = central(line_sums(SPEED_X[:half], u[0], inv_t, 7), u[0], 4)
    y_up = central(line_sums(SPEED_Y[half:], u[1], inv_t, 7), u[1], 4)
    y_dn = central(line_sums(SPEED_Y[:half], u[1], inv_t, 7), u[1], 4)
    z_all = central([scale * z for z in line_sums(SPEED_Z, u[2], inv_t, 6)], u[2], 3)
    x_all = [[p + q for p, q in zip(r, s)] for r, s in zip(x_up, x_dn)]
    y_all = [[p + q for p, q in zip(r, s)] for r, s in zip(y_up, y_dn)]
    gx, gy, gz = heat
    hx, hy, hz = gx * inv_t, gy * inv_t, gz * inv_t

    def whole(xs, ys):
        plane = {}

        def at(a, b):
            if (a, b) not in plane:
                x = [xs[i][a] for i in range(4)]
                y = [ys[i][b] for i in range(4)]
                x0y0 = x[0] * y[0]
                x1y0, x0y1 = x[1] * y[0], x[0] * y[1]
                x2y0, x0y2 = x[2] * y[0], x[0] * y[2]
                p0 = (
                    x0y0
                    + hx * (x[3] * y[0] + x[1] * y[2])
                    + hy * (x[2] * y[1] + x[0] * y[3])
                    - 5.0 * (gx * x1y0 + gy * x0y1)
                )
                p1 = hz * (x2y0 + x0y2) - 5.0 * gz * x0y0
                p2 = hx * x1y0 + hy * x0y1
                p3 = hz * x0y0
                plane[a, b] = (p0, p1, p2, p3)
            return plane[a, b]

        out = []
        for monos in MOMENTS:
            total = None
            for a, b, c in monos:
                p = at(a, b)
                term = (
                    p[0] * z_all[0][c] + p[1] * z_all[1][c] + p[2] * z_all[2][c] + p[3] * z_all[3][c]
                )
                total = term if total is None else total + term
            out.append(total)
        return out

    def weighted(table, factor):
        return [[factor * v for v in line[1:5]] for line in table]

    return (
        whole(x_all, y_all),
        whole(weighted(x_up, STEP), y_all),
        whole(weighted(x_dn, -STEP), y_all),
        whole(x_all, weighted(y_up, STEP)),
        whole(x_all, weighted(y_dn, -STEP)),
    )


def flat(cell):
    keep, amplitude, inv_t, u, heat = cell
    return [keep, amplitude, inv_t, *u, *heat]


def cell_of(v):
    return v[0], v[1], v[2], v[3:6], v[6:9]


def keep_out(cell, ref):
    for i, v in enumerate(flat(cell)):
        ref[i] = v


def first_kernel(
    q_ref, prev_ref, next_ref, class_ref, wall_ref, last_ref, first_ref, inner_last_ref, inner_first_ref,
    m_ref, add_ref, to_next_ref, to_prev_ref, cell_ref,
):
    block, iz = place()
    row = rows_of()
    shift = jnp.where(block >= 2, 1, 127)

    def line(ref, first, at):
        return ref[at[0] - first, at[1] : at[1] + 1, :]

    def whole_set(i):
        above, below = line(prev_ref, 0, row_up(i)), line(next_ref, 6, row_down(i))
        return q_ref[slot_of(i)] + jnp.where(row == 0, above, jnp.where(row == 7, below, 0.0))

    sets = [whole_set(i) for i in range(SETS)]
    scale = [1.0, 1.0, 1.0, 1.0, 0.5]
    state = []
    for k in range(5):
        far = jnp.where(row < 4, next_ref[1 + k], prev_ref[FIRST_SET + k])
        up, down = line(q_ref, 0, row_up(k)), line(q_ref, 0, row_down(k))
        far = far + jnp.where(row == 0, up, jnp.where(row == 7, down, 0.0))
        state.append(diffuse(scale[k] * sets[k], scale[k] * far, row))
    cell = cell_state(state, sets[:13], class_ref[...], wall_ref[...])
    keep = cell[0]
    keep_out(cell, cell_ref)
    sz = local_z(iz)

    for r, base_x, outer, inner, out in (
        (7, 0.0, last_ref, inner_last_ref, to_next_ref),
        (0, -EDGE, first_ref, inner_first_ref, to_prev_ref),
    ):
        line_cell = cell_of([jnp.broadcast_to(v[r : r + 1, :], (8, 128)) for v in flat(cell)])
        parts = []
        for j in range(2):
            sx = (row.astype(F32) + 0.5) * HX + (base_x + 8 * HX * j)
            dx = sx - line_cell[3][0]
            square = dx * dx * line_cell[2]
            parts.append(
                (STEP * jnp.abs(sx), jnp.exp(-0.5 * square), square, dx * line_cell[4][0])
            )

        def edge_y(iy, carry, line_cell=line_cell, parts=parts, outer=outer, inner=inner, out=out):
            sy = local_y(block, iy)
            courant_y = STEP * jnp.abs(sy)
            base, square, flux = apply_added(sy, sz, line_cell)
            for j, (courant_x, bell, square_x, flux_x) in enumerate(parts):
                value = outer[2 * iy + j]
                value = (
                    ((1.0 - courant_x) - courant_y) * value
                    + courant_x * inner[2 * iy + j]
                    + courant_y * pltpu.roll(value, shift, 1)
                )
                added = (base * bell) * (1.0 + (flux + flux_x) * (square + square_x))
                out[6 + 2 * iy + j] = line_cell[0] * value + added
            return carry

        lax.fori_loop(0, 8, edge_y, 0, unroll=True)

    g_all, g_xu, g_xd, g_yu, g_yd = added_moments(cell)
    part = 0.5 * STEP * keep
    for k, monos in enumerate(MOMENTS):
        sx_k, ax_k = sets[AT[key_of(times(monos, 0))]], sets[ABS_X + k]
        sy_k, ay_k = sets[AT[key_of(times(monos, 1))]], sets[ABS_Y + k]
        x_up = part * (ax_k + sx_k) + g_xu[k]
        x_dn = part * (ax_k - sx_k) + g_xd[k]
        y_up = part * (ay_k + sy_k) + g_yu[k]
        y_dn = part * (ay_k - sy_k) + g_yd[k]
        from_up, from_dn = pltpu.roll(x_up, 1, 0), pltpu.roll(x_dn, 7, 0)
        total = (
            (keep * sets[k] + g_all[k] - x_up - x_dn - y_up - y_dn)
            + jnp.where(row == 0, 0.0, from_up)
            + jnp.where(row == 7, 0.0, from_dn)
            + pltpu.roll(y_up, 1, 1)
            + pltpu.roll(y_dn, 127, 1)
        )
        m_ref[k] = total
        if k < 5:
            add_ref[k] = jnp.where(row == 0, from_up, jnp.where(row == 7, from_dn, 0.0))
            to_next_ref[k] = jnp.where(row == 0, from_up, total)
            to_prev_ref[k] = jnp.where(row == 7, from_dn, total)
        else:
            to_next_ref[5, k - 5 : k - 4, :] = x_up[7:8, :]
            to_prev_ref[5, k - 5 : k - 4, :] = x_dn[0:1, :]


def field_kernel(cell_ref, f_ref, before_ref, after_ref, t_ref, profile):
    block, iz = place()
    row = rows_of()
    shift = jnp.where(block >= 2, 1, 127)
    cell = cell_of([cell_ref[i] for i in range(9)])
    keep = cell[0]
    profile_x(cell, profile)
    sz = local_z(iz)

    def over_y(iy, carry):
        sy = local_y(block, iy)
        courant_y = STEP * jnp.abs(sy)
        base, square, flux = apply_added(sy, sz, cell)
        for ix in range(VX):
            k = ix % 16
            edge = (before_ref if SPEED_X[ix] > 0 else after_ref)[
                12 + 2 * iy + k // 8, k % 8 : k % 8 + 1, :
            ]
            value = moved(f_ref[iy * 32 + ix], ix, courant_y, shift, row, edge, edge)
            added = (base * profile[0, ix]) * (
                1.0 + (flux + profile[2, ix]) * (square + profile[1, ix])
            )
            value = keep * value + added
            t_ref[iy * 32 + ix] = moved(value, ix, courant_y, shift, row, 0.0, 0.0)
        return carry

    lax.fori_loop(0, 8, over_y, 0)


def second_kernel(
    m_ref, add_ref, prev_ref, next_ref, class_ref, wall_ref, t_ref,
    out_ref, state_ref, profile,
):
    block, iz = place()
    row = rows_of()
    moments = []
    for k in range(13):
        if k < 5:
            before, after = prev_ref[k], next_ref[k]
        else:
            before, after = prev_ref[5, k - 5 : k - 4, :], next_ref[5, k - 5 : k - 4, :]
        moments.append(
            m_ref[k] + jnp.where(row == 0, before, jnp.where(row == 7, after, 0.0))
        )
    scale = [1.0, 1.0, 1.0, 1.0, 0.5]
    state = []
    for k in range(5):
        far = jnp.where(row < 4, next_ref[k], prev_ref[k]) + add_ref[k]
        state.append(diffuse(scale[k] * moments[k], scale[k] * far, row))
        state_ref[k] = state[k]
    cell = cell_state(state, moments, class_ref[...], wall_ref[...])
    keep = cell[0]
    profile_x(cell, profile)
    sz = local_z(iz)

    def over_y(iy, carry):
        sy = local_y(block, iy)
        base, square, flux = apply_added(sy, sz, cell)
        for ix in range(VX):
            k = ix % 16
            edge = (prev_ref if SPEED_X[ix] > 0 else next_ref)[
                6 + 2 * iy + k // 8, k % 8 : k % 8 + 1, :
            ]
            courant_x = STEP * abs(SPEED_X[ix])
            here = row == (0 if SPEED_X[ix] > 0 else 7)
            value = t_ref[iy * 32 + ix] + jnp.where(here, courant_x * edge, 0.0)
            added = (base * profile[0, ix]) * (
                1.0 + (flux + profile[2, ix]) * (square + profile[1, ix])
            )
            out_ref[iy * 32 + ix] = keep * value + added
        return carry

    lax.fori_loop(0, 8, over_y, 0)


def kernel_call(body, outs, scratch, limit=32):
    return pl.pallas_call(
        body,
        out_shape=[jax.ShapeDtypeStruct(s, F32) for s in outs],
        scratch_shapes=[pltpu.VMEM(s, F32) for s in scratch],
        compiler_params=pltpu.CompilerParams(vmem_limit_bytes=limit * 1024 * 1024),
    )


def to_both(up_value, down_value):
    size = lax.axis_size("space")
    up = [(i, (i + 1) % size) for i in range(size)]
    down = [(j, i) for i, j in up]
    return lax.ppermute(up_value, "space", up), lax.ppermute(down_value, "space", down)


NEAR = [
    [(4 * b + k) * 4 + y for k in order for y in (2, 3, 0, 1)]
    for b, order in enumerate(((1, 0, 2, 3), (2, 3, 1, 0), (1, 0, 2, 3), (1, 0, 2, 3)))
]
FAR = [[NEAR[b][p] for b in (2, 3, 0, 1)] for p in range(16)]


def all_sum(part):
    piece = part.reshape(16, SLOTS // 2, 128)
    piece = lax.all_to_all(piece, "vel", 0, 0, tiled=True, axis_index_groups=NEAR)
    mine = jnp.sum(piece, 0)
    piece = jnp.broadcast_to(mine[None], (4,) + mine.shape)
    piece = lax.all_to_all(piece, "vel", 0, 0, tiled=True, axis_index_groups=FAR)
    mine = jnp.sum(piece, 0)
    piece = jnp.broadcast_to(mine[None], (16,) + mine.shape)
    piece = lax.all_to_all(piece, "vel", 0, 0, tiled=True, axis_index_groups=NEAR)
    return piece.reshape(SLOTS, 8, 128)


def per_device(distribution, rate_class, wall):
    block, edges, small = (256, 8, 128), (16, 8, 128), (22, 8, 128)
    part, last, first, inner_last, inner_first = kernel_call(
        moments_kernel, [(SLOTS, 8, 128)] + [edges] * 4, [(25, 8, 128), (2, 15, 8, 128)]
    )(distribution)
    sums = all_sum(part)
    prev_sums, next_sums = to_both(
        jnp.concatenate([sums[:12], last]), jnp.concatenate([sums[6:18], first])
    )
    moments, extra, to_next, to_prev, cell = kernel_call(
        first_kernel, [(13, 8, 128), (5, 8, 128), small, small, (9, 8, 128)], []
    )(sums, prev_sums, next_sums, rate_class, wall, last, first, inner_last, inner_first)
    prev, following = to_both(to_next, to_prev)
    (moved_field,) = kernel_call(field_kernel, [block], [(3, 32, 8, 128)])(
        cell, distribution, prev_sums, next_sums
    )
    field, state = kernel_call(second_kernel, [block, (5, 8, 128)], [(3, 32, 8, 128)])(
        moments, extra, prev, following, rate_class, wall, moved_field
    )
    return field, state


def solution(mesh):
    return jax.shard_map(
        per_device,
        mesh=mesh,
        in_specs=(P("vel", "space", None), P("space", None), P("space", None)),
        out_specs=(P("vel", "space", None), P(None, "space", None)),
        check_vma=False,
    )
```

```python
import jax
import jax.numpy as jnp
import numpy as np
from jax import lax
from jax.experimental import pallas as pl
from jax.experimental.pallas import tpu as pltpu
from jax.sharding import PartitionSpec as P

VX, VY, VZ = 32, 32, 16
SWEEPS = 4
EDGE = 5.0
STEP = 0.1
HX = 2.0 * EDGE / VX
HY = 2.0 * EDGE / VY
HZ = 2.0 * EDGE / VZ
QUAD = float(HX * HY * HZ / (2.0 * np.pi) ** 1.5)
SPEED_X = [-EDGE + (i + 0.5) * HX for i in range(VX)]
SPEED_Y = [-EDGE + (i + 0.5) * HY for i in range(VY)]
SPEED_Z = [-EDGE + (i + 0.5) * HZ for i in range(VZ)]
F32 = jnp.float32

MOMENTS = [
    ((0, 0, 0),),
    ((1, 0, 0),),
    ((0, 1, 0),),
    ((0, 0, 1),),
    ((2, 0, 0), (0, 2, 0), (0, 0, 2)),
    ((2, 0, 0),),
    ((0, 2, 0),),
    ((1, 1, 0),),
    ((1, 0, 1),),
    ((0, 1, 1),),
    ((3, 0, 0), (1, 2, 0), (1, 0, 2)),
    ((2, 1, 0), (0, 3, 0), (0, 1, 2)),
    ((2, 0, 1), (0, 2, 1), (0, 0, 3)),
]


def times(moment, axis):
    return tuple(tuple(p + (d == axis) for d, p in enumerate(m)) for m in moment)


def key_of(moment):
    return tuple(sorted(moment))


PLAIN = []
for _m in MOMENTS + [times(m, 0) for m in MOMENTS] + [times(m, 1) for m in MOMENTS]:
    if key_of(_m) not in PLAIN:
        PLAIN.append(key_of(_m))
AT = {k: i for i, k in enumerate(PLAIN)}
ABS_X = len(PLAIN)
ABS_Y = ABS_X + 13
SETS = ABS_Y + 13
SLOTS = 64
FIRST_SET = 7


def slot_of(i):
    return FIRST_SET + i if i < 5 else FIRST_SET + 6 + i


def row_up(i):
    return (i // 8, i % 8) if i < 48 else (6, i - 48)


def row_down(i):
    return (12 + i // 8, i % 8) if i < 48 else (6, i - 45)


def rows_of():
    return lax.broadcasted_iota(jnp.int32, (8, 128), 0)


def added_up(terms):
    total = None
    for t in terms:
        total = t if total is None else total + t
    return total


def place():
    vel = lax.axis_index("vel")
    return lax.rem(vel, 4), lax.div(vel, 4)


def local_y(block, iy):
    return -EDGE + ((block * 8 + iy).astype(F32) + 0.5) * HY


def local_z(iz):
    return -EDGE + (iz.astype(F32) + 0.5) * HZ


def moved(value, ix, courant_y, shift, row, before, after):
    courant_x = STEP * abs(SPEED_X[ix])
    if SPEED_X[ix] > 0:
        beside = jnp.where(row == 0, before, pltpu.roll(value, 1, 0))
    else:
        beside = jnp.where(row == 7, after, pltpu.roll(value, 7, 0))
    along = pltpu.roll(value, shift, 1)
    return ((1.0 - courant_x) - courant_y) * value + courant_x * beside + courant_y * along


def powers():
    full = [(a, b) for a in range(5) for b in range(5 - a)]
    odd = [(a, b) for a in range(1, 5) for b in range(5 - a)]
    return {p: i for i, p in enumerate(full)}, {p: 15 + i for i, p in enumerate(odd)}


def moments_kernel(
    f_ref, part_ref, to_next_ref, to_prev_ref, inner_last_ref, inner_first_ref, acc, edge_acc
):
    block, iz = place()
    row = rows_of()
    shift = jnp.where(block >= 2, 1, 127)
    full_at, odd_at = powers()
    acc[...] = jnp.zeros_like(acc)
    edge_acc[...] = jnp.zeros_like(edge_acc)
    lane_x = (row.astype(F32) + 0.5) * HX

    def over_y(iy, carry):
        sy = local_y(block, iy)
        courant_y = STEP * jnp.abs(sy)
        sums = [[None] * 5, [None] * 5]
        for ix in range(VX):
            half = 1 if SPEED_X[ix] > 0 else 0
            k = ix % 16
            raw = f_ref[iy * 32 + ix]
            at = (2 * iy + k // 8, slice(k % 8, k % 8 + 1), slice(None))
            if half:
                to_next_ref[at] = raw[7:8, :]
                inner_last_ref[at] = raw[6:7, :]
            else:
                to_prev_ref[at] = raw[0:1, :]
                inner_first_ref[at] = raw[1:2, :]
            value = moved(raw, ix, courant_y, shift, row, 0.0, 0.0)
            for a in range(5):
                term = value if a == 0 else (SPEED_X[ix] ** a) * value
                sums[half][a] = term if sums[half][a] is None else sums[half][a] + term
        power = [1.0, sy, sy * sy, sy * sy * sy, sy * sy * sy * sy]
        full = [sums[1][a] + sums[0][a] for a in range(5)]
        odd = [sums[1][a] - sums[0][a] for a in range(5)]
        for (a, b), n in full_at.items():
            acc[n] = acc[n] + power[b] * full[a]
        for (a, b), n in odd_at.items():
            acc[n] = acc[n] + power[b] * odd[a]
        for side, ref, base in ((0, to_next_ref, 0.0), (1, to_prev_ref, -EDGE)):
            edge = [None] * 5
            for j in range(2):
                sx = lane_x + (base + 8 * HX * j)
                term = (STEP * jnp.abs(sx)) * ref[2 * iy + j]
                for a in range(5):
                    term = term if a == 0 else sx * term
                    edge[a] = term if edge[a] is None else edge[a] + term
            for (a, b), n in full_at.items():
                edge_acc[side, n] = edge_acc[side, n] + power[b] * edge[a]
        return carry

    lax.fori_loop(0, 8, over_y, 0)
    sz = local_z(iz)
    zs = [QUAD * jnp.ones((), F32), QUAD * sz, QUAD * sz * sz, QUAD * sz * sz * sz]
    sign = jnp.where(block >= 2, 1.0, -1.0).astype(F32)
    zy = [sign * z for z in zs]

    def all_sets(full, odd):
        out = [added_up(zs[c] * full(a, b) for a, b, c in monos) for monos in PLAIN]
        out += [added_up(zs[c] * odd(a + 1, b) for a, b, c in monos) for monos in MOMENTS]
        out += [added_up(zy[c] * full(a, b + 1) for a, b, c in monos) for monos in MOMENTS]
        return out

    for i, v in enumerate(all_sets(lambda a, b: acc[full_at[a, b]], lambda a, b: acc[odd_at[a, b]])):
        part_ref[slot_of(i)] = v
    part_ref[6] = jnp.zeros((8, 128), F32)
    for side, where in ((0, row_up), (1, row_down)):
        lines = {p: jnp.sum(edge_acc[side, n], axis=0, keepdims=True) for p, n in full_at.items()}
        factor = -1.0 if side else 1.0
        for i, v in enumerate(
            all_sets(lambda a, b: lines[a, b], lambda a, b: factor * lines[a, b])
        ):
            slot, r = where(i)
            part_ref[slot, r : r + 1, :] = v


def diffuse(own_source, far_source, row):
    own, far = own_source, far_source
    for _ in range(SWEEPS):
        own_down, far_down = pltpu.roll(own, 1, 0), pltpu.roll(far, 1, 0)
        own_up, far_up = pltpu.roll(own, 7, 0), pltpu.roll(far, 7, 0)
        new_own = (
            jnp.where(row == 0, far_down, own_down)
            + jnp.where(row == 7, far_up, own_up)
            + pltpu.roll(own, 1, 1)
            + pltpu.roll(own, 127, 1)
        )
        new_far = (
            jnp.where(row == 0, own_down, far_down)
            + jnp.where(row == 7, own_up, far_up)
            + pltpu.roll(far, 1, 1)
            + pltpu.roll(far, 127, 1)
        )
        own = (own_source + new_own) * 0.2
        far = (far_source + new_far) * 0.2
    return own


def heat_flux(m):
    inv = 1.0 / m[0]
    u = [m[1] * inv, m[2] * inv, m[3] * inv]
    p_zz = m[4] - m[5] - m[6]
    p = [[m[5], m[7], m[8]], [m[7], m[6], m[9]], [m[8], m[9], p_zz]]
    sq = u[0] * u[0] + u[1] * u[1] + u[2] * u[2]
    mass_sq = 2.0 * m[0] * sq
    return [
        0.5
        * (
            m[10 + i]
            - 2.0 * (u[0] * p[i][0] + u[1] * p[i][1] + u[2] * p[i][2])
            + u[i] * (mass_sq - m[4])
        )
        for i in range(3)
    ]


def cell_state(state, moments, rate_class, wall):
    density = state[0]
    inv = 1.0 / density
    u = [state[i] * inv for i in (1, 2, 3)]
    temperature = (2.0 * state[4] * inv - (u[0] * u[0] + u[1] * u[1] + u[2] * u[2])) * (1.0 / 3.0)
    heat = heat_flux(moments)
    frequency = 0.5 * jnp.exp2(rate_class.astype(F32))
    power = jnp.exp((1.0 - 0.81) * jnp.log(temperature))
    keep = jnp.exp(-STEP * frequency * density * power)
    inv_t = 1.0 / temperature
    rate = 1.0 - keep
    skew = ((1.0 - 2.0 / 3.0) / 5.0) * inv * inv_t * inv_t
    amplitude = rate * density * inv_t * lax.rsqrt(temperature)
    solid = wall > 0
    keep = jnp.where(solid, 0.0, keep)
    amplitude = jnp.where(solid, density, amplitude)
    inv_t = jnp.where(solid, 1.0, inv_t)
    u = [jnp.where(solid, 0.0, c) for c in u]
    heat = [jnp.where(solid, 0.0, skew * h) for h in heat]
    return keep, amplitude, inv_t, u, heat


def apply_added(sy, sz, cell):
    _, amplitude, inv_t, u, heat = cell
    dy, dz = sy - u[1], sz - u[2]
    square = (dy * dy + dz * dz) * inv_t
    return amplitude * jnp.exp(-0.5 * square), square - 5.0, dy * heat[1] + dz * heat[2]


def profile_x(cell, profile):
    _, _, inv_t, u, heat = cell
    for ix in range(VX):
        dx = SPEED_X[ix] - u[0]
        square = dx * dx * inv_t
        profile[0, ix] = jnp.exp(-0.5 * square)
        profile[1, ix] = square
        profile[2, ix] = dx * heat[0]


def line_sums(speeds, u, inv_t, top):
    out = [None] * (top + 1)
    for s in speeds:
        d = s - u
        e = jnp.exp(-0.5 * (d * d * inv_t))
        for a in range(top + 1):
            term = e if a == 0 else (s**a) * e
            out[a] = term if out[a] is None else out[a] + term
    return out


def central(raw, u, top):
    table = [raw]
    for _ in range(3):
        last = table[-1]
        table.append([last[a + 1] - u * last[a] for a in range(len(last) - 1)])
    return [line[: top + 1] for line in table]


def added_moments(cell):
    _, amplitude, inv_t, u, heat = cell
    scale = amplitude * QUAD
    half = VX // 2
    x_up = central(line_sums(SPEED_X[half:], u[0], inv_t, 7), u[0], 4)
    x_dn = central(line_sums(SPEED_X[:half], u[0], inv_t, 7), u[0], 4)
    y_up = central(line_sums(SPEED_Y[half:], u[1], inv_t, 7), u[1], 4)
    y_dn = central(line_sums(SPEED_Y[:half], u[1], inv_t, 7), u[1], 4)
    z_all = central([scale * z for z in line_sums(SPEED_Z, u[2], inv_t, 6)], u[2], 3)
    x_all = [[p + q for p, q in zip(r, s)] for r, s in zip(x_up, x_dn)]
    y_all = [[p + q for p, q in zip(r, s)] for r, s in zip(y_up, y_dn)]
    gx, gy, gz = heat
    hx, hy, hz = gx * inv_t, gy * inv_t, gz * inv_t

    def whole(xs, ys):
        plane = {}

        def at(a, b):
            if (a, b) not in plane:
                x = [xs[i][a] for i in range(4)]
                y = [ys[i][b] for i in range(4)]
                x0y0 = x[0] * y[0]
                x1y0, x0y1 = x[1] * y[0], x[0] * y[1]
                x2y0, x0y2 = x[2] * y[0], x[0] * y[2]
                p0 = (
                    x0y0
                    + hx * (x[3] * y[0] + x[1] * y[2])
                    + hy * (x[2] * y[1] + x[0] * y[3])
                    - 5.0 * (gx * x1y0 + gy * x0y1)
                )
                p1 = hz * (x2y0 + x0y2) - 5.0 * gz * x0y0
                p2 = hx * x1y0 + hy * x0y1
                p3 = hz * x0y0
                plane[a, b] = (p0, p1, p2, p3)
            return plane[a, b]

        out = []
        for monos in MOMENTS:
            total = None
            for a, b, c in monos:
                p = at(a, b)
                term = (
                    p[0] * z_all[0][c] + p[1] * z_all[1][c] + p[2] * z_all[2][c] + p[3] * z_all[3][c]
                )
                total = term if total is None else total + term
            out.append(total)
        return out

    def weighted(table, factor):
        return [[factor * v for v in line[1:5]] for line in table]

    return (
        whole(x_all, y_all),
        whole(weighted(x_up, STEP), y_all),
        whole(weighted(x_dn, -STEP), y_all),
        whole(x_all, weighted(y_up, STEP)),
        whole(x_all, weighted(y_dn, -STEP)),
    )


def flat(cell):
    keep, amplitude, inv_t, u, heat = cell
    return [keep, amplitude, inv_t, *u, *heat]


def cell_of(v):
    return v[0], v[1], v[2], v[3:6], v[6:9]


def keep_out(cell, ref):
    for i, v in enumerate(flat(cell)):
        ref[i] = v


def first_kernel(
    q_ref, prev_ref, next_ref, class_ref, wall_ref, last_ref, first_ref, inner_last_ref, inner_first_ref,
    m_ref, add_ref, to_next_ref, to_prev_ref, cell_ref,
):
    block, iz = place()
    row = rows_of()
    shift = jnp.where(block >= 2, 1, 127)

    def line(ref, first, at):
        return ref[at[0] - first, at[1] : at[1] + 1, :]

    def whole_set(i):
        above, below = line(prev_ref, 0, row_up(i)), line(next_ref, 6, row_down(i))
        return q_ref[(slot_of(i) + TURN) % SLOTS] + jnp.where(row == 0, above, jnp.where(row == 7, below, 0.0))

    sets = [whole_set(i) for i in range(SETS)]
    scale = [1.0, 1.0, 1.0, 1.0, 0.5]
    state = []
    for k in range(5):
        far = jnp.where(row < 4, next_ref[1 + k], prev_ref[FIRST_SET + k])
        up, down = line(q_ref, -TURN, row_up(k)), line(q_ref, -TURN, row_down(k))
        far = far + jnp.where(row == 0, up, jnp.where(row == 7, down, 0.0))
        state.append(diffuse(scale[k] * sets[k], scale[k] * far, row))
    cell = cell_state(state, sets[:13], class_ref[...], wall_ref[...])
    keep = cell[0]
    keep_out(cell, cell_ref)
    sz = local_z(iz)

    for r, base_x, outer, inner, out in (
        (7, 0.0, last_ref, inner_last_ref, to_next_ref),
        (0, -EDGE, first_ref, inner_first_ref, to_prev_ref),
    ):
        line_cell = cell_of([jnp.broadcast_to(v[r : r + 1, :], (8, 128)) for v in flat(cell)])
        parts = []
        for j in range(2):
            sx = (row.astype(F32) + 0.5) * HX + (base_x + 8 * HX * j)
            dx = sx - line_cell[3][0]
            square = dx * dx * line_cell[2]
            parts.append(
                (STEP * jnp.abs(sx), jnp.exp(-0.5 * square), square, dx * line_cell[4][0])
            )

        def edge_y(iy, carry, line_cell=line_cell, parts=parts, outer=outer, inner=inner, out=out):
            sy = local_y(block, iy)
            courant_y = STEP * jnp.abs(sy)
            base, square, flux = apply_added(sy, sz, line_cell)
            for j, (courant_x, bell, square_x, flux_x) in enumerate(parts):
                value = outer[2 * iy + j]
                value = (
                    ((1.0 - courant_x) - courant_y) * value
                    + courant_x * inner[2 * iy + j]
                    + courant_y * pltpu.roll(value, shift, 1)
                )
                added = (base * bell) * (1.0 + (flux + flux_x) * (square + square_x))
                out[6 + 2 * iy + j] = line_cell[0] * value + added
            return carry

        lax.fori_loop(0, 8, edge_y, 0, unroll=True)

    g_all, g_xu, g_xd, g_yu, g_yd = added_moments(cell)
    part = 0.5 * STEP * keep
    for k, monos in enumerate(MOMENTS):
        sx_k, ax_k = sets[AT[key_of(times(monos, 0))]], sets[ABS_X + k]
        sy_k, ay_k = sets[AT[key_of(times(monos, 1))]], sets[ABS_Y + k]
        x_up = part * (ax_k + sx_k) + g_xu[k]
        x_dn = part * (ax_k - sx_k) + g_xd[k]
        y_up = part * (ay_k + sy_k) + g_yu[k]
        y_dn = part * (ay_k - sy_k) + g_yd[k]
        from_up, from_dn = pltpu.roll(x_up, 1, 0), pltpu.roll(x_dn, 7, 0)
        total = (
            (keep * sets[k] + g_all[k] - x_up - x_dn - y_up - y_dn)
            + jnp.where(row == 0, 0.0, from_up)
            + jnp.where(row == 7, 0.0, from_dn)
            + pltpu.roll(y_up, 1, 1)
            + pltpu.roll(y_dn, 127, 1)
        )
        m_ref[k] = total
        if k < 5:
            add_ref[k] = jnp.where(row == 0, from_up, jnp.where(row == 7, from_dn, 0.0))
            to_next_ref[k] = jnp.where(row == 0, from_up, total)
            to_prev_ref[k] = jnp.where(row == 7, from_dn, total)
        else:
            to_next_ref[5, k - 5 : k - 4, :] = x_up[7:8, :]
            to_prev_ref[5, k - 5 : k - 4, :] = x_dn[0:1, :]


def field_kernel(cell_ref, f_ref, before_ref, after_ref, t_ref, profile):
    block, iz = place()
    row = rows_of()
    shift = jnp.where(block >= 2, 1, 127)
    cell = cell_of([cell_ref[i] for i in range(9)])
    keep = cell[0]
    profile_x(cell, profile)
    sz = local_z(iz)

    def over_y(iy, carry):
        sy = local_y(block, iy)
        courant_y = STEP * jnp.abs(sy)
        base, square, flux = apply_added(sy, sz, cell)
        for ix in range(VX):
            k = ix % 16
            edge = (before_ref if SPEED_X[ix] > 0 else after_ref)[
                12 + 2 * iy + k // 8, k % 8 : k % 8 + 1, :
            ]
            value = moved(f_ref[iy * 32 + ix], ix, courant_y, shift, row, edge, edge)
            added = (base * profile[0, ix]) * (
                1.0 + (flux + profile[2, ix]) * (square + profile[1, ix])
            )
            value = keep * value + added
            t_ref[iy * 32 + ix] = moved(value, ix, courant_y, shift, row, 0.0, 0.0)
        return carry

    lax.fori_loop(0, 8, over_y, 0)


def second_kernel(
    m_ref, add_ref, prev_ref, next_ref, class_ref, wall_ref, t_ref,
    out_ref, state_ref, profile,
):
    block, iz = place()
    row = rows_of()
    moments = []
    for k in range(13):
        if k < 5:
            before, after = prev_ref[k], next_ref[k]
        else:
            before, after = prev_ref[5, k - 5 : k - 4, :], next_ref[5, k - 5 : k - 4, :]
        moments.append(
            m_ref[k] + jnp.where(row == 0, before, jnp.where(row == 7, after, 0.0))
        )
    scale = [1.0, 1.0, 1.0, 1.0, 0.5]
    state = []
    for k in range(5):
        far = jnp.where(row < 4, next_ref[k], prev_ref[k]) + add_ref[k]
        state.append(diffuse(scale[k] * moments[k], scale[k] * far, row))
        state_ref[k] = state[k]
    cell = cell_state(state, moments, class_ref[...], wall_ref[...])
    keep = cell[0]
    profile_x(cell, profile)
    sz = local_z(iz)

    def over_y(iy, carry):
        sy = local_y(block, iy)
        base, square, flux = apply_added(sy, sz, cell)
        for ix in range(VX):
            k = ix % 16
            edge = (prev_ref if SPEED_X[ix] > 0 else next_ref)[
                6 + 2 * iy + k // 8, k % 8 : k % 8 + 1, :
            ]
            courant_x = STEP * abs(SPEED_X[ix])
            here = row == (0 if SPEED_X[ix] > 0 else 7)
            value = t_ref[iy * 32 + ix] + jnp.where(here, courant_x * edge, 0.0)
            added = (base * profile[0, ix]) * (
                1.0 + (flux + profile[2, ix]) * (square + profile[1, ix])
            )
            out_ref[iy * 32 + ix] = keep * value + added
        return carry

    lax.fori_loop(0, 8, over_y, 0)


def kernel_call(body, outs, scratch, limit=32):
    return pl.pallas_call(
        body,
        out_shape=[jax.ShapeDtypeStruct(s, F32) for s in outs],
        scratch_shapes=[pltpu.VMEM(s, F32) for s in scratch],
        compiler_params=pltpu.CompilerParams(vmem_limit_bytes=limit * 1024 * 1024),
    )


def to_both(up_value, down_value):
    size = lax.axis_size("space")
    up = [(i, (i + 1) % size) for i in range(size)]
    down = [(j, i) for i, j in up]
    return lax.ppermute(up_value, "space", up), lax.ppermute(down_value, "space", down)


PLACES = ((3, 0, 1, 2), (2, 3, 0, 1), (0, 2, 2, 0), (1, 1, 3, 3))


def near(quarters):
    return [
        [(4 * b + PLACES[p][b]) * 4 + y for p in quarters for y in (2, 3, 0, 1)] for b in range(4)
    ]


SCATTER = near((0, 1, 2, 3))
GATHER = near((3, 0, 1, 2))
FAR = [[SCATTER[b][p] for b in (2, 3, 0, 1)] for p in range(16)]
TURN = 16


def all_sum(part):
    piece = part.reshape(16, SLOTS // 2, 128)
    piece = lax.all_to_all(piece, "vel", 0, 0, tiled=True, axis_index_groups=SCATTER)
    mine = jnp.sum(piece, 0)
    piece = jnp.broadcast_to(mine[None], (4,) + mine.shape)
    piece = lax.all_to_all(piece, "vel", 0, 0, tiled=True, axis_index_groups=FAR)
    mine = jnp.sum(piece, 0)
    piece = jnp.broadcast_to(mine[None], (16,) + mine.shape)
    piece = lax.all_to_all(piece, "vel", 0, 0, tiled=True, axis_index_groups=GATHER)
    return piece.reshape(SLOTS, 8, 128)


def per_device(distribution, rate_class, wall):
    block, edges, small = (256, 8, 128), (16, 8, 128), (22, 8, 128)
    part, last, first, inner_last, inner_first = kernel_call(
        moments_kernel, [(SLOTS, 8, 128)] + [edges] * 4, [(25, 8, 128), (2, 15, 8, 128)]
    )(distribution)
    sums = all_sum(part)
    prev_sums, next_sums = to_both(
        jnp.concatenate([sums[TURN : TURN + 12], last]), jnp.concatenate([sums[TURN + 6 : TURN + 18], first])
    )
    moments, extra, to_next, to_prev, cell = kernel_call(
        first_kernel, [(13, 8, 128), (5, 8, 128), small, small, (9, 8, 128)], []
    )(sums, prev_sums, next_sums, rate_class, wall, last, first, inner_last, inner_first)
    prev, following = to_both(to_next, to_prev)
    (moved_field,) = kernel_call(field_kernel, [block], [(3, 32, 8, 128)])(
        cell, distribution, prev_sums, next_sums
    )
    field, state = kernel_call(second_kernel, [block, (5, 8, 128)], [(3, 32, 8, 128)])(
        moments, extra, prev, following, rate_class, wall, moved_field
    )
    return field, state


def solution(mesh):
    return jax.shard_map(
        per_device,
        mesh=mesh,
        in_specs=(P("vel", "space", None), P("space", None), P("space", None)),
        out_specs=(P("vel", "space", None), P(None, "space", None)),
        check_vma=False,
    )
```

```python
import jax
import jax.numpy as jnp
import numpy as np
from jax import lax
from jax.experimental import pallas as pl
from jax.experimental.pallas import tpu as pltpu
from jax.sharding import PartitionSpec as P

VX, VY, VZ = 32, 32, 16
SWEEPS = 4
EDGE = 5.0
STEP = 0.1
HX = 2.0 * EDGE / VX
HY = 2.0 * EDGE / VY
HZ = 2.0 * EDGE / VZ
QUAD = float(HX * HY * HZ / (2.0 * np.pi) ** 1.5)
SPEED_X = [-EDGE + (i + 0.5) * HX for i in range(VX)]
SPEED_Y = [-EDGE + (i + 0.5) * HY for i in range(VY)]
SPEED_Z = [-EDGE + (i + 0.5) * HZ for i in range(VZ)]
F32 = jnp.float32

MOMENTS = [
    ((0, 0, 0),),
    ((1, 0, 0),),
    ((0, 1, 0),),
    ((0, 0, 1),),
    ((2, 0, 0), (0, 2, 0), (0, 0, 2)),
    ((2, 0, 0),),
    ((0, 2, 0),),
    ((1, 1, 0),),
    ((1, 0, 1),),
    ((0, 1, 1),),
    ((3, 0, 0), (1, 2, 0), (1, 0, 2)),
    ((2, 1, 0), (0, 3, 0), (0, 1, 2)),
    ((2, 0, 1), (0, 2, 1), (0, 0, 3)),
]


def times(moment, axis):
    return tuple(tuple(p + (d == axis) for d, p in enumerate(m)) for m in moment)


def key_of(moment):
    return tuple(sorted(moment))


PLAIN = []
for _m in MOMENTS + [times(m, 0) for m in MOMENTS] + [times(m, 1) for m in MOMENTS]:
    if key_of(_m) not in PLAIN:
        PLAIN.append(key_of(_m))
AT = {k: i for i, k in enumerate(PLAIN)}
ABS_X = len(PLAIN)
ABS_Y = ABS_X + 13
SETS = ABS_Y + 13
SLOTS = 64
FIRST_SET = 7


def slot_of(i):
    return FIRST_SET + i if i < 5 else FIRST_SET + 6 + i


def row_up(i):
    return (i // 8, i % 8) if i < 48 else (6, i - 48)


def row_down(i):
    return (12 + i // 8, i % 8) if i < 48 else (6, i - 45)


def rows_of():
    return lax.broadcasted_iota(jnp.int32, (8, 128), 0)


def added_up(terms):
    total = None
    for t in terms:
        total = t if total is None else total + t
    return total


def place():
    vel = lax.axis_index("vel")
    return lax.rem(vel, 4), lax.div(vel, 4)


def local_y(block, iy):
    return -EDGE + ((block * 8 + iy).astype(F32) + 0.5) * HY


def local_z(iz):
    return -EDGE + (iz.astype(F32) + 0.5) * HZ


def moved(value, ix, courant_y, shift, row, before, after):
    courant_x = STEP * abs(SPEED_X[ix])
    if SPEED_X[ix] > 0:
        beside = jnp.where(row == 0, before, pltpu.roll(value, 1, 0))
    else:
        beside = jnp.where(row == 7, after, pltpu.roll(value, 7, 0))
    along = pltpu.roll(value, shift, 1)
    return ((1.0 - courant_x) - courant_y) * value + courant_x * beside + courant_y * along


def powers():
    full = [(a, b) for a in range(5) for b in range(5 - a)]
    odd = [(a, b) for a in range(1, 5) for b in range(5 - a)]
    return {p: i for i, p in enumerate(full)}, {p: 15 + i for i, p in enumerate(odd)}


def moments_kernel(
    f_ref, part_ref, to_next_ref, to_prev_ref, inner_last_ref, inner_first_ref, acc, edge_acc
):
    block, iz = place()
    row = rows_of()
    shift = jnp.where(block >= 2, 1, 127)
    full_at, odd_at = powers()
    acc[...] = jnp.zeros_like(acc)
    edge_acc[...] = jnp.zeros_like(edge_acc)
    lane_x = (row.astype(F32) + 0.5) * HX

    def over_y(iy, carry):
        sy = local_y(block, iy)
        courant_y = STEP * jnp.abs(sy)
        sums = [[None] * 5, [None] * 5]
        for ix in range(VX):
            half = 1 if SPEED_X[ix] > 0 else 0
            k = ix % 16
            raw = f_ref[iy * 32 + ix]
            at = (2 * iy + k // 8, slice(k % 8, k % 8 + 1), slice(None))
            if half:
                to_next_ref[at] = raw[7:8, :]
                inner_last_ref[at] = raw[6:7, :]
            else:
                to_prev_ref[at] = raw[0:1, :]
                inner_first_ref[at] = raw[1:2, :]
            value = moved(raw, ix, courant_y, shift, row, 0.0, 0.0)
            for a in range(5):
                term = value if a == 0 else (SPEED_X[ix] ** a) * value
                sums[half][a] = term if sums[half][a] is None else sums[half][a] + term
        power = [1.0, sy, sy * sy, sy * sy * sy, sy * sy * sy * sy]
        full = [sums[1][a] + sums[0][a] for a in range(5)]
        odd = [sums[1][a] - sums[0][a] for a in range(5)]
        for (a, b), n in full_at.items():
            acc[n] = acc[n] + power[b] * full[a]
        for (a, b), n in odd_at.items():
            acc[n] = acc[n] + power[b] * odd[a]
        for side, ref, base in ((0, to_next_ref, 0.0), (1, to_prev_ref, -EDGE)):
            edge = [None] * 5
            for j in range(2):
                sx = lane_x + (base + 8 * HX * j)
                term = (STEP * jnp.abs(sx)) * ref[2 * iy + j]
                for a in range(5):
                    term = term if a == 0 else sx * term
                    edge[a] = term if edge[a] is None else edge[a] + term
            for (a, b), n in full_at.items():
                edge_acc[side, n] = edge_acc[side, n] + power[b] * edge[a]
        return carry

    lax.fori_loop(0, 8, over_y, 0)
    sz = local_z(iz)
    zs = [QUAD * jnp.ones((), F32), QUAD * sz, QUAD * sz * sz, QUAD * sz * sz * sz]
    sign = jnp.where(block >= 2, 1.0, -1.0).astype(F32)
    zy = [sign * z for z in zs]

    def all_sets(full, odd):
        out = [added_up(zs[c] * full(a, b) for a, b, c in monos) for monos in PLAIN]
        out += [added_up(zs[c] * odd(a + 1, b) for a, b, c in monos) for monos in MOMENTS]
        out += [added_up(zy[c] * full(a, b + 1) for a, b, c in monos) for monos in MOMENTS]
        return out

    for i, v in enumerate(all_sets(lambda a, b: acc[full_at[a, b]], lambda a, b: acc[odd_at[a, b]])):
        part_ref[slot_of(i)] = v
    part_ref[6] = jnp.zeros((8, 128), F32)
    for side, where in ((0, row_up), (1, row_down)):
        lines = {p: jnp.sum(edge_acc[side, n], axis=0, keepdims=True) for p, n in full_at.items()}
        factor = -1.0 if side else 1.0
        for i, v in enumerate(
            all_sets(lambda a, b: lines[a, b], lambda a, b: factor * lines[a, b])
        ):
            slot, r = where(i)
            part_ref[slot, r : r + 1, :] = v


def diffuse(own_source, far_source, row):
    own, far = own_source, far_source
    for _ in range(SWEEPS):
        own_down, far_down = pltpu.roll(own, 1, 0), pltpu.roll(far, 1, 0)
        own_up, far_up = pltpu.roll(own, 7, 0), pltpu.roll(far, 7, 0)
        new_own = (
            jnp.where(row == 0, far_down, own_down)
            + jnp.where(row == 7, far_up, own_up)
            + pltpu.roll(own, 1, 1)
            + pltpu.roll(own, 127, 1)
        )
        new_far = (
            jnp.where(row == 0, own_down, far_down)
            + jnp.where(row == 7, own_up, far_up)
            + pltpu.roll(far, 1, 1)
            + pltpu.roll(far, 127, 1)
        )
        own = (own_source + new_own) * 0.2
        far = (far_source + new_far) * 0.2
    return own


def heat_flux(m):
    inv = 1.0 / m[0]
    u = [m[1] * inv, m[2] * inv, m[3] * inv]
    p_zz = m[4] - m[5] - m[6]
    p = [[m[5], m[7], m[8]], [m[7], m[6], m[9]], [m[8], m[9], p_zz]]
    sq = u[0] * u[0] + u[1] * u[1] + u[2] * u[2]
    mass_sq = 2.0 * m[0] * sq
    return [
        0.5
        * (
            m[10 + i]
            - 2.0 * (u[0] * p[i][0] + u[1] * p[i][1] + u[2] * p[i][2])
            + u[i] * (mass_sq - m[4])
        )
        for i in range(3)
    ]


def cell_state(state, moments, rate_class, wall):
    density = state[0]
    inv = 1.0 / density
    u = [state[i] * inv for i in (1, 2, 3)]
    temperature = (2.0 * state[4] * inv - (u[0] * u[0] + u[1] * u[1] + u[2] * u[2])) * (1.0 / 3.0)
    heat = heat_flux(moments)
    frequency = 0.5 * jnp.exp2(rate_class.astype(F32))
    power = jnp.exp((1.0 - 0.81) * jnp.log(temperature))
    keep = jnp.exp(-STEP * frequency * density * power)
    inv_t = 1.0 / temperature
    rate = 1.0 - keep
    skew = ((1.0 - 2.0 / 3.0) / 5.0) * inv * inv_t * inv_t
    amplitude = rate * density * inv_t * lax.rsqrt(temperature)
    solid = wall > 0
    keep = jnp.where(solid, 0.0, keep)
    amplitude = jnp.where(solid, density, amplitude)
    inv_t = jnp.where(solid, 1.0, inv_t)
    u = [jnp.where(solid, 0.0, c) for c in u]
    heat = [jnp.where(solid, 0.0, skew * h) for h in heat]
    return keep, amplitude, inv_t, u, heat


def apply_added(sy, sz, cell):
    _, amplitude, inv_t, u, heat = cell
    dy, dz = sy - u[1], sz - u[2]
    square = (dy * dy + dz * dz) * inv_t
    return amplitude * jnp.exp(-0.5 * square), square - 5.0, dy * heat[1] + dz * heat[2]


def profile_x(cell, profile):
    _, _, inv_t, u, heat = cell
    for ix in range(VX):
        dx = SPEED_X[ix] - u[0]
        square = dx * dx * inv_t
        profile[0, ix] = jnp.exp(-0.5 * square)
        profile[1, ix] = square
        profile[2, ix] = dx * heat[0]


def line_sums(speeds, u, inv_t, top):
    out = [None] * (top + 1)
    for s in speeds:
        d = s - u
        term = jnp.exp(-0.5 * (d * d * inv_t))
        for b in range(top + 1):
            term = term if b == 0 else d * term
            out[b] = term if out[b] is None else out[b] + term
    return out


def mixed(raw, u, top):
    columns = [raw]
    for _ in range(top):
        last = columns[-1]
        columns.append([u * last[b] + last[b + 1] for b in range(len(last) - 1)])
    return [[column[b] for column in columns] for b in range(4)]


def added_moments(cell):
    _, amplitude, inv_t, u, heat = cell
    scale = amplitude * QUAD
    half = VX // 2
    x_up = mixed(line_sums(SPEED_X[half:], u[0], inv_t, 7), u[0], 4)
    x_dn = mixed(line_sums(SPEED_X[:half], u[0], inv_t, 7), u[0], 4)
    y_up = mixed(line_sums(SPEED_Y[half:], u[1], inv_t, 7), u[1], 4)
    y_dn = mixed(line_sums(SPEED_Y[:half], u[1], inv_t, 7), u[1], 4)
    z_all = mixed([scale * z for z in line_sums(SPEED_Z, u[2], inv_t, 6)], u[2], 3)
    x_all = [[p + q for p, q in zip(r, s)] for r, s in zip(x_up, x_dn)]
    y_all = [[p + q for p, q in zip(r, s)] for r, s in zip(y_up, y_dn)]
    gx, gy, gz = heat
    hx, hy, hz = gx * inv_t, gy * inv_t, gz * inv_t

    def whole(xs, ys):
        plane = {}

        def at(a, b):
            if (a, b) not in plane:
                x = [xs[i][a] for i in range(4)]
                y = [ys[i][b] for i in range(4)]
                x0y0 = x[0] * y[0]
                x1y0, x0y1 = x[1] * y[0], x[0] * y[1]
                x2y0, x0y2 = x[2] * y[0], x[0] * y[2]
                p0 = (
                    x0y0
                    + hx * (x[3] * y[0] + x[1] * y[2])
                    + hy * (x[2] * y[1] + x[0] * y[3])
                    - 5.0 * (gx * x1y0 + gy * x0y1)
                )
                p1 = hz * (x2y0 + x0y2) - 5.0 * gz * x0y0
                p2 = hx * x1y0 + hy * x0y1
                p3 = hz * x0y0
                plane[a, b] = (p0, p1, p2, p3)
            return plane[a, b]

        out = []
        for monos in MOMENTS:
            total = None
            for a, b, c in monos:
                p = at(a, b)
                term = (
                    p[0] * z_all[0][c] + p[1] * z_all[1][c] + p[2] * z_all[2][c] + p[3] * z_all[3][c]
                )
                total = term if total is None else total + term
            out.append(total)
        return out

    def weighted(table, factor):
        return [[factor * v for v in line[1:5]] for line in table]

    return (
        whole(x_all, y_all),
        whole(weighted(x_up, STEP), y_all),
        whole(weighted(x_dn, -STEP), y_all),
        whole(x_all, weighted(y_up, STEP)),
        whole(x_all, weighted(y_dn, -STEP)),
    )


def flat(cell):
    keep, amplitude, inv_t, u, heat = cell
    return [keep, amplitude, inv_t, *u, *heat]


def cell_of(v):
    return v[0], v[1], v[2], v[3:6], v[6:9]


def keep_out(cell, ref):
    for i, v in enumerate(flat(cell)):
        ref[i] = v


def first_kernel(
    q_ref, prev_ref, next_ref, class_ref, wall_ref, last_ref, first_ref, inner_last_ref, inner_first_ref,
    m_ref, add_ref, to_next_ref, to_prev_ref, cell_ref,
):
    block, iz = place()
    row = rows_of()
    shift = jnp.where(block >= 2, 1, 127)

    def line(ref, first, at):
        return ref[at[0] - first, at[1] : at[1] + 1, :]

    def whole_set(i):
        above, below = line(prev_ref, 0, row_up(i)), line(next_ref, 6, row_down(i))
        return q_ref[slot_of(i)] + jnp.where(row == 0, above, jnp.where(row == 7, below, 0.0))

    sets = [whole_set(i) for i in range(SETS)]
    scale = [1.0, 1.0, 1.0, 1.0, 0.5]
    state = []
    for k in range(5):
        far = jnp.where(row < 4, next_ref[1 + k], prev_ref[FIRST_SET + k])
        up, down = line(q_ref, 0, row_up(k)), line(q_ref, 0, row_down(k))
        far = far + jnp.where(row == 0, up, jnp.where(row == 7, down, 0.0))
        state.append(diffuse(scale[k] * sets[k], scale[k] * far, row))
    cell = cell_state(state, sets[:13], class_ref[...], wall_ref[...])
    keep = cell[0]
    keep_out(cell, cell_ref)
    sz = local_z(iz)

    for r, base_x, outer, inner, out in (
        (7, 0.0, last_ref, inner_last_ref, to_next_ref),
        (0, -EDGE, first_ref, inner_first_ref, to_prev_ref),
    ):
        line_cell = cell_of([jnp.broadcast_to(v[r : r + 1, :], (8, 128)) for v in flat(cell)])
        parts = []
        for j in range(2):
            sx = (row.astype(F32) + 0.5) * HX + (base_x + 8 * HX * j)
            dx = sx - line_cell[3][0]
            square = dx * dx * line_cell[2]
            parts.append(
                (STEP * jnp.abs(sx), jnp.exp(-0.5 * square), square, dx * line_cell[4][0])
            )

        def edge_y(iy, carry, line_cell=line_cell, parts=parts, outer=outer, inner=inner, out=out):
            sy = local_y(block, iy)
            courant_y = STEP * jnp.abs(sy)
            base, square, flux = apply_added(sy, sz, line_cell)
            for j, (courant_x, bell, square_x, flux_x) in enumerate(parts):
                value = outer[2 * iy + j]
                value = (
                    ((1.0 - courant_x) - courant_y) * value
                    + courant_x * inner[2 * iy + j]
                    + courant_y * pltpu.roll(value, shift, 1)
                )
                added = (base * bell) * (1.0 + (flux + flux_x) * (square + square_x))
                out[6 + 2 * iy + j] = line_cell[0] * value + added
            return carry

        lax.fori_loop(0, 8, edge_y, 0, unroll=True)

    g_all, g_xu, g_xd, g_yu, g_yd = added_moments(cell)
    part = 0.5 * STEP * keep
    for k, monos in enumerate(MOMENTS):
        sx_k, ax_k = sets[AT[key_of(times(monos, 0))]], sets[ABS_X + k]
        sy_k, ay_k = sets[AT[key_of(times(monos, 1))]], sets[ABS_Y + k]
        x_up = part * (ax_k + sx_k) + g_xu[k]
        x_dn = part * (ax_k - sx_k) + g_xd[k]
        y_up = part * (ay_k + sy_k) + g_yu[k]
        y_dn = part * (ay_k - sy_k) + g_yd[k]
        from_up, from_dn = pltpu.roll(x_up, 1, 0), pltpu.roll(x_dn, 7, 0)
        total = (
            (keep * sets[k] + g_all[k] - x_up - x_dn - y_up - y_dn)
            + jnp.where(row == 0, 0.0, from_up)
            + jnp.where(row == 7, 0.0, from_dn)
            + pltpu.roll(y_up, 1, 1)
            + pltpu.roll(y_dn, 127, 1)
        )
        m_ref[k] = total
        if k < 5:
            add_ref[k] = jnp.where(row == 0, from_up, jnp.where(row == 7, from_dn, 0.0))
            to_next_ref[k] = jnp.where(row == 0, from_up, total)
            to_prev_ref[k] = jnp.where(row == 7, from_dn, total)
        else:
            to_next_ref[5, k - 5 : k - 4, :] = x_up[7:8, :]
            to_prev_ref[5, k - 5 : k - 4, :] = x_dn[0:1, :]


def field_kernel(cell_ref, f_ref, before_ref, after_ref, t_ref, profile):
    block, iz = place()
    row = rows_of()
    shift = jnp.where(block >= 2, 1, 127)
    cell = cell_of([cell_ref[i] for i in range(9)])
    keep = cell[0]
    profile_x(cell, profile)
    sz = local_z(iz)

    def over_y(iy, carry):
        sy = local_y(block, iy)
        courant_y = STEP * jnp.abs(sy)
        base, square, flux = apply_added(sy, sz, cell)
        for ix in range(VX):
            k = ix % 16
            edge = (before_ref if SPEED_X[ix] > 0 else after_ref)[
                12 + 2 * iy + k // 8, k % 8 : k % 8 + 1, :
            ]
            value = moved(f_ref[iy * 32 + ix], ix, courant_y, shift, row, edge, edge)
            added = (base * profile[0, ix]) * (
                1.0 + (flux + profile[2, ix]) * (square + profile[1, ix])
            )
            value = keep * value + added
            t_ref[iy * 32 + ix] = moved(value, ix, courant_y, shift, row, 0.0, 0.0)
        return carry

    lax.fori_loop(0, 8, over_y, 0)


def second_kernel(
    m_ref, add_ref, prev_ref, next_ref, class_ref, wall_ref, t_ref,
    out_ref, state_ref, profile, cell_ref,
):
    block, iz = place()
    row = rows_of()
    step = pl.program_id(0)

    @pl.when(step == 0)
    def _():
        moments = []
        for k in range(13):
            if k < 5:
                before, after = prev_ref[k], next_ref[k]
            else:
                before, after = prev_ref[5, k - 5 : k - 4, :], next_ref[5, k - 5 : k - 4, :]
            moments.append(
                m_ref[k] + jnp.where(row == 0, before, jnp.where(row == 7, after, 0.0))
            )
        scale = [1.0, 1.0, 1.0, 1.0, 0.5]
        state = []
        for k in range(5):
            far = jnp.where(row < 4, next_ref[k], prev_ref[k]) + add_ref[k]
            state.append(diffuse(scale[k] * moments[k], scale[k] * far, row))
            state_ref[k] = state[k]
        cell = cell_state(state, moments, class_ref[...], wall_ref[...])
        profile_x(cell, profile)
        keep_out(cell, cell_ref)

    cell = cell_of([cell_ref[i] for i in range(9)])
    keep = cell[0]
    sz = local_z(iz)

    def over_y(iy, carry):
        sy = local_y(block, iy)
        base, square, flux = apply_added(sy, sz, cell)
        for ix in range(VX):
            k = ix % 16
            edge = (prev_ref if SPEED_X[ix] > 0 else next_ref)[
                6 + 2 * iy + k // 8, k % 8 : k % 8 + 1, :
            ]
            courant_x = STEP * abs(SPEED_X[ix])
            here = row == (0 if SPEED_X[ix] > 0 else 7)
            value = t_ref[iy * 32 + ix] + jnp.where(here, courant_x * edge, 0.0)
            added = (base * profile[0, ix]) * (
                1.0 + (flux + profile[2, ix]) * (square + profile[1, ix])
            )
            out_ref[(iy - 4 * step) * 32 + ix] = keep * value + added
        return carry

    lax.fori_loop(4 * step, 4 * (step + 1), over_y, 0)


def kernel_call(body, outs, scratch, limit=32, **kw):
    return pl.pallas_call(
        body,
        out_shape=[jax.ShapeDtypeStruct(s, F32) for s in outs],
        scratch_shapes=[pltpu.VMEM(s, F32) for s in scratch],
        **kw,
        compiler_params=pltpu.CompilerParams(vmem_limit_bytes=limit * 1024 * 1024),
    )


def to_both(up_value, down_value):
    size = lax.axis_size("space")
    up = [(i, (i + 1) % size) for i in range(size)]
    down = [(j, i) for i, j in up]
    return lax.ppermute(up_value, "space", up), lax.ppermute(down_value, "space", down)


NEAR = [
    [(4 * b + k) * 4 + y for k in order for y in (2, 3, 0, 1)]
    for b, order in enumerate(((1, 0, 2, 3), (2, 3, 1, 0), (1, 0, 2, 3), (1, 0, 2, 3)))
]
FAR = [[NEAR[b][p] for b in (2, 3, 0, 1)] for p in range(16)]


def all_sum(part):
    piece = part.reshape(16, SLOTS // 2, 128)
    piece = lax.all_to_all(piece, "vel", 0, 0, tiled=True, axis_index_groups=NEAR)
    mine = jnp.sum(piece, 0)
    piece = jnp.broadcast_to(mine[None], (4,) + mine.shape)
    piece = lax.all_to_all(piece, "vel", 0, 0, tiled=True, axis_index_groups=FAR)
    mine = jnp.sum(piece, 0)
    piece = jnp.broadcast_to(mine[None], (16,) + mine.shape)
    piece = lax.all_to_all(piece, "vel", 0, 0, tiled=True, axis_index_groups=NEAR)
    return piece.reshape(SLOTS, 8, 128)


def per_device(distribution, rate_class, wall):
    block, edges, small = (256, 8, 128), (16, 8, 128), (22, 8, 128)
    part, last, first, inner_last, inner_first = kernel_call(
        moments_kernel, [(SLOTS, 8, 128)] + [edges] * 4, [(25, 8, 128), (2, 15, 8, 128)]
    )(distribution)
    sums = all_sum(part)
    prev_sums, next_sums = to_both(
        jnp.concatenate([sums[:12], last]), jnp.concatenate([sums[6:18], first])
    )
    moments, extra, to_next, to_prev, cell = kernel_call(
        first_kernel, [(13, 8, 128), (5, 8, 128), small, small, (9, 8, 128)], []
    )(sums, prev_sums, next_sums, rate_class, wall, last, first, inner_last, inner_first)
    prev, following = to_both(to_next, to_prev)
    (moved_field,) = kernel_call(field_kernel, [block], [(3, 32, 8, 128)])(
        cell, distribution, prev_sums, next_sums
    )
    whole = pl.BlockSpec(memory_space=pltpu.VMEM)
    field, state = kernel_call(
        second_kernel,
        [block, (5, 8, 128)],
        [(3, 32, 8, 128), (9, 8, 128)],
        grid=(2,),
        in_specs=[whole] * 7,
        out_specs=[
            pl.BlockSpec((128, 8, 128), lambda i: (i, 0, 0)),
            pl.BlockSpec((5, 8, 128), lambda i: (0, 0, 0)),
        ],
    )(
        moments, extra, prev, following, rate_class, wall, moved_field
    )
    return field, state


def solution(mesh):
    return jax.shard_map(
        per_device,
        mesh=mesh,
        in_specs=(P("vel", "space", None), P("space", None), P("space", None)),
        out_specs=(P("vel", "space", None), P(None, "space", None)),
        check_vma=False,
    )
```

```python
import jax
import jax.numpy as jnp
import numpy as np
from jax import lax
from jax.experimental import pallas as pl
from jax.experimental.pallas import tpu as pltpu
from jax.sharding import PartitionSpec as P

VX, VY, VZ = 32, 32, 16
SWEEPS = 4
EDGE = 5.0
STEP = 0.1
HX = 2.0 * EDGE / VX
HY = 2.0 * EDGE / VY
HZ = 2.0 * EDGE / VZ
QUAD = float(HX * HY * HZ / (2.0 * np.pi) ** 1.5)
SPEED_X = [-EDGE + (i + 0.5) * HX for i in range(VX)]
SPEED_Y = [-EDGE + (i + 0.5) * HY for i in range(VY)]
SPEED_Z = [-EDGE + (i + 0.5) * HZ for i in range(VZ)]
F32 = jnp.float32

MOMENTS = [
    ((0, 0, 0),),
    ((1, 0, 0),),
    ((0, 1, 0),),
    ((0, 0, 1),),
    ((2, 0, 0), (0, 2, 0), (0, 0, 2)),
    ((2, 0, 0),),
    ((0, 2, 0),),
    ((1, 1, 0),),
    ((1, 0, 1),),
    ((0, 1, 1),),
    ((3, 0, 0), (1, 2, 0), (1, 0, 2)),
    ((2, 1, 0), (0, 3, 0), (0, 1, 2)),
    ((2, 0, 1), (0, 2, 1), (0, 0, 3)),
]


def times(moment, axis):
    return tuple(tuple(p + (d == axis) for d, p in enumerate(m)) for m in moment)


def key_of(moment):
    return tuple(sorted(moment))


PLAIN = []
for _m in MOMENTS + [times(m, 0) for m in MOMENTS] + [times(m, 1) for m in MOMENTS]:
    if key_of(_m) not in PLAIN:
        PLAIN.append(key_of(_m))
AT = {k: i for i, k in enumerate(PLAIN)}
ABS_X = len(PLAIN)
ABS_Y = ABS_X + 13
SETS = ABS_Y + 13
SLOTS = 64
FIRST_SET = 7


def slot_of(i):
    return FIRST_SET + i if i < 5 else FIRST_SET + 6 + i


def row_up(i):
    return (i // 8, i % 8) if i < 48 else (6, i - 48)


def row_down(i):
    return (12 + i // 8, i % 8) if i < 48 else (6, i - 45)


def rows_of():
    return lax.broadcasted_iota(jnp.int32, (8, 128), 0)


def added_up(terms):
    total = None
    for t in terms:
        total = t if total is None else total + t
    return total


def place():
    vel = lax.axis_index("vel")
    return lax.rem(vel, 4), lax.div(vel, 4)


def local_y(block, iy):
    return -EDGE + ((block * 8 + iy).astype(F32) + 0.5) * HY


def local_z(iz):
    return -EDGE + (iz.astype(F32) + 0.5) * HZ


def moved(value, ix, courant_y, shift, row, before, after):
    courant_x = STEP * abs(SPEED_X[ix])
    if SPEED_X[ix] > 0:
        beside = jnp.where(row == 0, before, pltpu.roll(value, 1, 0))
    else:
        beside = jnp.where(row == 7, after, pltpu.roll(value, 7, 0))
    along = pltpu.roll(value, shift, 1)
    return ((1.0 - courant_x) - courant_y) * value + courant_x * beside + courant_y * along


def powers():
    full = [(a, b) for a in range(5) for b in range(5 - a)]
    odd = [(a, b) for a in range(1, 5) for b in range(5 - a)]
    return {p: i for i, p in enumerate(full)}, {p: 15 + i for i, p in enumerate(odd)}


def moments_kernel(
    f_hbm, part_ref, to_next_ref, to_prev_ref, inner_last_ref, inner_first_ref,
    field, acc, edge_acc, sems,
):
    block, iz = place()
    row = rows_of()
    shift = jnp.where(block >= 2, 1, 127)
    full_at, odd_at = powers()

    def chunk(i):
        rows = pl.ds(i * 64, 64)
        return pltpu.make_async_copy(f_hbm.at[rows], field.at[rows], sems.at[i])

    for i in range(4):
        chunk(i).start()
    acc[...] = jnp.zeros_like(acc)
    edge_acc[...] = jnp.zeros_like(edge_acc)
    lane_x = (row.astype(F32) + 0.5) * HX

    def over_y(iy, carry):
        @pl.when(lax.rem(iy, 2) == 0)
        def _():
            chunk(lax.div(iy, 2)).wait()

        sy = local_y(block, iy)
        courant_y = STEP * jnp.abs(sy)
        sums = [[None] * 5, [None] * 5]
        for ix in range(VX):
            half = 1 if SPEED_X[ix] > 0 else 0
            k = ix % 16
            raw = field[iy * 32 + ix]
            at = (2 * iy + k // 8, slice(k % 8, k % 8 + 1), slice(None))
            if half:
                to_next_ref[at] = raw[7:8, :]
                inner_last_ref[at] = raw[6:7, :]
            else:
                to_prev_ref[at] = raw[0:1, :]
                inner_first_ref[at] = raw[1:2, :]
            value = moved(raw, ix, courant_y, shift, row, 0.0, 0.0)
            for a in range(5):
                term = value if a == 0 else (SPEED_X[ix] ** a) * value
                sums[half][a] = term if sums[half][a] is None else sums[half][a] + term
        power = [1.0, sy, sy * sy, sy * sy * sy, sy * sy * sy * sy]
        full = [sums[1][a] + sums[0][a] for a in range(5)]
        odd = [sums[1][a] - sums[0][a] for a in range(5)]
        for (a, b), n in full_at.items():
            acc[n] = acc[n] + power[b] * full[a]
        for (a, b), n in odd_at.items():
            acc[n] = acc[n] + power[b] * odd[a]
        for side, ref, base in ((0, to_next_ref, 0.0), (1, to_prev_ref, -EDGE)):
            edge = [None] * 5
            for j in range(2):
                sx = lane_x + (base + 8 * HX * j)
                term = (STEP * jnp.abs(sx)) * ref[2 * iy + j]
                for a in range(5):
                    term = term if a == 0 else sx * term
                    edge[a] = term if edge[a] is None else edge[a] + term
            for (a, b), n in full_at.items():
                edge_acc[side, n] = edge_acc[side, n] + power[b] * edge[a]
        return carry

    lax.fori_loop(0, 8, over_y, 0)
    sz = local_z(iz)
    zs = [QUAD * jnp.ones((), F32), QUAD * sz, QUAD * sz * sz, QUAD * sz * sz * sz]
    sign = jnp.where(block >= 2, 1.0, -1.0).astype(F32)
    zy = [sign * z for z in zs]

    def all_sets(full, odd):
        out = [added_up(zs[c] * full(a, b) for a, b, c in monos) for monos in PLAIN]
        out += [added_up(zs[c] * odd(a + 1, b) for a, b, c in monos) for monos in MOMENTS]
        out += [added_up(zy[c] * full(a, b + 1) for a, b, c in monos) for monos in MOMENTS]
        return out

    for i, v in enumerate(all_sets(lambda a, b: acc[full_at[a, b]], lambda a, b: acc[odd_at[a, b]])):
        part_ref[slot_of(i)] = v
    part_ref[6] = jnp.zeros((8, 128), F32)
    for side, where in ((0, row_up), (1, row_down)):
        lines = {p: jnp.sum(edge_acc[side, n], axis=0, keepdims=True) for p, n in full_at.items()}
        factor = -1.0 if side else 1.0
        for i, v in enumerate(
            all_sets(lambda a, b: lines[a, b], lambda a, b: factor * lines[a, b])
        ):
            slot, r = where(i)
            part_ref[slot, r : r + 1, :] = v


def diffuse(own_source, far_source, row):
    own, far = own_source, far_source
    for _ in range(SWEEPS):
        own_down, far_down = pltpu.roll(own, 1, 0), pltpu.roll(far, 1, 0)
        own_up, far_up = pltpu.roll(own, 7, 0), pltpu.roll(far, 7, 0)
        new_own = (
            jnp.where(row == 0, far_down, own_down)
            + jnp.where(row == 7, far_up, own_up)
            + pltpu.roll(own, 1, 1)
            + pltpu.roll(own, 127, 1)
        )
        new_far = (
            jnp.where(row == 0, own_down, far_down)
            + jnp.where(row == 7, own_up, far_up)
            + pltpu.roll(far, 1, 1)
            + pltpu.roll(far, 127, 1)
        )
        own = (own_source + new_own) * 0.2
        far = (far_source + new_far) * 0.2
    return own


def heat_flux(m):
    inv = 1.0 / m[0]
    u = [m[1] * inv, m[2] * inv, m[3] * inv]
    p_zz = m[4] - m[5] - m[6]
    p = [[m[5], m[7], m[8]], [m[7], m[6], m[9]], [m[8], m[9], p_zz]]
    sq = u[0] * u[0] + u[1] * u[1] + u[2] * u[2]
    mass_sq = 2.0 * m[0] * sq
    return [
        0.5
        * (
            m[10 + i]
            - 2.0 * (u[0] * p[i][0] + u[1] * p[i][1] + u[2] * p[i][2])
            + u[i] * (mass_sq - m[4])
        )
        for i in range(3)
    ]


def cell_state(state, moments, rate_class, wall):
    density = state[0]
    inv = 1.0 / density
    u = [state[i] * inv for i in (1, 2, 3)]
    temperature = (2.0 * state[4] * inv - (u[0] * u[0] + u[1] * u[1] + u[2] * u[2])) * (1.0 / 3.0)
    heat = heat_flux(moments)
    frequency = 0.5 * jnp.exp2(rate_class.astype(F32))
    power = jnp.exp((1.0 - 0.81) * jnp.log(temperature))
    keep = jnp.exp(-STEP * frequency * density * power)
    inv_t = 1.0 / temperature
    rate = 1.0 - keep
    skew = ((1.0 - 2.0 / 3.0) / 5.0) * inv * inv_t * inv_t
    amplitude = rate * density * inv_t * lax.rsqrt(temperature)
    solid = wall > 0
    keep = jnp.where(solid, 0.0, keep)
    amplitude = jnp.where(solid, density, amplitude)
    inv_t = jnp.where(solid, 1.0, inv_t)
    u = [jnp.where(solid, 0.0, c) for c in u]
    heat = [jnp.where(solid, 0.0, skew * h) for h in heat]
    return keep, amplitude, inv_t, u, heat


def apply_added(sy, sz, cell):
    _, amplitude, inv_t, u, heat = cell
    dy, dz = sy - u[1], sz - u[2]
    square = (dy * dy + dz * dz) * inv_t
    return amplitude * jnp.exp(-0.5 * square), square - 5.0, dy * heat[1] + dz * heat[2]


def profile_x(cell, profile):
    _, _, inv_t, u, heat = cell
    for ix in range(VX):
        dx = SPEED_X[ix] - u[0]
        square = dx * dx * inv_t
        profile[0, ix] = jnp.exp(-0.5 * square)
        profile[1, ix] = square
        profile[2, ix] = dx * heat[0]


def line_sums(speeds, u, inv_t, top):
    out = [None] * (top + 1)
    for s in speeds:
        d = s - u
        term = jnp.exp(-0.5 * (d * d * inv_t))
        for b in range(top + 1):
            term = term if b == 0 else d * term
            out[b] = term if out[b] is None else out[b] + term
    return out


def mixed(raw, u, top):
    columns = [raw]
    for _ in range(top):
        last = columns[-1]
        columns.append([u * last[b] + last[b + 1] for b in range(len(last) - 1)])
    return [[column[b] for column in columns] for b in range(4)]


def added_moments(cell):
    _, amplitude, inv_t, u, heat = cell
    scale = amplitude * QUAD
    half = VX // 2
    x_up = mixed(line_sums(SPEED_X[half:], u[0], inv_t, 7), u[0], 4)
    x_dn = mixed(line_sums(SPEED_X[:half], u[0], inv_t, 7), u[0], 4)
    y_up = mixed(line_sums(SPEED_Y[half:], u[1], inv_t, 7), u[1], 4)
    y_dn = mixed(line_sums(SPEED_Y[:half], u[1], inv_t, 7), u[1], 4)
    z_all = mixed([scale * z for z in line_sums(SPEED_Z, u[2], inv_t, 6)], u[2], 3)
    x_all = [[p + q for p, q in zip(r, s)] for r, s in zip(x_up, x_dn)]
    y_all = [[p + q for p, q in zip(r, s)] for r, s in zip(y_up, y_dn)]
    gx, gy, gz = heat
    hx, hy, hz = gx * inv_t, gy * inv_t, gz * inv_t

    def whole(xs, ys):
        plane = {}

        def at(a, b):
            if (a, b) not in plane:
                x = [xs[i][a] for i in range(4)]
                y = [ys[i][b] for i in range(4)]
                x0y0 = x[0] * y[0]
                x1y0, x0y1 = x[1] * y[0], x[0] * y[1]
                x2y0, x0y2 = x[2] * y[0], x[0] * y[2]
                p0 = (
                    x0y0
                    + hx * (x[3] * y[0] + x[1] * y[2])
                    + hy * (x[2] * y[1] + x[0] * y[3])
                    - 5.0 * (gx * x1y0 + gy * x0y1)
                )
                p1 = hz * (x2y0 + x0y2) - 5.0 * gz * x0y0
                p2 = hx * x1y0 + hy * x0y1
                p3 = hz * x0y0
                plane[a, b] = (p0, p1, p2, p3)
            return plane[a, b]

        out = []
        for monos in MOMENTS:
            total = None
            for a, b, c in monos:
                p = at(a, b)
                term = (
                    p[0] * z_all[0][c] + p[1] * z_all[1][c] + p[2] * z_all[2][c] + p[3] * z_all[3][c]
                )
                total = term if total is None else total + term
            out.append(total)
        return out

    def weighted(table, factor):
        return [[factor * v for v in line[1:5]] for line in table]

    return (
        whole(x_all, y_all),
        whole(weighted(x_up, STEP), y_all),
        whole(weighted(x_dn, -STEP), y_all),
        whole(x_all, weighted(y_up, STEP)),
        whole(x_all, weighted(y_dn, -STEP)),
    )


def flat(cell):
    keep, amplitude, inv_t, u, heat = cell
    return [keep, amplitude, inv_t, *u, *heat]


def cell_of(v):
    return v[0], v[1], v[2], v[3:6], v[6:9]


def keep_out(cell, ref):
    for i, v in enumerate(flat(cell)):
        ref[i] = v


def first_kernel(
    q_ref, prev_ref, next_ref, class_ref, wall_ref, last_ref, first_ref, inner_last_ref, inner_first_ref,
    m_ref, add_ref, to_next_ref, to_prev_ref, cell_ref,
):
    block, iz = place()
    row = rows_of()
    shift = jnp.where(block >= 2, 1, 127)

    def line(ref, first, at):
        return ref[at[0] - first, at[1] : at[1] + 1, :]

    def whole_set(i):
        above, below = line(prev_ref, 0, row_up(i)), line(next_ref, 6, row_down(i))
        return q_ref[slot_of(i)] + jnp.where(row == 0, above, jnp.where(row == 7, below, 0.0))

    sets = [whole_set(i) for i in range(SETS)]
    scale = [1.0, 1.0, 1.0, 1.0, 0.5]
    state = []
    for k in range(5):
        far = jnp.where(row < 4, next_ref[1 + k], prev_ref[FIRST_SET + k])
        up, down = line(q_ref, 0, row_up(k)), line(q_ref, 0, row_down(k))
        far = far + jnp.where(row == 0, up, jnp.where(row == 7, down, 0.0))
        state.append(diffuse(scale[k] * sets[k], scale[k] * far, row))
    cell = cell_state(state, sets[:13], class_ref[...], wall_ref[...])
    keep = cell[0]
    keep_out(cell, cell_ref)
    sz = local_z(iz)

    for r, base_x, outer, inner, out in (
        (7, 0.0, last_ref, inner_last_ref, to_next_ref),
        (0, -EDGE, first_ref, inner_first_ref, to_prev_ref),
    ):
        line_cell = cell_of([jnp.broadcast_to(v[r : r + 1, :], (8, 128)) for v in flat(cell)])
        parts = []
        for j in range(2):
            sx = (row.astype(F32) + 0.5) * HX + (base_x + 8 * HX * j)
            dx = sx - line_cell[3][0]
            square = dx * dx * line_cell[2]
            parts.append(
                (STEP * jnp.abs(sx), jnp.exp(-0.5 * square), square, dx * line_cell[4][0])
            )

        def edge_y(iy, carry, line_cell=line_cell, parts=parts, outer=outer, inner=inner, out=out):
            sy = local_y(block, iy)
            courant_y = STEP * jnp.abs(sy)
            base, square, flux = apply_added(sy, sz, line_cell)
            for j, (courant_x, bell, square_x, flux_x) in enumerate(parts):
                value = outer[2 * iy + j]
                value = (
                    ((1.0 - courant_x) - courant_y) * value
                    + courant_x * inner[2 * iy + j]
                    + courant_y * pltpu.roll(value, shift, 1)
                )
                added = (base * bell) * (1.0 + (flux + flux_x) * (square + square_x))
                out[6 + 2 * iy + j] = line_cell[0] * value + added
            return carry

        lax.fori_loop(0, 8, edge_y, 0, unroll=True)

    g_all, g_xu, g_xd, g_yu, g_yd = added_moments(cell)
    part = 0.5 * STEP * keep
    for k, monos in enumerate(MOMENTS):
        sx_k, ax_k = sets[AT[key_of(times(monos, 0))]], sets[ABS_X + k]
        sy_k, ay_k = sets[AT[key_of(times(monos, 1))]], sets[ABS_Y + k]
        x_up = part * (ax_k + sx_k) + g_xu[k]
        x_dn = part * (ax_k - sx_k) + g_xd[k]
        y_up = part * (ay_k + sy_k) + g_yu[k]
        y_dn = part * (ay_k - sy_k) + g_yd[k]
        from_up, from_dn = pltpu.roll(x_up, 1, 0), pltpu.roll(x_dn, 7, 0)
        total = (
            (keep * sets[k] + g_all[k] - x_up - x_dn - y_up - y_dn)
            + jnp.where(row == 0, 0.0, from_up)
            + jnp.where(row == 7, 0.0, from_dn)
            + pltpu.roll(y_up, 1, 1)
            + pltpu.roll(y_dn, 127, 1)
        )
        m_ref[k] = total
        if k < 5:
            add_ref[k] = jnp.where(row == 0, from_up, jnp.where(row == 7, from_dn, 0.0))
            to_next_ref[k] = jnp.where(row == 0, from_up, total)
            to_prev_ref[k] = jnp.where(row == 7, from_dn, total)
        else:
            to_next_ref[5, k - 5 : k - 4, :] = x_up[7:8, :]
            to_prev_ref[5, k - 5 : k - 4, :] = x_dn[0:1, :]


def field_kernel(cell_ref, f_ref, before_ref, after_ref, t_ref, profile):
    block, iz = place()
    row = rows_of()
    shift = jnp.where(block >= 2, 1, 127)
    cell = cell_of([cell_ref[i] for i in range(9)])
    keep = cell[0]
    profile_x(cell, profile)
    sz = local_z(iz)

    def over_y(iy, carry):
        sy = local_y(block, iy)
        courant_y = STEP * jnp.abs(sy)
        base, square, flux = apply_added(sy, sz, cell)
        for ix in range(VX):
            k = ix % 16
            edge = (before_ref if SPEED_X[ix] > 0 else after_ref)[
                12 + 2 * iy + k // 8, k % 8 : k % 8 + 1, :
            ]
            value = moved(f_ref[iy * 32 + ix], ix, courant_y, shift, row, edge, edge)
            added = (base * profile[0, ix]) * (
                1.0 + (flux + profile[2, ix]) * (square + profile[1, ix])
            )
            value = keep * value + added
            t_ref[iy * 32 + ix] = moved(value, ix, courant_y, shift, row, 0.0, 0.0)
        return carry

    lax.fori_loop(0, 8, over_y, 0)


def second_kernel(
    m_ref, add_ref, prev_ref, next_ref, class_ref, wall_ref, t_ref,
    out_ref, state_ref, profile, cell_ref,
):
    block, iz = place()
    row = rows_of()
    step = pl.program_id(0)

    @pl.when(step == 0)
    def _():
        moments = []
        for k in range(13):
            if k < 5:
                before, after = prev_ref[k], next_ref[k]
            else:
                before, after = prev_ref[5, k - 5 : k - 4, :], next_ref[5, k - 5 : k - 4, :]
            moments.append(
                m_ref[k] + jnp.where(row == 0, before, jnp.where(row == 7, after, 0.0))
            )
        scale = [1.0, 1.0, 1.0, 1.0, 0.5]
        state = []
        for k in range(5):
            far = jnp.where(row < 4, next_ref[k], prev_ref[k]) + add_ref[k]
            state.append(diffuse(scale[k] * moments[k], scale[k] * far, row))
            state_ref[k] = state[k]
        cell = cell_state(state, moments, class_ref[...], wall_ref[...])
        profile_x(cell, profile)
        keep_out(cell, cell_ref)

    cell = cell_of([cell_ref[i] for i in range(9)])
    keep = cell[0]
    sz = local_z(iz)

    def over_y(iy, carry):
        sy = local_y(block, iy)
        base, square, flux = apply_added(sy, sz, cell)
        for ix in range(VX):
            k = ix % 16
            edge = (prev_ref if SPEED_X[ix] > 0 else next_ref)[
                6 + 2 * iy + k // 8, k % 8 : k % 8 + 1, :
            ]
            courant_x = STEP * abs(SPEED_X[ix])
            here = row == (0 if SPEED_X[ix] > 0 else 7)
            value = t_ref[iy * 32 + ix] + jnp.where(here, courant_x * edge, 0.0)
            added = (base * profile[0, ix]) * (
                1.0 + (flux + profile[2, ix]) * (square + profile[1, ix])
            )
            out_ref[(iy - 4 * step) * 32 + ix] = keep * value + added
        return carry

    lax.fori_loop(4 * step, 4 * (step + 1), over_y, 0)


def kernel_call(body, outs, scratch, limit=32, **kw):
    return pl.pallas_call(
        body,
        out_shape=[jax.ShapeDtypeStruct(s, F32) for s in outs],
        scratch_shapes=[pltpu.VMEM(s, F32) if isinstance(s, tuple) else s for s in scratch],
        **kw,
        compiler_params=pltpu.CompilerParams(vmem_limit_bytes=limit * 1024 * 1024),
    )


def to_both(up_value, down_value):
    size = lax.axis_size("space")
    up = [(i, (i + 1) % size) for i in range(size)]
    down = [(j, i) for i, j in up]
    return lax.ppermute(up_value, "space", up), lax.ppermute(down_value, "space", down)


NEAR = [
    [(4 * b + k) * 4 + y for k in order for y in (2, 3, 1, 0)]
    for b, order in enumerate(((1, 0, 2, 3), (2, 3, 1, 0), (1, 0, 2, 3), (1, 0, 2, 3)))
]
FAR = [[NEAR[b][p] for b in (2, 0, 1, 3)] for p in range(16)]


def all_sum(part):
    piece = part.reshape(16, SLOTS // 2, 128)
    piece = lax.all_to_all(piece, "vel", 0, 0, tiled=True, axis_index_groups=NEAR)
    mine = jnp.sum(piece, 0)
    piece = jnp.broadcast_to(mine[None], (4,) + mine.shape)
    piece = lax.all_to_all(piece, "vel", 0, 0, tiled=True, axis_index_groups=FAR)
    mine = jnp.sum(piece, 0)
    piece = jnp.broadcast_to(mine[None], (16,) + mine.shape)
    piece = lax.all_to_all(piece, "vel", 0, 0, tiled=True, axis_index_groups=NEAR)
    return piece.reshape(SLOTS, 8, 128)


def per_device(distribution, rate_class, wall):
    block, edges, small = (256, 8, 128), (16, 8, 128), (22, 8, 128)
    part, last, first, inner_last, inner_first = kernel_call(
        moments_kernel,
        [(SLOTS, 8, 128)] + [edges] * 4,
        [block, (25, 8, 128), (2, 15, 8, 128), pltpu.SemaphoreType.DMA((4,))],
        limit=53,
        in_specs=[pl.BlockSpec(memory_space=pltpu.HBM)],
    )(distribution)
    sums = all_sum(part)
    prev_sums, next_sums = to_both(
        jnp.concatenate([sums[:12], last]), jnp.concatenate([sums[6:18], first])
    )
    moments, extra, to_next, to_prev, cell = kernel_call(
        first_kernel, [(13, 8, 128), (5, 8, 128), small, small, (9, 8, 128)], []
    )(sums, prev_sums, next_sums, rate_class, wall, last, first, inner_last, inner_first)
    prev, following = to_both(to_next, to_prev)
    (moved_field,) = kernel_call(field_kernel, [block], [(3, 32, 8, 128)])(
        cell, distribution, prev_sums, next_sums
    )
    whole = pl.BlockSpec(memory_space=pltpu.VMEM)
    field, state = kernel_call(
        second_kernel,
        [block, (5, 8, 128)],
        [(3, 32, 8, 128), (9, 8, 128)],
        grid=(2,),
        in_specs=[whole] * 7,
        out_specs=[
            pl.BlockSpec((128, 8, 128), lambda i: (i, 0, 0)),
            pl.BlockSpec((5, 8, 128), lambda i: (0, 0, 0)),
        ],
    )(
        moments, extra, prev, following, rate_class, wall, moved_field
    )
    return field, state


def solution(mesh):
    return jax.shard_map(
        per_device,
        mesh=mesh,
        in_specs=(P("vel", "space", None), P("space", None), P("space", None)),
        out_specs=(P("vel", "space", None), P(None, "space", None)),
        check_vma=False,
    )
```

```python
import math

import jax
import jax.numpy as jnp
import numpy as np
from jax import lax
from jax.experimental import pallas as pl
from jax.experimental.pallas import tpu as pltpu
from jax.sharding import PartitionSpec as P

VX, VY, VZ = 32, 32, 16
SWEEPS = 4
EDGE = 5.0
STEP = 0.1
HX = 2.0 * EDGE / VX
HY = 2.0 * EDGE / VY
HZ = 2.0 * EDGE / VZ
QUAD = float(HX * HY * HZ / (2.0 * np.pi) ** 1.5)
SPEED_X = [-EDGE + (i + 0.5) * HX for i in range(VX)]
SPEED_Y = [-EDGE + (i + 0.5) * HY for i in range(VY)]
SPEED_Z = [-EDGE + (i + 0.5) * HZ for i in range(VZ)]
F32 = jnp.float32

MOMENTS = [
    ((0, 0, 0),),
    ((1, 0, 0),),
    ((0, 1, 0),),
    ((0, 0, 1),),
    ((2, 0, 0), (0, 2, 0), (0, 0, 2)),
    ((2, 0, 0),),
    ((0, 2, 0),),
    ((1, 1, 0),),
    ((1, 0, 1),),
    ((0, 1, 1),),
    ((3, 0, 0), (1, 2, 0), (1, 0, 2)),
    ((2, 1, 0), (0, 3, 0), (0, 1, 2)),
    ((2, 0, 1), (0, 2, 1), (0, 0, 3)),
]


def times(moment, axis):
    return tuple(tuple(p + (d == axis) for d, p in enumerate(m)) for m in moment)


def key_of(moment):
    return tuple(sorted(moment))


PLAIN = []
for _m in MOMENTS + [times(m, 0) for m in MOMENTS] + [times(m, 1) for m in MOMENTS]:
    if key_of(_m) not in PLAIN:
        PLAIN.append(key_of(_m))
AT = {k: i for i, k in enumerate(PLAIN)}
ABS_X = len(PLAIN)
ABS_Y = ABS_X + 13
SETS = ABS_Y + 13
SLOTS = 64
FIRST_SET = 7


def slot_of(i):
    return FIRST_SET + i if i < 5 else FIRST_SET + 6 + i


def row_up(i):
    return (i // 8, i % 8) if i < 48 else (6, i - 48)


def row_down(i):
    return (12 + i // 8, i % 8) if i < 48 else (6, i - 45)


def rows_of():
    return lax.broadcasted_iota(jnp.int32, (8, 128), 0)


def added_up(terms):
    total = None
    for t in terms:
        total = t if total is None else total + t
    return total


def place():
    vel = lax.axis_index("vel")
    return lax.rem(vel, 4), lax.div(vel, 4)


def local_y(block, iy):
    return -EDGE + ((block * 8 + iy).astype(F32) + 0.5) * HY


def local_z(iz):
    return -EDGE + (iz.astype(F32) + 0.5) * HZ


def moved(value, ix, courant_y, shift, row, before, after):
    courant_x = STEP * abs(SPEED_X[ix])
    if SPEED_X[ix] > 0:
        beside = jnp.where(row == 0, before, pltpu.roll(value, 1, 0))
    else:
        beside = jnp.where(row == 7, after, pltpu.roll(value, 7, 0))
    along = pltpu.roll(value, shift, 1)
    return ((1.0 - courant_x) - courant_y) * value + courant_x * beside + courant_y * along


def powers():
    full = [(a, b) for a in range(5) for b in range(5 - a)]
    odd = [(a, b) for a in range(1, 5) for b in range(5 - a)]
    return {p: i for i, p in enumerate(full)}, {p: 15 + i for i, p in enumerate(odd)}


def moments_kernel(
    f_hbm, part_ref, to_next_ref, to_prev_ref, inner_last_ref, inner_first_ref,
    field, acc, edge_acc, sems,
):
    block, iz = place()
    row = rows_of()
    shift = jnp.where(block >= 2, 1, 127)
    full_at, odd_at = powers()

    def chunk(i):
        rows = pl.ds(i * 64, 64)
        return pltpu.make_async_copy(f_hbm.at[rows], field.at[rows], sems.at[i])

    for i in range(4):
        chunk(i).start()
    acc[...] = jnp.zeros_like(acc)
    edge_acc[...] = jnp.zeros_like(edge_acc)
    lane_x = (row.astype(F32) + 0.5) * HX

    def over_y(iy, carry):
        @pl.when(lax.rem(iy, 2) == 0)
        def _():
            chunk(lax.div(iy, 2)).wait()

        sy = local_y(block, iy)
        courant_y = STEP * jnp.abs(sy)
        sums = [[None] * 5, [None] * 5]
        for ix in range(VX):
            half = 1 if SPEED_X[ix] > 0 else 0
            k = ix % 16
            raw = field[iy * 32 + ix]
            at = (2 * iy + k // 8, slice(k % 8, k % 8 + 1), slice(None))
            if half:
                to_next_ref[at] = raw[7:8, :]
                inner_last_ref[at] = raw[6:7, :]
            else:
                to_prev_ref[at] = raw[0:1, :]
                inner_first_ref[at] = raw[1:2, :]
            value = moved(raw, ix, courant_y, shift, row, 0.0, 0.0)
            for a in range(5):
                term = value if a == 0 else (SPEED_X[ix] ** a) * value
                sums[half][a] = term if sums[half][a] is None else sums[half][a] + term
        power = [1.0, sy, sy * sy, sy * sy * sy, sy * sy * sy * sy]
        full = [sums[1][a] + sums[0][a] for a in range(5)]
        odd = [sums[1][a] - sums[0][a] for a in range(5)]
        for (a, b), n in full_at.items():
            acc[n] = acc[n] + power[b] * full[a]
        for (a, b), n in odd_at.items():
            acc[n] = acc[n] + power[b] * odd[a]
        for side, ref, base in ((0, to_next_ref, 0.0), (1, to_prev_ref, -EDGE)):
            edge = [None] * 5
            for j in range(2):
                sx = lane_x + (base + 8 * HX * j)
                term = (STEP * jnp.abs(sx)) * ref[2 * iy + j]
                for a in range(5):
                    term = term if a == 0 else sx * term
                    edge[a] = term if edge[a] is None else edge[a] + term
            for (a, b), n in full_at.items():
                edge_acc[side, n] = edge_acc[side, n] + power[b] * edge[a]
        return carry

    lax.fori_loop(0, 8, over_y, 0)
    sz = local_z(iz)
    zs = [QUAD * jnp.ones((), F32), QUAD * sz, QUAD * sz * sz, QUAD * sz * sz * sz]
    sign = jnp.where(block >= 2, 1.0, -1.0).astype(F32)
    zy = [sign * z for z in zs]

    def all_sets(full, odd):
        out = [added_up(zs[c] * full(a, b) for a, b, c in monos) for monos in PLAIN]
        out += [added_up(zs[c] * odd(a + 1, b) for a, b, c in monos) for monos in MOMENTS]
        out += [added_up(zy[c] * full(a, b + 1) for a, b, c in monos) for monos in MOMENTS]
        return out

    for i, v in enumerate(all_sets(lambda a, b: acc[full_at[a, b]], lambda a, b: acc[odd_at[a, b]])):
        part_ref[slot_of(i)] = v
    part_ref[6] = jnp.zeros((8, 128), F32)
    for side, where in ((0, row_up), (1, row_down)):
        lines = {p: jnp.sum(edge_acc[side, n], axis=0, keepdims=True) for p, n in full_at.items()}
        factor = -1.0 if side else 1.0
        for i, v in enumerate(
            all_sets(lambda a, b: lines[a, b], lambda a, b: factor * lines[a, b])
        ):
            slot, r = where(i)
            part_ref[slot, r : r + 1, :] = v


def diffuse(own_source, far_source, row):
    weight = [0.2 ** (m + 1) for m in range(SWEEPS)] + [0.2**SWEEPS]

    def along(x):
        r = [None] + [pltpu.roll(x, d, 1) + pltpu.roll(x, 128 - d, 1) for d in (1, 2, 3, 4)]
        h = [x, r[1], r[2] + 2.0 * x, r[3] + 3.0 * r[1], r[4] + 4.0 * r[2] + 6.0 * x]
        return [
            added_up((weight[i + j] * math.comb(i + j, i)) * h[j] for j in range(5 - i))
            for i in range(5)
        ]

    own_terms, far_terms = along(own_source), along(far_source)
    own, far = own_terms[4], far_terms[4]
    for i in (3, 2, 1, 0):
        own_down, far_down = pltpu.roll(own, 1, 0), pltpu.roll(far, 1, 0)
        own_up, far_up = pltpu.roll(own, 7, 0), pltpu.roll(far, 7, 0)
        own = (
            own_terms[i]
            + jnp.where(row == 0, far_down, own_down)
            + jnp.where(row == 7, far_up, own_up)
        )
        if i:
            far = (
                far_terms[i]
                + jnp.where(row == 0, own_down, far_down)
                + jnp.where(row == 7, own_up, far_up)
            )
    return own


def heat_flux(m):
    inv = 1.0 / m[0]
    u = [m[1] * inv, m[2] * inv, m[3] * inv]
    p_zz = m[4] - m[5] - m[6]
    p = [[m[5], m[7], m[8]], [m[7], m[6], m[9]], [m[8], m[9], p_zz]]
    sq = u[0] * u[0] + u[1] * u[1] + u[2] * u[2]
    mass_sq = 2.0 * m[0] * sq
    return [
        0.5
        * (
            m[10 + i]
            - 2.0 * (u[0] * p[i][0] + u[1] * p[i][1] + u[2] * p[i][2])
            + u[i] * (mass_sq - m[4])
        )
        for i in range(3)
    ]


def cell_state(state, moments, rate_class, wall):
    density = state[0]
    inv = 1.0 / density
    u = [state[i] * inv for i in (1, 2, 3)]
    temperature = (2.0 * state[4] * inv - (u[0] * u[0] + u[1] * u[1] + u[2] * u[2])) * (1.0 / 3.0)
    heat = heat_flux(moments)
    frequency = 0.5 * jnp.exp2(rate_class.astype(F32))
    power = jnp.exp((1.0 - 0.81) * jnp.log(temperature))
    keep = jnp.exp(-STEP * frequency * density * power)
    inv_t = 1.0 / temperature
    rate = 1.0 - keep
    skew = ((1.0 - 2.0 / 3.0) / 5.0) * inv * inv_t * inv_t
    amplitude = rate * density * inv_t * lax.rsqrt(temperature)
    solid = wall > 0
    keep = jnp.where(solid, 0.0, keep)
    amplitude = jnp.where(solid, density, amplitude)
    inv_t = jnp.where(solid, 1.0, inv_t)
    u = [jnp.where(solid, 0.0, c) for c in u]
    heat = [jnp.where(solid, 0.0, skew * h) for h in heat]
    return keep, amplitude, inv_t, u, heat


def apply_added(sy, sz, cell):
    _, amplitude, inv_t, u, heat = cell
    dy, dz = sy - u[1], sz - u[2]
    square = (dy * dy + dz * dz) * inv_t
    return amplitude * jnp.exp(-0.5 * square), square - 5.0, dy * heat[1] + dz * heat[2]


def profile_x(cell, profile):
    _, _, inv_t, u, heat = cell
    for ix in range(VX):
        dx = SPEED_X[ix] - u[0]
        square = dx * dx * inv_t
        profile[0, ix] = jnp.exp(-0.5 * square)
        profile[1, ix] = square
        profile[2, ix] = dx * heat[0]


def line_sums(speeds, u, inv_t, top):
    out = [None] * (top + 1)
    for s in speeds:
        d = s - u
        term = jnp.exp(-0.5 * (d * d * inv_t))
        for b in range(top + 1):
            term = term if b == 0 else d * term
            out[b] = term if out[b] is None else out[b] + term
    return out


def mixed(raw, u, top):
    columns = [raw]
    for _ in range(top):
        last = columns[-1]
        columns.append([u * last[b] + last[b + 1] for b in range(len(last) - 1)])
    return [[column[b] for column in columns] for b in range(4)]


def added_moments(cell):
    _, amplitude, inv_t, u, heat = cell
    scale = amplitude * QUAD
    half = VX // 2
    x_up = mixed(line_sums(SPEED_X[half:], u[0], inv_t, 7), u[0], 4)
    x_dn = mixed(line_sums(SPEED_X[:half], u[0], inv_t, 7), u[0], 4)
    y_up = mixed(line_sums(SPEED_Y[half:], u[1], inv_t, 7), u[1], 4)
    y_dn = mixed(line_sums(SPEED_Y[:half], u[1], inv_t, 7), u[1], 4)
    z_all = mixed([scale * z for z in line_sums(SPEED_Z, u[2], inv_t, 6)], u[2], 3)
    x_all = [[p + q for p, q in zip(r, s)] for r, s in zip(x_up, x_dn)]
    y_all = [[p + q for p, q in zip(r, s)] for r, s in zip(y_up, y_dn)]
    gx, gy, gz = heat
    hx, hy, hz = gx * inv_t, gy * inv_t, gz * inv_t

    def whole(xs, ys):
        plane = {}

        def at(a, b):
            if (a, b) not in plane:
                x = [xs[i][a] for i in range(4)]
                y = [ys[i][b] for i in range(4)]
                x0y0 = x[0] * y[0]
                x1y0, x0y1 = x[1] * y[0], x[0] * y[1]
                x2y0, x0y2 = x[2] * y[0], x[0] * y[2]
                p0 = (
                    x0y0
                    + hx * (x[3] * y[0] + x[1] * y[2])
                    + hy * (x[2] * y[1] + x[0] * y[3])
                    - 5.0 * (gx * x1y0 + gy * x0y1)
                )
                p1 = hz * (x2y0 + x0y2) - 5.0 * gz * x0y0
                p2 = hx * x1y0 + hy * x0y1
                p3 = hz * x0y0
                plane[a, b] = (p0, p1, p2, p3)
            return plane[a, b]

        out = []
        for monos in MOMENTS:
            total = None
            for a, b, c in monos:
                p = at(a, b)
                term = (
                    p[0] * z_all[0][c] + p[1] * z_all[1][c] + p[2] * z_all[2][c] + p[3] * z_all[3][c]
                )
                total = term if total is None else total + term
            out.append(total)
        return out

    def weighted(table, factor):
        return [[factor * v for v in line[1:5]] for line in table]

    return (
        whole(x_all, y_all),
        whole(weighted(x_up, STEP), y_all),
        whole(weighted(x_dn, -STEP), y_all),
        whole(x_all, weighted(y_up, STEP)),
        whole(x_all, weighted(y_dn, -STEP)),
    )


def flat(cell):
    keep, amplitude, inv_t, u, heat = cell
    return [keep, amplitude, inv_t, *u, *heat]


def cell_of(v):
    return v[0], v[1], v[2], v[3:6], v[6:9]


def keep_out(cell, ref):
    for i, v in enumerate(flat(cell)):
        ref[i] = v


def first_kernel(
    q_ref, prev_ref, next_ref, class_ref, wall_ref, last_ref, first_ref, inner_last_ref, inner_first_ref,
    m_ref, add_ref, to_next_ref, to_prev_ref, cell_ref,
):
    block, iz = place()
    row = rows_of()
    shift = jnp.where(block >= 2, 1, 127)

    def line(ref, first, at):
        return ref[at[0] - first, at[1] : at[1] + 1, :]

    def whole_set(i):
        above, below = line(prev_ref, 0, row_up(i)), line(next_ref, 6, row_down(i))
        return q_ref[slot_of(i)] + jnp.where(row == 0, above, jnp.where(row == 7, below, 0.0))

    sets = [whole_set(i) for i in range(SETS)]
    scale = [1.0, 1.0, 1.0, 1.0, 0.5]
    state = []
    for k in range(5):
        far = jnp.where(row < 4, next_ref[1 + k], prev_ref[FIRST_SET + k])
        up, down = line(q_ref, 0, row_up(k)), line(q_ref, 0, row_down(k))
        far = far + jnp.where(row == 0, up, jnp.where(row == 7, down, 0.0))
        state.append(diffuse(scale[k] * sets[k], scale[k] * far, row))
    cell = cell_state(state, sets[:13], class_ref[...], wall_ref[...])
    keep = cell[0]
    keep_out(cell, cell_ref)
    sz = local_z(iz)

    for r, base_x, outer, inner, out in (
        (7, 0.0, last_ref, inner_last_ref, to_next_ref),
        (0, -EDGE, first_ref, inner_first_ref, to_prev_ref),
    ):
        line_cell = cell_of([jnp.broadcast_to(v[r : r + 1, :], (8, 128)) for v in flat(cell)])
        parts = []
        for j in range(2):
            sx = (row.astype(F32) + 0.5) * HX + (base_x + 8 * HX * j)
            dx = sx - line_cell[3][0]
            square = dx * dx * line_cell[2]
            parts.append(
                (STEP * jnp.abs(sx), jnp.exp(-0.5 * square), square, dx * line_cell[4][0])
            )

        def edge_y(iy, carry, line_cell=line_cell, parts=parts, outer=outer, inner=inner, out=out):
            sy = local_y(block, iy)
            courant_y = STEP * jnp.abs(sy)
            base, square, flux = apply_added(sy, sz, line_cell)
            for j, (courant_x, bell, square_x, flux_x) in enumerate(parts):
                value = outer[2 * iy + j]
                value = (
                    ((1.0 - courant_x) - courant_y) * value
                    + courant_x * inner[2 * iy + j]
                    + courant_y * pltpu.roll(value, shift, 1)
                )
                added = (base * bell) * (1.0 + (flux + flux_x) * (square + square_x))
                out[6 + 2 * iy + j] = line_cell[0] * value + added
            return carry

        lax.fori_loop(0, 8, edge_y, 0, unroll=True)

    g_all, g_xu, g_xd, g_yu, g_yd = added_moments(cell)
    part = 0.5 * STEP * keep
    for k, monos in enumerate(MOMENTS):
        sx_k, ax_k = sets[AT[key_of(times(monos, 0))]], sets[ABS_X + k]
        sy_k, ay_k = sets[AT[key_of(times(monos, 1))]], sets[ABS_Y + k]
        x_up = part * (ax_k + sx_k) + g_xu[k]
        x_dn = part * (ax_k - sx_k) + g_xd[k]
        y_up = part * (ay_k + sy_k) + g_yu[k]
        y_dn = part * (ay_k - sy_k) + g_yd[k]
        from_up, from_dn = pltpu.roll(x_up, 1, 0), pltpu.roll(x_dn, 7, 0)
        total = (
            (keep * sets[k] + g_all[k] - x_up - x_dn - y_up - y_dn)
            + jnp.where(row == 0, 0.0, from_up)
            + jnp.where(row == 7, 0.0, from_dn)
            + pltpu.roll(y_up, 1, 1)
            + pltpu.roll(y_dn, 127, 1)
        )
        m_ref[k] = total
        if k < 5:
            add_ref[k] = jnp.where(row == 0, from_up, jnp.where(row == 7, from_dn, 0.0))
            to_next_ref[k] = jnp.where(row == 0, from_up, total)
            to_prev_ref[k] = jnp.where(row == 7, from_dn, total)
        else:
            to_next_ref[5, k - 5 : k - 4, :] = x_up[7:8, :]
            to_prev_ref[5, k - 5 : k - 4, :] = x_dn[0:1, :]


def field_kernel(cell_ref, f_ref, before_ref, after_ref, t_ref, profile):
    block, iz = place()
    row = rows_of()
    shift = jnp.where(block >= 2, 1, 127)
    cell = cell_of([cell_ref[i] for i in range(9)])
    keep = cell[0]
    profile_x(cell, profile)
    sz = local_z(iz)

    def over_y(iy, carry):
        sy = local_y(block, iy)
        courant_y = STEP * jnp.abs(sy)
        base, square, flux = apply_added(sy, sz, cell)
        for ix in range(VX):
            k = ix % 16
            edge = (before_ref if SPEED_X[ix] > 0 else after_ref)[
                12 + 2 * iy + k // 8, k % 8 : k % 8 + 1, :
            ]
            value = moved(f_ref[iy * 32 + ix], ix, courant_y, shift, row, edge, edge)
            added = (base * profile[0, ix]) * (
                1.0 + (flux + profile[2, ix]) * (square + profile[1, ix])
            )
            value = keep * value + added
            t_ref[iy * 32 + ix] = moved(value, ix, courant_y, shift, row, 0.0, 0.0)
        return carry

    lax.fori_loop(0, 8, over_y, 0)


def second_kernel(
    m_ref, add_ref, prev_ref, next_ref, class_ref, wall_ref, t_ref,
    out_ref, state_ref, profile, cell_ref,
):
    block, iz = place()
    row = rows_of()
    step = pl.program_id(0)

    @pl.when(step == 0)
    def _():
        moments = []
        for k in range(13):
            if k < 5:
                before, after = prev_ref[k], next_ref[k]
            else:
                before, after = prev_ref[5, k - 5 : k - 4, :], next_ref[5, k - 5 : k - 4, :]
            moments.append(
                m_ref[k] + jnp.where(row == 0, before, jnp.where(row == 7, after, 0.0))
            )
        scale = [1.0, 1.0, 1.0, 1.0, 0.5]
        state = []
        for k in range(5):
            far = jnp.where(row < 4, next_ref[k], prev_ref[k]) + add_ref[k]
            state.append(diffuse(scale[k] * moments[k], scale[k] * far, row))
            state_ref[k] = state[k]
        cell = cell_state(state, moments, class_ref[...], wall_ref[...])
        profile_x(cell, profile)
        keep_out(cell, cell_ref)

    cell = cell_of([cell_ref[i] for i in range(9)])
    keep = cell[0]
    sz = local_z(iz)

    def over_y(iy, carry):
        sy = local_y(block, iy)
        base, square, flux = apply_added(sy, sz, cell)
        for ix in range(VX):
            k = ix % 16
            edge = (prev_ref if SPEED_X[ix] > 0 else next_ref)[
                6 + 2 * iy + k // 8, k % 8 : k % 8 + 1, :
            ]
            courant_x = STEP * abs(SPEED_X[ix])
            here = row == (0 if SPEED_X[ix] > 0 else 7)
            value = t_ref[iy * 32 + ix] + jnp.where(here, courant_x * edge, 0.0)
            added = (base * profile[0, ix]) * (
                1.0 + (flux + profile[2, ix]) * (square + profile[1, ix])
            )
            out_ref[(iy - 4 * step) * 32 + ix] = keep * value + added
        return carry

    lax.fori_loop(4 * step, 4 * (step + 1), over_y, 0)


def kernel_call(body, outs, scratch, limit=32, **kw):
    return pl.pallas_call(
        body,
        out_shape=[jax.ShapeDtypeStruct(s, F32) for s in outs],
        scratch_shapes=[pltpu.VMEM(s, F32) if isinstance(s, tuple) else s for s in scratch],
        **kw,
        compiler_params=pltpu.CompilerParams(vmem_limit_bytes=limit * 1024 * 1024),
    )


def to_both(up_value, down_value):
    size = lax.axis_size("space")
    up = [(i, (i + 1) % size) for i in range(size)]
    down = [(j, i) for i, j in up]
    return lax.ppermute(up_value, "space", up), lax.ppermute(down_value, "space", down)


NEAR = [
    [(4 * b + k) * 4 + y for k in order for y in (2, 3, 1, 0)]
    for b, order in enumerate(((1, 0, 2, 3), (2, 3, 1, 0), (1, 0, 2, 3), (1, 0, 2, 3)))
]
FAR = [[NEAR[b][p] for b in (2, 0, 1, 3)] for p in range(16)]


def all_sum(part):
    piece = part.reshape(16, SLOTS // 2, 128)
    piece = lax.all_to_all(piece, "vel", 0, 0, tiled=True, axis_index_groups=NEAR)
    mine = jnp.sum(piece, 0)
    piece = jnp.broadcast_to(mine[None], (4,) + mine.shape)
    piece = lax.all_to_all(piece, "vel", 0, 0, tiled=True, axis_index_groups=FAR)
    mine = jnp.sum(piece, 0)
    piece = jnp.broadcast_to(mine[None], (16,) + mine.shape)
    piece = lax.all_to_all(piece, "vel", 0, 0, tiled=True, axis_index_groups=NEAR)
    return piece.reshape(SLOTS, 8, 128)


def per_device(distribution, rate_class, wall):
    block, edges, small = (256, 8, 128), (16, 8, 128), (22, 8, 128)
    part, last, first, inner_last, inner_first = kernel_call(
        moments_kernel,
        [(SLOTS, 8, 128)] + [edges] * 4,
        [block, (25, 8, 128), (2, 15, 8, 128), pltpu.SemaphoreType.DMA((4,))],
        limit=53,
        in_specs=[pl.BlockSpec(memory_space=pltpu.HBM)],
    )(distribution)
    sums = all_sum(part)
    prev_sums, next_sums = to_both(
        jnp.concatenate([sums[:12], last]), jnp.concatenate([sums[6:18], first])
    )
    moments, extra, to_next, to_prev, cell = kernel_call(
        first_kernel, [(13, 8, 128), (5, 8, 128), small, small, (9, 8, 128)], []
    )(sums, prev_sums, next_sums, rate_class, wall, last, first, inner_last, inner_first)
    prev, following = to_both(to_next, to_prev)
    (moved_field,) = kernel_call(field_kernel, [block], [(3, 32, 8, 128)])(
        cell, distribution, prev_sums, next_sums
    )
    whole = pl.BlockSpec(memory_space=pltpu.VMEM)
    field, state = kernel_call(
        second_kernel,
        [block, (5, 8, 128)],
        [(3, 32, 8, 128), (9, 8, 128)],
        grid=(2,),
        in_specs=[whole] * 7,
        out_specs=[
            pl.BlockSpec((128, 8, 128), lambda i: (i, 0, 0)),
            pl.BlockSpec((5, 8, 128), lambda i: (0, 0, 0)),
        ],
    )(
        moments, extra, prev, following, rate_class, wall, moved_field
    )
    return field, state


def solution(mesh):
    return jax.shard_map(
        per_device,
        mesh=mesh,
        in_specs=(P("vel", "space", None), P("space", None), P("space", None)),
        out_specs=(P("vel", "space", None), P(None, "space", None)),
        check_vma=False,
    )
```
